32 devices in a mesh: dp: 8 (over z, x), ctx: 4 (over y, core).
Axes of the slice: x: 2, y: 2, z: 4, core: 2. Of those that a mesh axis runs over, the one named last changes fastest.
Arguments:
- hidden: bfloat16 [16384, 1024], P(('dp', 'ctx')), may hold values from -6 to 6
- memory: bfloat16 [8192, 1024], P(('dp', 'ctx')), may hold values from -6 to 6
- cotangent: bfloat16 [16384, 1024], P(('dp', 'ctx')), may hold values from -6 to 6
- dec_segment: int32 [32, 512], P(('dp', 'ctx')), may hold values from 0 to 31, as said below
- pad_length: int32 [32], P(('dp', 'ctx')), may hold values from 0 to 127
- mem_segment: int32 [8192], P(('dp', 'ctx')), may hold values from -1 to 31, as said below
- self_query: bfloat16 [1024, 1024], P(('dp', 'ctx')), may hold values from -0.1875 to 0.1875
- self_key: bfloat16 [1024, 1024], P(('dp', 'ctx')), may hold values from -0.1875 to 0.1875
- self_value: bfloat16 [1024, 1024], P(('dp', 'ctx')), may hold values from -0.1875 to 0.1875
- self_output: bfloat16 [1024, 1024], P(('dp', 'ctx')), may hold values from -3 to 3
- norm1_gain: float32 [1024], P(('dp', 'ctx')), may hold values from 0.5 to 1.5
- norm1_bias: float32 [1024], P(('dp', 'ctx')), may hold values from -1.2 to 1.2
- cross_query: bfloat16 [1024, 1024], P(('dp', 'ctx')), may hold values from -0.1875 to 0.1875
- cross_key: bfloat16 [1024, 1024], P(('dp', 'ctx')), may hold values from -0.1875 to 0.1875
- cross_value: bfloat16 [1024, 1024], P(('dp', 'ctx')), may hold values from -0.1875 to 0.1875
- cross_output: bfloat16 [1024, 1024], P(('dp', 'ctx')), may hold values from -3 to 3
- norm2_gain: float32 [1024], P(('dp', 'ctx')), may hold values from 0.5 to 1.5
- norm2_bias: float32 [1024], P(('dp', 'ctx')), may hold values from -1.2 to 1.2
- ffn_up: bfloat16 [1024, 4096], P(('dp', 'ctx')), may hold values from -0.1875 to 0.1875
- ffn_down: bfloat16 [4096, 1024], P(('dp', 'ctx')), may hold values from -0.75 to 0.75
- norm3_gain: float32 [1024], P(('dp', 'ctx')), may hold values from 0.5 to 1.5
- norm3_bias: float32 [1024], P(('dp', 'ctx')), may hold values from -1.2 to 1.2
Outputs:
- output: bfloat16 [16384, 1024], P(('dp', 'ctx'))
- grad_input: float32 [16384, 1024], P(('dp', 'ctx'))
- grad_memory: float32 [8192, 1024], P(('dp', 'ctx'))
- grad_self_query: float32 [1024, 1024], P(('dp', 'ctx'))
- grad_self_key: float32 [1024, 1024], P(('dp', 'ctx'))
- grad_self_value: float32 [1024, 1024], P(('dp', 'ctx'))
- grad_self_output: float32 [1024, 1024], P(('dp', 'ctx'))
- grad_norm1_gain: float32 [1024], P(('dp', 'ctx'))
- grad_norm1_bias: float32 [1024], P(('dp', 'ctx'))
- grad_cross_query: float32 [1024, 1024], P(('dp', 'ctx'))
- grad_cross_key: float32 [1024, 1024], P(('dp', 'ctx'))
- grad_cross_value: float32 [1024, 1024], P(('dp', 'ctx'))
- grad_cross_output: float32 [1024, 1024], P(('dp', 'ctx'))
- grad_norm2_gain: float32 [1024], P(('dp', 'ctx'))
- grad_norm2_bias: float32 [1024], P(('dp', 'ctx'))
- grad_ffn_up: float32 [1024, 4096], P(('dp', 'ctx'))
- grad_ffn_down: float32 [4096, 1024], P(('dp', 'ctx'))
- grad_norm3_gain: float32 [1024], P(('dp', 'ctx'))
- grad_norm3_bias: float32 [1024], P(('dp', 'ctx'))
The draws below stay inside these ranges and needn't reach their ends.
Inputs may be any that keep to these rules, and one draw needn't show every extreme that they name: `dec_segment`: ids count the sentence pairs of a group (4 rows of one index of dp): row j of a group holds pairs j * 8 to j * 8 + 7 in order, each on one or more positions. `mem_segment`: within each group's 1024 memory tokens the ids never fall; every pair of the group has one or more tokens; -1 marks one or more padding tokens at the group's end.
All inputs are finite; a program needn't handle non-finite values.
Results may differ from the reference program's by a relative error of at most 0.02.
Values may be sent and summed in bfloat16 or wider, within the bound.
No kernel may reach another device: no remote copies, remote signals or barrier semaphores. Data moves between devices by JAX's collectives and lax.ppermute only.
A program may use at most 256 MiB of HBM per device.

```python
import jax
import jax.numpy as jnp
from jax import lax

D = 1024
FF = 4096
HD = 64
ROW_LEN = 512
PAIRS_ROW = 8
ROWS = 32
TOKENS = 16384
PAIRS_GRP = 32
MEM_GRP = 1024
MEM_TOKENS = 8192
N_DP = 8
N_CTX = 4


def draw_dec_segment(key, part):
    row_keys = jax.random.split(key, ROWS)
    positions = jnp.arange(ROW_LEN)

    def one_row(row_key):
        boundaries = jax.random.permutation(row_key, ROW_LEN - 1)[:PAIRS_ROW - 1] + 1
        return jnp.sum((positions[:, None] >= boundaries[None, :]).astype(jnp.int32), axis=1)
    within = jax.vmap(one_row)(row_keys)
    offsets = jnp.arange(ROWS) % (PAIRS_GRP // PAIRS_ROW) * PAIRS_ROW
    return (within + offsets[:, None]).astype(jnp.int32)


def draw_mem_segment(key, part):
    groups = MEM_TOKENS // MEM_GRP
    group_keys = jax.random.split(key, groups)
    positions = jnp.arange(MEM_GRP)

    def one_group(group_key):
        boundaries = jax.random.permutation(group_key, MEM_GRP - 1)[:PAIRS_GRP] + 1
        counted = jnp.sum((positions[:, None] >= boundaries[None, :]).astype(jnp.int32), axis=1)
        return jnp.where(counted == PAIRS_GRP, -1, counted)
    return jax.vmap(one_group)(group_keys).reshape(-1).astype(jnp.int32)


def with_ends(array, rng, low, high):
    index_at = [jax.random.randint(jax.random.fold_in(rng, axis), (), 0, length) for axis, length in enumerate(array.shape)]
    longest = array.shape.index(max(array.shape))
    beside = index_at[:longest] + [(index_at[longest] + 1) % array.shape[longest]] + index_at[longest + 1:]
    return array.at[tuple(index_at)].set(low).at[tuple(beside)].set(high)


def block_scale(stream_key, shape, cuts, least, largest):
    level, own = 1.0, jax.random.fold_in(stream_key, 6)
    for position, blocks in cuts:
        draws = jnp.exp(jax.random.uniform(jax.random.fold_in(own, position), (blocks,), jnp.float32, least / len(cuts), largest / len(cuts)))
        level = level * jnp.repeat(draws, shape[position] // blocks).reshape([-1 if axis == position else 1 for axis in range(len(shape))])
    return level


def gaussian(key, dims, scale, most, cuts=(), held_as=jnp.bfloat16):
    values = scale * jax.random.normal(key, dims, jnp.float32)
    if cuts:
        values = values * block_scale(key, dims, cuts, -0.22, 0.18)
    return jnp.clip(values, -most, most).astype(held_as)


def setup_inputs(seed: int = 0) -> dict:
    splits = jax.random.split(jax.random.key(seed), 23)
    return {
        "hidden": gaussian(splits[0], (TOKENS, D), 1.0, 6.0, ((0, 32),)),
        "memory": gaussian(splits[1], (MEM_TOKENS, D), 1.0, 6.0, ((0, 32),)),
        "cotangent": gaussian(splits[2], (TOKENS, D), 1.0, 6.0, ((0, 32),)),
        "dec_segment": draw_dec_segment(jax.random.fold_in(splits[22], 71), 0),
        "pad_length": with_ends(jax.random.randint(splits[4], (ROWS,), 0, ROW_LEN // 4), jax.random.fold_in(splits[4], 1), 0, (ROW_LEN // 4) - 1).astype(jnp.int32),
        "mem_segment": draw_mem_segment(jax.random.fold_in(splits[22], 71), 0),
        "self_query": gaussian(splits[6], (D, D), D ** -0.5, 0.1875, ((0, 32),)),
        "self_key": gaussian(splits[7], (D, D), D ** -0.5, 0.1875, ((0, 32),)),
        "self_value": gaussian(splits[8], (D, D), D ** -0.5, 0.1875, ((0, 32),)),
        "self_output": gaussian(splits[9], (D, D), (max(D // 256, 1)) ** -0.5, 3.0, ((0, 32),)),
        "norm1_gain": jnp.clip(1.0 + 0.1 * jax.random.normal(splits[10], (D,), jnp.float32), 0.5, 1.5),
        "norm1_bias": gaussian(splits[11], (D,), 0.2, 1.2, ((0, 32),), jnp.float32),
        "cross_query": gaussian(splits[12], (D, D), D ** -0.5, 0.1875, ((0, 32),)),
        "cross_key": gaussian(splits[13], (D, D), D ** -0.5, 0.1875, ((0, 32),)),
        "cross_value": gaussian(splits[14], (D, D), D ** -0.5, 0.1875, ((0, 32),)),
        "cross_output": gaussian(splits[15], (D, D), (max(D // 256, 1)) ** -0.5, 3.0, ((0, 32),)),
        "norm2_gain": jnp.clip(1.0 + 0.1 * jax.random.normal(splits[16], (D,), jnp.float32), 0.5, 1.5),
        "norm2_bias": gaussian(splits[17], (D,), 0.2, 1.2, ((0, 32),), jnp.float32),
        "ffn_up": gaussian(splits[18], (D, FF), D ** -0.5, 0.1875, ((0, 32),)),
        "ffn_down": gaussian(splits[19], (FF, D), (FF // 64) ** -0.5, 0.75, ((0, 32),)),
        "norm3_gain": jnp.clip(1.0 + 0.1 * jax.random.normal(splits[20], (D,), jnp.float32), 0.5, 1.5),
        "norm3_bias": gaussian(splits[21], (D,), 0.2, 1.2, ((0, 32),), jnp.float32),
    }


@jax.custom_vjp
def low(v):
    return lax.optimization_barrier(v.astype(jnp.bfloat16)).astype(jnp.float32)

@jax.custom_vjp
def low_back(v):
    return v

def low_keep(v):
    return (low(v), None)

def low_pass(kept, grad):
    return (grad,)

def back_keep(v):
    return (v, None)

def back_low(kept, grad):
    return (low(grad),)
low.defvjp(low_keep, low_pass)
low_back.defvjp(back_keep, back_low)
ALPHA_RES = 4.16
EPSILON = 1e-05
MASKED = -1e+30
SCORE_SCALE = 0.125
HIGHEST = lax.Precision.HIGHEST

def matmul(left, right):
    return jnp.dot(left, right, precision=HIGHEST, preferred_element_type=jnp.float32)

def normalize(resid, gain, bias):
    center = resid - lax.optimization_barrier(jnp.mean(resid, axis=-1, keepdims=True))
    spread = lax.optimization_barrier(jnp.mean(center * center, axis=-1, keepdims=True))
    return center * lax.rsqrt(spread + EPSILON) * gain + bias

def smooth_gate(values):
    return jax.nn.gelu(values, approximate=False)

def self_mask(segment, padding):
    length = segment.shape[1]
    positions = jnp.arange(length).astype(jnp.int32)
    same_pair = segment[:, :, None] == segment[:, None, :]
    causal = positions[None, :, None] >= positions[None, None, :]
    limit = (jnp.zeros_like(padding) + length - padding).astype(jnp.int32)
    live_key = positions[None, None, :] < limit[:, None, None]
    diagonal = positions[:, None] == positions[None, :]
    return same_pair & causal & (live_key | diagonal[None])

def group_layer(params, hidden, memory, live, cross_active_mask):
    self_query, self_key, self_value, self_output, norm1_gain, norm1_bias, cross_query, cross_key, cross_value, cross_output, norm2_gain, norm2_bias, ffn_up, ffn_down, norm3_gain, norm3_bias = params
    norm1_gain = low(norm1_gain)
    norm1_bias = low(norm1_bias)
    norm2_gain = low(norm2_gain)
    norm2_bias = low(norm2_bias)
    norm3_gain = low(norm3_gain)
    norm3_bias = low(norm3_bias)
    row_count, length = (live.shape[0], live.shape[1])
    model_width = hidden.shape[1]
    head_count = model_width // HD
    queries = low_back(low(matmul(hidden, self_query))).reshape(row_count, length, head_count, HD)
    key_rows = low_back(low(matmul(hidden, self_key))).reshape(row_count, length, head_count, HD)
    value_rows = low_back(low(matmul(hidden, self_value))).reshape(row_count, length, head_count, HD)
    attention_scores = jnp.einsum('rqhd,rkhd->rhqk', queries, key_rows, precision=HIGHEST) * SCORE_SCALE
    attention_scores = low_back(jnp.where(live[:, None], attention_scores, MASKED))
    exponent = jnp.exp(attention_scores - lax.optimization_barrier(jnp.max(attention_scores, axis=-1, keepdims=True)))
    self_probs = low(exponent / lax.optimization_barrier(jnp.sum(exponent, axis=-1, keepdims=True)))
    self_att = jnp.einsum('rhqk,rkhd->rqhd', self_probs, value_rows, precision=HIGHEST)
    self_att = low_back(low(self_att.reshape(row_count * length, model_width)))
    branch = low_back(matmul(self_att, self_output))
    first_out = normalize(ALPHA_RES * hidden + branch, norm1_gain, norm1_bias)
    first_low = low(first_out)
    total_rows = row_count * length
    cross_rows = low_back(low(matmul(first_low, cross_query)))
    mem_keys = low_back(low(matmul(memory, cross_key)))
    mem_values = low_back(low(matmul(memory, cross_value)))

    def head_attend(inputs):
        query_head, key_head, value_head = inputs
        head_scores = matmul(query_head, key_head.T) * SCORE_SCALE
        head_scores = low_back(jnp.where(cross_active_mask, head_scores, MASKED))
        head_exp = jnp.exp(head_scores - lax.optimization_barrier(jnp.max(head_scores, axis=-1, keepdims=True)))
        head_probs = low(head_exp / lax.optimization_barrier(jnp.sum(head_exp, axis=-1, keepdims=True)))
        return matmul(head_probs, value_head)
    query_heads = cross_rows.reshape(total_rows, head_count, HD).transpose(1, 0, 2)
    key_heads = mem_keys.reshape(-1, head_count, HD).transpose(1, 0, 2)
    value_heads = mem_values.reshape(-1, head_count, HD).transpose(1, 0, 2)
    attended = lax.map(jax.checkpoint(head_attend), (query_heads, key_heads, value_heads))
    cross_att = low_back(low(attended.transpose(1, 0, 2).reshape(total_rows, model_width)))
    cross_branch = low_back(matmul(cross_att, cross_output))
    second = normalize(ALPHA_RES * first_out + cross_branch, norm2_gain, norm2_bias)
    pre_act = low_back(matmul(low(second), ffn_up))
    activated = low(smooth_gate(pre_act))
    ffn_branch = low_back(matmul(activated, ffn_down))
    return normalize(ALPHA_RES * second + ffn_branch, norm3_gain, norm3_bias)

def reference(hidden, memory, cotangent, dec_segment, pad_length, mem_segment, self_query, self_key, self_value, self_output, norm1_gain, norm1_bias, cross_query, cross_key, cross_value, cross_output, norm2_gain, norm2_bias, ffn_up, ffn_down, norm3_gain, norm3_bias):
    params = jax.tree.map(lambda weight: weight.astype(jnp.float32), (self_query, self_key, self_value, self_output, norm1_gain, norm1_bias, cross_query, cross_key, cross_value, cross_output, norm2_gain, norm2_bias, ffn_up, ffn_down, norm3_gain, norm3_bias))
    hidden_groups = hidden.astype(jnp.float32).reshape(N_DP, -1, D)
    memory_groups = memory.astype(jnp.float32).reshape(N_DP, -1, D)
    segment_groups = dec_segment.astype(jnp.int32).reshape(N_DP, N_CTX, ROW_LEN)
    padding_groups = pad_length.astype(jnp.int32).reshape(N_DP, N_CTX)
    mem_groups = mem_segment.astype(jnp.int32).reshape(N_DP, MEM_GRP)

    def forward(weights, hidden_all, memory_all):

        def group_step(carry, inputs):
            hidden_one, memory_one, segment_one, padding_one, mem_one = inputs
            live_one = self_mask(segment_one, padding_one)
            cross_one = segment_one.reshape(-1)[:, None] == mem_one[None, :]

            def float_layer(weights_in, hidden_in, memory_in):
                return group_layer(weights_in, hidden_in, memory_in, live_one, cross_one)
            result = jax.checkpoint(float_layer)(weights, hidden_one, memory_one)
            return (carry, result)
        start = jnp.zeros((), hidden_all.dtype)
        carry_out, results = lax.scan(group_step, start, (hidden_all, memory_all, segment_groups, padding_groups, mem_groups))
        return results
    result, pullback = jax.vjp(forward, params, hidden_groups, memory_groups)
    grad_params, grad_hidden, grad_memory = pullback(cotangent.astype(jnp.float32).reshape(N_DP, -1, D))
    return (result.reshape(-1, D).astype(jnp.bfloat16), grad_hidden.reshape(-1, D), grad_memory.reshape(-1, D), grad_params[0], grad_params[1], grad_params[2], grad_params[3], grad_params[4], grad_params[5], grad_params[6], grad_params[7], grad_params[8], grad_params[9], grad_params[10], grad_params[11], grad_params[12], grad_params[13], grad_params[14], grad_params[15])
```

```python
import functools

import jax
import jax.numpy as jnp
from jax import lax
from jax.experimental import pallas as pl
from jax.experimental.pallas import tpu as pltpu
from jax.sharding import PartitionSpec as P

HD = 64
ALPHA_RES = 4.16
EPSILON = 1e-05
MASKED = -1e30
SCORE_SCALE = 0.125
BF = jnp.bfloat16
F32 = jnp.float32
BOTH = ("dp", "ctx")


class Grid:
    def __init__(self, dp, ctx):
        cores = 2
        y = ctx // cores
        x = y
        z = dp // x
        self.size = {"z": z, "x": x, "y": y, "c": cores}
        self.order = ("z", "x", "y", "c")
        self.total = dp * ctx

    def index(self, coords):
        value = 0
        for name in self.order:
            value = value * self.size[name] + coords[name]
        return value

    def coords(self, index):
        out = {}
        for name in reversed(self.order):
            out[name] = index % self.size[name]
            index = index // self.size[name]
        return out

    def here(self):
        dp, ctx = lax.axis_index("dp"), lax.axis_index("ctx")
        return {
            "z": dp // self.size["x"],
            "x": dp % self.size["x"],
            "y": ctx // self.size["c"],
            "c": ctx % self.size["c"],
        }

    def exchange(self, array, name, bit):
        pairs = []
        for source in range(self.total):
            coords = self.coords(source)
            coords[name] ^= bit
            pairs.append((source, self.index(coords)))
        return lax.ppermute(array, BOTH, pairs)

    def gather(self, array, name):
        return [array] + [self.exchange(array, name, k) for k in range(1, self.size[name])]

    def scatter(self, chunks, name):
        total = chunks[0].astype(F32)
        for k in range(1, self.size[name]):
            total = total + self.exchange(chunks[k].astype(BF), name, k).astype(F32)
        return total

    def blocks(self):
        return [
            (i, j, k)
            for i in range(self.size["x"])
            for j in range(self.size["y"])
            for k in range(self.size["c"])
        ]

    def positions(self):
        here = self.here()
        return jnp.stack(
            [
                ((i ^ here["x"]) * self.size["y"] + (j ^ here["y"])) * self.size["c"]
                + (k ^ here["c"])
                for i, j, k in self.blocks()
            ]
            + [k ^ here["z"] for k in range(self.size["z"])]
        ).astype(jnp.int32)

    def gather_weights(self, array, split):
        line = jnp.stack(self.gather(array, "z"))
        out = []
        for part, first, then in ((line[:, :, :split], "x", "y"), (line[:, :, split:], "y", "x")):
            part = jnp.stack(self.gather(part, first))
            part = jnp.stack(self.gather(part, then))
            out.append(self.gather(part, "c"))
        return out


def assemble(grid, positions, pieces, widths):
    nx, ny, nz, nc = (grid.size[name] for name in "xyzc")
    count = nx * ny * nc
    rows = pieces[0][0].shape[3]
    copies = []
    at = 0
    for which in range(2):
        half = pieces[which][0].shape[4]
        start = 0
        for matrix, width in enumerate(widths):
            low, high = max(at, start), min(at + half, start + width)
            if low < high:
                copies.append((which, low - at, matrix, low - start, high - low))
            start += width
        at += half

    def kernel(where, *refs):
        sources = refs[: 2 * nc]
        targets = refs[2 * nc : 2 * nc + len(widths)]
        sems = refs[-1]
        started = []
        for which, source_at, matrix, target_at, width in copies:
            for number, (i, j, k) in enumerate(grid.blocks()):
                for z in range(nz):
                    a, b = (j, i) if which == 0 else (i, j)
                    started.append(
                        pltpu.make_async_copy(
                            sources[which * nc + k].at[a, b, z, :, pl.ds(source_at, width)],
                            targets[matrix].at[
                                where[count + z], where[number], :, pl.ds(target_at, width)
                            ],
                            sems.at[len(started)],
                        )
                    )
        for copy in started:
            copy.start()
        for copy in started:
            copy.wait()

    out = pl.pallas_call(
        kernel,
        out_shape=[jax.ShapeDtypeStruct((nz, count, rows, width), BF) for width in widths],
        in_specs=[pl.BlockSpec(memory_space=pltpu.SMEM)]
        + [pl.BlockSpec(memory_space=pl.ANY)] * (2 * nc),
        out_specs=[pl.BlockSpec(memory_space=pltpu.VMEM)] * len(widths),
        scratch_shapes=[pltpu.SemaphoreType.DMA((len(copies) * count * nz,))],
        compiler_params=pltpu.CompilerParams(vmem_limit_bytes=40 * 2**20),
    )(positions, *pieces[0], *pieces[1])
    return [a.reshape(nz * count * rows, a.shape[3]) for a in out]


def matmul(left, right):
    return jnp.dot(left, right, preferred_element_type=F32)


def outer_right(left, right):
    return lax.dot_general(left, right, (((1,), (1,)), ((), ())), preferred_element_type=F32)


def norm_forward(resid, gain, bias):
    center = resid - jnp.mean(resid, axis=-1, keepdims=True)
    scale = lax.rsqrt(jnp.mean(center * center, axis=-1, keepdims=True) + EPSILON)
    normal = center * scale
    return normal * gain + bias, normal, scale


def norm_backward(dy, normal, scale, gain):
    dn = dy * gain
    grad = (
        dn
        - jnp.mean(dn, axis=-1, keepdims=True)
        - normal * jnp.mean(dn * normal, axis=-1, keepdims=True)
    ) * scale
    return grad, jnp.sum(dy * normal, axis=0), jnp.sum(dy, axis=0)


def turn(grid, positions, left):
    z, count = grid.size["z"], len(grid.blocks())
    rows = left.shape[1] // grid.total
    turned = left.T.reshape(z, count, rows, left.shape[0])
    out = {}
    for n, key in enumerate(grid.blocks()):
        for k in range(z):
            out[key + (k,)] = lax.dynamic_slice(
                turned, (positions[count + k], positions[n], 0, 0), (1, 1, rows, left.shape[0])
            )[0]
    return out


def weight_grad(grid, products):
    x, y, z, c = (grid.size[name] for name in "xyzc")

    def product(part, keys):
        outs = []
        for left, right in part:
            rows = jnp.concatenate([left[key] for key in keys], axis=0)
            tokens = rows.shape[2]
            got = matmul(rows.reshape(-1, tokens), right)
            outs.append(got.reshape(len(keys), rows.shape[1], right.shape[1]))
        return outs[0] if len(outs) == 1 else jnp.concatenate(outs, axis=-1)

    def group(part, first, then):
        def keys(one, core):
            out = []
            for two in range(grid.size[then]):
                i, j = (one, two) if first == "x" else (two, one)
                out += [(i, j, core, k) for k in range(z)]
            return out

        away = [product(part, [b for one in range(grid.size[first]) for b in keys(one, k)]) for k in range(1, c)]
        kept = [product(part, keys(one, 0)) for one in range(grid.size[first])]
        for k in range(1, c):
            got = grid.exchange(away[k - 1].astype(BF), "c", k)
            got = got.reshape((grid.size[first],) + kept[0].shape).astype(F32)
            kept = [a + got[n] for n, a in enumerate(kept)]
        kept = grid.scatter(kept, first)
        kept = kept.reshape((grid.size[then], z) + kept.shape[1:])
        return grid.scatter([kept[n] for n in range(grid.size[then])], then)

    one = group(products[0], "x", "y")
    two = group(products[1], "y", "x")
    both = jnp.concatenate([one, two], axis=-1)
    return grid.scatter([both[k] for k in range(z)], "z")


PAIR = 2 * HD
BLOCK = 128
DIMS_NT = (((1,), (1,)), ((), ()))
DIMS_TN = (((0,), (0,)), ((), ()))


def head_of(array, which, scale=None):
    lane = lax.broadcasted_iota(jnp.int32, array.shape, 1)
    mine = (lane < HD) if which == 0 else (lane >= HD)
    out = jnp.where(mine, array.astype(F32), 0.0)
    return (out if scale is None else out * scale).astype(BF)


def probabilities(q, k, bias):
    scores = lax.dot_general(q, k, DIMS_NT, preferred_element_type=F32) + bias
    exponent = jnp.exp(scores - jnp.max(scores, axis=-1, keepdims=True))
    return exponent * (1.0 / jnp.sum(exponent, axis=-1, keepdims=True))


def pair_forward(q, k, v, bias):
    lane = lax.broadcasted_iota(jnp.int32, q.shape, 1)
    outs = []
    for which in range(2):
        probs = probabilities(head_of(q, which, SCORE_SCALE), k, bias)
        outs.append(matmul(probs.astype(BF), v))
    return jnp.where(lane < HD, outs[0], outs[1]).astype(BF)


def pair_backward(q, k, v, grad, bias):
    gq, gk, gv = 0.0, 0.0, 0.0
    for which in range(2):
        q_one = head_of(q, which, SCORE_SCALE)
        g_one = head_of(grad, which)
        probs = probabilities(q_one, k, bias)
        dprob = lax.dot_general(g_one, v, DIMS_NT, preferred_element_type=F32)
        delta = jnp.sum(probs * dprob, axis=-1, keepdims=True)
        dscore = (probs * (dprob - delta)).astype(BF)
        gq = gq + matmul(dscore, head_of(k, which, SCORE_SCALE))
        gk = gk + lax.dot_general(dscore, q_one, DIMS_TN, preferred_element_type=F32)
        gv = gv + lax.dot_general(probs.astype(BF), g_one, DIMS_TN, preferred_element_type=F32)
    return gq, gk, gv


def self_bias(column, row, pad):
    length = column.shape[0]
    at_q = lax.broadcasted_iota(jnp.int32, (length, length), 0)
    at_k = lax.broadcasted_iota(jnp.int32, (length, length), 1)
    live = (column == row) & (at_q >= at_k) & ((at_k < length - pad) | (at_q == at_k))
    return jnp.where(live, 0.0, MASKED)


def pair_spec(array):
    return pl.BlockSpec((array.shape[0], PAIR), lambda n: (0, n))


def whole_spec(array):
    return pl.BlockSpec(array.shape, lambda n: (0,) * array.ndim)


def self_forward(pad, column, row, q, k, v):
    length, width = q.shape

    def kernel(pad_ref, column_ref, row_ref, q_ref, k_ref, v_ref, out_ref, bias_ref):
        @pl.when(pl.program_id(0) == 0)
        def _():
            bias_ref[...] = self_bias(column_ref[...], row_ref[...], pad_ref[0])

        for start in range(0, length, BLOCK):
            mine, seen = pl.ds(start, BLOCK), pl.ds(0, start + BLOCK)
            out_ref[mine, :] = pair_forward(
                q_ref[mine, :], k_ref[seen, :], v_ref[seen, :], bias_ref[mine, seen]
            )

    return pl.pallas_call(
        kernel,
        grid=(width // PAIR,),
        out_shape=jax.ShapeDtypeStruct(q.shape, BF),
        in_specs=[pl.BlockSpec(memory_space=pltpu.SMEM), whole_spec(column), whole_spec(row)]
        + [pair_spec(q)] * 3,
        out_specs=pair_spec(q),
        scratch_shapes=[pltpu.VMEM((length, length), F32)],
        compiler_params=pltpu.CompilerParams(vmem_limit_bytes=40 * 2**20),
    )(pad, column, row, q, k, v)


def self_backward(pad, column, row, q, k, v, grad):
    length, width = q.shape

    def kernel(pad_ref, column_ref, row_ref, q_ref, k_ref, v_ref, g_ref, gq_ref, gk_ref, gv_ref, bias_ref, k_sum, v_sum):
        @pl.when(pl.program_id(0) == 0)
        def _():
            bias_ref[...] = self_bias(column_ref[...], row_ref[...], pad_ref[0])

        for start in reversed(range(0, length, BLOCK)):
            mine, seen = pl.ds(start, BLOCK), pl.ds(0, start + BLOCK)
            gq, gk, gv = pair_backward(
                q_ref[mine, :], k_ref[seen, :], v_ref[seen, :], g_ref[mine, :], bias_ref[mine, seen]
            )
            gq_ref[mine, :] = gq.astype(BF)
            if start + BLOCK == length:
                k_sum[...] = gk
                v_sum[...] = gv
            else:
                k_sum[seen, :] += gk
                v_sum[seen, :] += gv
        gk_ref[...] = k_sum[...].astype(BF)
        gv_ref[...] = v_sum[...].astype(BF)

    return pl.pallas_call(
        kernel,
        grid=(width // PAIR,),
        out_shape=[jax.ShapeDtypeStruct(q.shape, BF)] * 3,
        in_specs=[pl.BlockSpec(memory_space=pltpu.SMEM), whole_spec(column), whole_spec(row)]
        + [pair_spec(q)] * 4,
        out_specs=[pair_spec(q)] * 3,
        scratch_shapes=[pltpu.VMEM((length, length), F32)] + [pltpu.VMEM((length, PAIR), F32)] * 2,
        compiler_params=pltpu.CompilerParams(vmem_limit_bytes=40 * 2**20),
    )(pad, column, row, q, k, v, grad)


def windows(total):
    return sorted({min(512, total), min(640, total), total})


def choose_window(segment, ids):
    total = ids.shape[0]
    at = jnp.arange(total, dtype=jnp.int32)
    live = (ids >= segment[0]) & (ids <= segment[-1])
    low = jnp.min(jnp.where(live, at, total))
    high = jnp.max(jnp.where(live, at + 1, 0))
    choice, starts, rows = jnp.int32(0), [], []
    for size in windows(total):
        start = jnp.clip(low // 16 * 16, 0, total - size)
        starts.append(start)
        rows.append(lax.dynamic_slice(ids, (start,), (size,)).reshape(1, size))
        choice = choice + (high - start > size).astype(jnp.int32)
    return jnp.stack([choice] + starts), rows


def on_window(window_ref, total, run):
    for n, size in enumerate(windows(total)):
        @pl.when(window_ref[0] == n)
        def _():
            run(n, size, pl.ds(pl.multiple_of(window_ref[1 + n], 16), size))


def cross_forward(window, column, rows, q, k, v):
    length, width = q.shape
    total = k.shape[0]

    def kernel(window_ref, column_ref, *refs):
        row_refs = refs[: len(rows)]
        q_ref, k_ref, v_ref, out_ref, bias_ref = refs[len(rows) :]

        def run(n, size, seen):
            @pl.when(pl.program_id(0) == 0)
            def _():
                bias_ref[:, :size] = jnp.where(column_ref[...] == row_refs[n][...], 0.0, MASKED)

            for start in range(0, length, BLOCK):
                mine = pl.ds(start, BLOCK)
                out_ref[mine, :] = pair_forward(
                    q_ref[mine, :], k_ref[seen, :], v_ref[seen, :], bias_ref[mine, :size]
                )

        on_window(window_ref, total, run)

    return pl.pallas_call(
        kernel,
        grid=(width // PAIR,),
        out_shape=jax.ShapeDtypeStruct(q.shape, BF),
        in_specs=[pl.BlockSpec(memory_space=pltpu.SMEM), whole_spec(column)]
        + [whole_spec(row) for row in rows]
        + [pair_spec(q), pair_spec(k), pair_spec(v)],
        out_specs=pair_spec(q),
        scratch_shapes=[pltpu.VMEM((length, total), F32)],
        compiler_params=pltpu.CompilerParams(vmem_limit_bytes=40 * 2**20),
    )(window, column, *rows, q, k, v)


def cross_backward(window, column, rows, q, k, v, grad):
    length, width = q.shape
    total = k.shape[0]

    def kernel(window_ref, column_ref, *refs):
        row_refs = refs[: len(rows)]
        q_ref, k_ref, v_ref, g_ref, gq_ref, gk_ref, gv_ref, bias_ref, k_sum, v_sum = refs[len(rows) :]

        def run(n, size, seen):
            @pl.when(pl.program_id(0) == 0)
            def _():
                bias_ref[:, :size] = jnp.where(column_ref[...] == row_refs[n][...], 0.0, MASKED)

            if size < total:
                gk_ref[...] = jnp.zeros_like(gk_ref)
                gv_ref[...] = jnp.zeros_like(gv_ref)
            for start in range(0, length, BLOCK):
                mine = pl.ds(start, BLOCK)
                gq, gk, gv = pair_backward(
                    q_ref[mine, :], k_ref[seen, :], v_ref[seen, :], g_ref[mine, :], bias_ref[mine, :size]
                )
                gq_ref[mine, :] = gq.astype(BF)
                if start == 0:
                    k_sum[:size, :] = gk
                    v_sum[:size, :] = gv
                else:
                    k_sum[:size, :] += gk
                    v_sum[:size, :] += gv
            gk_ref[seen, :] = k_sum[:size, :].astype(BF)
            gv_ref[seen, :] = v_sum[:size, :].astype(BF)

        on_window(window_ref, total, run)

    return pl.pallas_call(
        kernel,
        grid=(width // PAIR,),
        out_shape=[jax.ShapeDtypeStruct(a.shape, BF) for a in (q, k, v)],
        in_specs=[pl.BlockSpec(memory_space=pltpu.SMEM), whole_spec(column)]
        + [whole_spec(row) for row in rows]
        + [pair_spec(q), pair_spec(k), pair_spec(v), pair_spec(q)],
        out_specs=[pair_spec(q), pair_spec(k), pair_spec(v)],
        scratch_shapes=[pltpu.VMEM((length, total), F32)] + [pltpu.VMEM((total, PAIR), F32)] * 2,
        compiler_params=pltpu.CompilerParams(vmem_limit_bytes=40 * 2**20),
    )(window, column, *rows, q, k, v, grad)


def body(
    grid,
    hidden,
    memory,
    cotangent,
    dec_segment,
    pad_length,
    mem_segment,
    self_query,
    self_key,
    self_value,
    self_output,
    norm1_gain,
    norm1_bias,
    cross_query,
    cross_key,
    cross_value,
    cross_output,
    norm2_gain,
    norm2_bias,
    ffn_up,
    ffn_down,
    norm3_gain,
    norm3_bias,
):
    width = hidden.shape[1]
    mem_rows = memory.shape[0]
    own_rows = self_query.shape[0]
    positions = grid.positions()
    me = lax.axis_index("dp") * lax.axis_size("ctx") + lax.axis_index("ctx")
    own_width = norm1_gain.shape[0]

    vectors = [norm1_gain, norm1_bias, norm2_gain, norm2_bias, norm3_gain, norm3_bias]
    vectors = jnp.pad(jnp.stack(vectors, axis=1).astype(BF), ((0, 0), (0, 122)))
    pieces = grid.gather_weights(
        jnp.concatenate([self_query, self_key, self_value, self_output, vectors], axis=1), 2 * width
    )
    w_sq, w_sk, w_sv, w_so, vectors = assemble(grid, positions, pieces, [width] * 4 + [128])
    vectors = vectors[:, :6].T.astype(F32)
    gain1, bias1, gain2, bias2, gain3, bias3 = [vectors[n] for n in range(6)]

    ny, nc = grid.size["y"], grid.size["c"]
    here = grid.here()

    def group_all(array):
        found = jnp.stack(
            [jnp.stack(grid.gather(a, "c")) for a in grid.gather(array, "y")]
        )
        rows = [
            lax.dynamic_index_in_dim(
                lax.dynamic_index_in_dim(found, n ^ here["y"], 0, keepdims=False),
                m ^ here["c"],
                0,
                keepdims=False,
            )
            for n in range(ny)
            for m in range(nc)
        ]
        return jnp.concatenate(rows, axis=0)

    mem_all = group_all(memory)
    ids_all = group_all(mem_segment)

    pieces = grid.gather_weights(
        jnp.concatenate([cross_query, cross_key, cross_value, cross_output], axis=1), 2 * width
    )
    w_cq, w_ck, w_cv, w_co = assemble(grid, positions, pieces, [width] * 4)
    ffn = ffn_up.shape[1]
    (w_up,) = assemble(grid, positions, grid.gather_weights(ffn_up, ffn // 2), [ffn])
    (w_down,) = assemble(grid, positions, grid.gather_weights(ffn_down, width // 2), [width])

    segment = dec_segment.reshape(-1)
    column, row = segment.reshape(-1, 1), segment.reshape(1, -1)
    q = matmul(hidden, w_sq).astype(BF)
    k = matmul(hidden, w_sk).astype(BF)
    v = matmul(hidden, w_sv).astype(BF)
    self_att = self_forward(pad_length, column, row, q, k, v)
    first, normal1, scale1 = norm_forward(
        ALPHA_RES * hidden.astype(F32) + matmul(self_att, w_so), gain1, bias1
    )
    first_low = first.astype(BF)
    window, rows = choose_window(segment, ids_all)
    cq = matmul(first_low, w_cq).astype(BF)
    mk = matmul(mem_all, w_ck).astype(BF)
    mv = matmul(mem_all, w_cv).astype(BF)
    cross_att = cross_forward(window, column, rows, cq, mk, mv)
    second, normal2, scale2 = norm_forward(
        ALPHA_RES * first + matmul(cross_att, w_co), gain2, bias2
    )
    second_low = second.astype(BF)
    pre = matmul(second_low, w_up)
    erf = 1.0 + lax.erf(pre * (0.5**0.5))
    act = (0.5 * pre * erf).astype(BF)
    slope = 0.5 * erf + pre * jnp.exp(-0.5 * pre * pre) * 0.3989422804014327
    third, normal3, scale3 = norm_forward(ALPHA_RES * second + matmul(act, w_down), gain3, bias3)

    def turned(left):
        return turn(grid, positions, left)

    grad_third, g_gain3, g_bias3 = norm_backward(cotangent.astype(F32), normal3, scale3, gain3)
    third_low = grad_third.astype(BF)
    grad_pre = (slope * outer_right(third_low, w_down)).astype(BF)
    act_t = turned(act)
    out_down = weight_grad(
        grid, ([(act_t, third_low[:, : width // 2])], [(act_t, third_low[:, width // 2 :])])
    )
    grad_second = ALPHA_RES * grad_third + outer_right(grad_pre, w_up)
    second_t = turned(second_low)
    out_up = weight_grad(
        grid, ([(second_t, grad_pre[:, : ffn // 2])], [(second_t, grad_pre[:, ffn // 2 :])])
    )
    grad_mid, g_gain2, g_bias2 = norm_backward(grad_second, normal2, scale2, gain2)
    mid_low = grad_mid.astype(BF)
    grad_catt = outer_right(mid_low, w_co).astype(BF)
    grad_cq, grad_mk, grad_mv = cross_backward(window, column, rows, cq, mk, mv, grad_catt)
    mem_t = turned(mem_all)
    out_cross = weight_grad(
        grid,
        (
            [(turned(cross_att), mid_low), (turned(first_low), grad_cq)],
            [(mem_t, grad_mk), (mem_t, grad_mv)],
        ),
    )
    grad_mem = outer_right(grad_mk, w_ck) + outer_right(grad_mv, w_cv)
    grad_mem = grad_mem.reshape(ny, nc, mem_rows, width)
    grad_mem = grid.scatter(
        [lax.dynamic_index_in_dim(grad_mem, n ^ here["c"], 1, keepdims=False) for n in range(nc)], "c"
    )
    grad_mem = grid.scatter(
        [lax.dynamic_index_in_dim(grad_mem, n ^ here["y"], 0, keepdims=False) for n in range(ny)], "y"
    )
    grad_first = ALPHA_RES * grad_mid + outer_right(grad_cq, w_cq)
    grad_res, g_gain1, g_bias1 = norm_backward(grad_first, normal1, scale1, gain1)
    res_low = grad_res.astype(BF)
    grad_satt = outer_right(res_low, w_so).astype(BF)
    grad_q, grad_k, grad_v = self_backward(pad_length, column, row, q, k, v, grad_satt)
    hidden_t = turned(hidden)
    out_self = weight_grad(
        grid,
        (
            [(turned(self_att), res_low), (hidden_t, grad_q)],
            [(hidden_t, grad_k), (hidden_t, grad_v)],
        ),
    )
    grad_in = (
        ALPHA_RES * grad_res
        + outer_right(grad_q, w_sq)
        + outer_right(grad_k, w_sk)
        + outer_right(grad_v, w_sv)
    )
    out_so, out_sq, out_sk, out_sv = [out_self[:, n * width : (n + 1) * width] for n in range(4)]
    out_co, out_cq, out_ck, out_cv = [out_cross[:, n * width : (n + 1) * width] for n in range(4)]

    def own_part(vectors):
        total = lax.psum(jnp.stack(vectors), BOTH).reshape(-1, grid.total, own_width)
        return lax.dynamic_index_in_dim(total, me, 1, keepdims=False)

    late = own_part([g_gain2, g_bias2, g_gain3, g_bias3])
    last = own_part([g_gain1, g_bias1])
    return (
        third.astype(BF),
        grad_in,
        grad_mem,
        out_sq,
        out_sk,
        out_sv,
        out_so,
        last[0],
        last[1],
        out_cq,
        out_ck,
        out_cv,
        out_co,
        late[0],
        late[1],
        out_up,
        out_down,
        late[2],
        late[3],
    )


def solution(mesh):
    grid = Grid(mesh.shape["dp"], mesh.shape["ctx"])
    row, flat = P(BOTH, None), P(BOTH)
    block = (row,) * 4 + (flat,) * 2
    return jax.shard_map(
        functools.partial(body, grid),
        mesh=mesh,
        in_specs=(row, row, row, row, flat, flat) + block + block + (row, row, flat, flat),
        out_specs=(row, row, row) + block + block + (row, row, flat, flat),
        check_vma=False,
    )
```

```python
import functools

import jax
import jax.numpy as jnp
from jax import lax
from jax.experimental import pallas as pl
from jax.experimental.pallas import tpu as pltpu
from jax.sharding import PartitionSpec as P

HD = 64
ALPHA_RES = 4.16
EPSILON = 1e-05
MASKED = -1e30
SCORE_SCALE = 0.125
BF = jnp.bfloat16
F32 = jnp.float32
BOTH = ("dp", "ctx")


class Grid:
    def __init__(self, dp, ctx):
        y = ctx // 2
        x = y
        self.size = {"z": dp // x, "x": x, "y": y, "c": 2}
        self.total = dp * ctx

    def index(self, coords):
        value = 0
        for name in "zxyc":
            value = value * self.size[name] + coords[name]
        return value

    def coords(self, index):
        out = {}
        for name in "cyxz":
            out[name] = index % self.size[name]
            index = index // self.size[name]
        return out

    def here(self):
        dp, ctx = lax.axis_index("dp"), lax.axis_index("ctx")
        nx = self.size["x"]
        return {"z": dp // nx, "x": dp % nx, "y": ctx // 2, "c": ctx % 2}

    def exchange(self, array, name, bit):
        pairs = []
        for source in range(self.total):
            coords = self.coords(source)
            coords[name] ^= bit
            pairs.append((source, self.index(coords)))
        return lax.ppermute(array, BOTH, pairs)

    def others(self, array, name):
        return [self.exchange(array, name, k) for k in range(1, self.size[name])]

    def blocks(self):
        nz, nx, ny = self.size["z"], self.size["x"], self.size["y"]
        out = []
        for c in range(2):
            out += [(z, x, y, c) for x in range(nx) for y in range(ny) for z in range(nz // 2)]
            out += [(z, x, y, c) for y in range(ny) for x in range(nx) for z in range(nz // 2, nz)]
        return out

    def positions(self):
        here = self.here()
        return jnp.stack(
            [
                self.index({name: k ^ here[name] for name, k in zip("zxyc", block)})
                for block in self.blocks()
            ]
        ).astype(jnp.int32)


def after(value, *before):
    return lax.optimization_barrier((value,) + before)[0]


SHORT = pl.CostEstimate(flops=1, bytes_accessed=1, transcendentals=0)
call = functools.partial(pl.pallas_call, cost_estimate=SHORT)


def params(mib=48):
    return pltpu.CompilerParams(vmem_limit_bytes=mib * 2**20)


def full(shape):
    return pl.BlockSpec(shape, lambda *_: (0,) * len(shape))


SCALARS = pl.BlockSpec(memory_space=pltpu.SMEM)
ANYWHERE = pl.BlockSpec(memory_space=pl.ANY)


def side_by_side(arrays):
    widths = [a.shape[1] for a in arrays]

    def kernel(*refs):
        at = 0
        for ref, width in zip(refs, widths):
            refs[-1][:, at : at + width] = ref[...]
            at += width

    return call(
        kernel, out_shape=jax.ShapeDtypeStruct((arrays[0].shape[0], sum(widths)), BF)
    )(*arrays)


def stack(groups):
    flat = [a for group in groups for a in group]

    def kernel(*refs):
        outs, sems = refs[len(flat) : -1], refs[-1]
        started = []
        for group, out in zip(groups, outs):
            for n in range(len(group)):
                at = len(started)
                started.append(pltpu.make_async_copy(refs[at], out.at[n], sems.at[at]))
        for copy in started:
            copy.start()
        for copy in started:
            copy.wait()

    return list(call(
        kernel,
        out_shape=[
            jax.ShapeDtypeStruct((len(group),) + group[0].shape, group[0].dtype) for group in groups
        ],
        in_specs=[ANYWHERE] * len(flat),
        out_specs=[pl.BlockSpec(memory_space=pltpu.VMEM)] * len(groups),
        scratch_shapes=[pltpu.SemaphoreType.DMA((len(flat),))],
        compiler_params=params(),
    )(*flat))


def assemble(grid, positions, part_a, part_b, parts, shapes):
    blocks = grid.blocks()
    nx, ny, nz = (grid.size[name] for name in "xyz")
    rows = part_a[0][0].shape[2]
    arrays = [a for part in part_a + part_b for a in part]

    def kernel(where, *refs):
        sources = refs[: len(arrays)]
        targets = refs[len(arrays) : -1]
        sems = refs[-1]
        started = []
        for column, width, result, at in parts:
            for n, (z, x, y, c) in enumerate(blocks):
                if z < nz // 2:
                    source = sources[c * ny + y].at[x, z]
                else:
                    source = sources[2 * ny + c * nx + x].at[y, z - nz // 2]
                started.append(
                    pltpu.make_async_copy(
                        source.at[:, pl.ds(column, width)],
                        targets[result].at[where[n], pl.ds(at, rows), :],
                        sems.at[len(started)],
                    )
                )
        for copy in started:
            copy.start()
        for copy in started:
            copy.wait()

    out = call(
        kernel,
        out_shape=[jax.ShapeDtypeStruct((len(blocks),) + shape, BF) for shape in shapes],
        in_specs=[SCALARS] + [ANYWHERE] * len(arrays),
        out_specs=[pl.BlockSpec(memory_space=pltpu.VMEM)] * len(shapes),
        scratch_shapes=[pltpu.SemaphoreType.DMA((len(parts) * len(blocks),))],
        compiler_params=params(),
    )(positions, *arrays)
    return [a.reshape(-1, a.shape[2]) for a in out]


def turn(grid, positions, left):
    tokens, width = left.shape
    rows = width // grid.total

    def kernel(where, left_ref, out_ref, turned):
        turned[...] = left_ref[...].T
        for n in range(grid.total):
            at = pl.multiple_of(where[n] * rows, rows)
            out_ref[n * rows : (n + 1) * rows, :] = turned[pl.ds(at, rows), :]

    return call(
        kernel,
        out_shape=jax.ShapeDtypeStruct((width, tokens), BF),
        in_specs=[SCALARS, pl.BlockSpec(memory_space=pltpu.VMEM)],
        out_specs=pl.BlockSpec(memory_space=pltpu.VMEM),
        scratch_shapes=[pltpu.VMEM((width, tokens), BF)],
        compiler_params=params(),
    )(positions, left)


def products(pairs, core, groups, got=None):
    rows = pairs[0][0].shape[0] // 2
    if len(pairs) == 1:
        width = pairs[0][1].shape[1]
        block = min(width, 1024)
        if width == block:
            block = width // 2
        steps = width // block
    else:
        block = pairs[0][1].shape[1]
        steps = len(pairs)
        width = sum(b.shape[1] for _, b in pairs)
    starts = [sum(groups[:n]) for n in range(len(groups))]

    def kernel(*refs):
        lefts, rights = refs[: len(pairs)], refs[len(pairs) : 2 * len(pairs)]
        rest = refs[2 * len(pairs) :]
        got_ref, outs = (None, rest) if got is None else (rest[0], rest[1:])

        def run(left, right):
            for start, size, out in zip(starts, groups, outs):
                value = matmul(left[start : start + size, :], right[...])
                cols = slice(0, right.shape[1])
                if got_ref is not None:
                    value = value + got_ref[start : start + size, cols].astype(F32)
                out[:, cols] = value.astype(BF)

        if len(pairs) == 1:
            run(lefts[0], rights[0])
        else:
            for n in range(len(pairs)):
                @pl.when(pl.program_id(0) == n)
                def _():
                    run(lefts[n], rights[n])

    left_specs = [pl.BlockSpec((rows, a.shape[1]), lambda n: (core, 0)) for a, _ in pairs]
    if len(pairs) == 1:
        right_specs = [pl.BlockSpec((pairs[0][1].shape[0], block), lambda n: (0, n))]
    else:
        right_specs = [full(b.shape) for _, b in pairs]
    operands = [a for a, _ in pairs] + [b for _, b in pairs]
    got_specs = []
    if got is not None:
        operands.append(got)
        got_specs = [pl.BlockSpec((rows, block), lambda n: (0, n))]
    return call(
        kernel,
        grid=(steps,),
        out_shape=[jax.ShapeDtypeStruct((size, width), BF) for size in groups],
        in_specs=left_specs + right_specs + got_specs,
        out_specs=[pl.BlockSpec((size, block), lambda n: (0, n)) for size in groups],
        compiler_params=params(),
    )(*operands)


def add_split(sums, counts):
    rows = [arrays[0].shape[0] for arrays in sums]
    width = sums[0][0].shape[1]
    steps = next(n for n in (2, 3, 1) if width % (n * 128) == 0)

    def kernel(*refs):
        at = 0
        out = sum(len(arrays) for arrays in sums)
        for arrays, count, total in zip(sums, counts, rows):
            each = total // count
            for n in range(count):
                value = refs[at][n * each : (n + 1) * each, :].astype(F32)
                for m in range(1, len(arrays)):
                    value = value + refs[at + m][n * each : (n + 1) * each, :].astype(F32)
                refs[out + n][...] = value.astype(BF)
            at += len(arrays)
            out += count

    block = width // steps
    out = call(
        kernel,
        grid=(steps,),
        out_shape=[
            jax.ShapeDtypeStruct((total // count, width), BF)
            for count, total in zip(counts, rows)
            for _ in range(count)
        ],
        in_specs=[
            pl.BlockSpec((total, block), lambda n: (0, n))
            for arrays, total in zip(sums, rows)
            for _ in arrays
        ],
        out_specs=[
            pl.BlockSpec((total // count, block), lambda n: (0, n))
            for count, total in zip(counts, rows)
            for _ in range(count)
        ],
        compiler_params=params(),
    )(*[a for arrays in sums for a in arrays])
    split, at = [], 0
    for count in counts:
        split.append(list(out[at : at + count]))
        at += count
    return split


class Reduction:
    def __init__(self, grid, pairs):
        self.grid = grid
        self.pairs = pairs
        self.rows = pairs[0][0].shape[0]
        self.got, self.got_a, self.got_b = None, [], []

    def start(self):
        (self.away,) = products(self.pairs, 1, [self.rows // 2])
        return self.away

    def wait(self, *before):
        if self.got is not None:
            self.got = after(self.got, *before)
        self.got_a = [after(a, *before) for a in self.got_a]
        self.got_b = [after(b, *before) for b in self.got_b]

    def cores(self, *before):
        away = after(self.away, *before) if before else self.away
        self.got = self.grid.exchange(away, "c", 1)

    def keep(self):
        nx, ny = self.grid.size["x"], self.grid.size["y"]
        quarter = self.rows // 4
        outs = products(
            self.pairs, 0, [quarter // nx] * nx + [quarter // ny] * ny, self.got
        )
        self.got = None
        self.a, self.b = list(outs[:nx]), list(outs[nx:])
        return self.a + self.b

    def hold(self, *before):
        self.a = list(lax.optimization_barrier(tuple(self.a) + before)[: len(self.a)])
        self.b = list(lax.optimization_barrier(tuple(self.b) + before)[: len(self.b)])

    def send(self, name_a, name_b):
        self.got_a = [self.grid.exchange(a, name_a, k + 1) for k, a in enumerate(self.a[1:])]
        self.got_b = [self.grid.exchange(b, name_b, k + 1) for k, b in enumerate(self.b[1:])]
        return self.got_a + self.got_b

    def first(self):
        return self.send("x", "y")

    def add_first(self):
        counts = [self.grid.size["y"], self.grid.size["x"]]
        self.a, self.b = add_split([[self.a[0]] + self.got_a, [self.b[0]] + self.got_b], counts)
        return self.a + self.b

    def second(self):
        return self.send("y", "x")

    def add_second(self):
        half = self.grid.size["z"] // 2
        low, high = add_split([[self.a[0]] + self.got_a, [self.b[0]] + self.got_b], [half, half])
        self.a = low + high
        return self.a

    def last(self):
        self.got_a = [self.grid.exchange(a, "z", k + 1) for k, a in enumerate(self.a[1:])]
        self.got_b = []
        return self.got_a

    def finish(self, widths):
        arrays = [self.a[0]] + self.got_a

        def kernel(*refs):
            at = 0
            for width, out in zip(widths, refs[len(arrays) :]):
                value = refs[0][:, at : at + width].astype(F32)
                for ref in refs[1 : len(arrays)]:
                    value = value + ref[:, at : at + width].astype(F32)
                out[...] = value
                at += width

        return call(
            kernel,
            out_shape=[jax.ShapeDtypeStruct((self.a[0].shape[0], width), F32) for width in widths],
            compiler_params=params(),
        )(*arrays)


def matmul(left, right):
    return jnp.dot(left, right, preferred_element_type=F32)


def outer_right(left, right):
    return lax.dot_general(left, right, (((1,), (1,)), ((), ())), preferred_element_type=F32)


def norm_forward(resid, gain, bias):
    center = resid - jnp.mean(resid, axis=-1, keepdims=True)
    scale = lax.rsqrt(jnp.mean(center * center, axis=-1, keepdims=True) + EPSILON)
    normal = center * scale
    return normal * gain + bias, normal, scale


def norm_backward(dy, normal, scale, gain):
    dn = dy * gain
    grad = (
        dn
        - jnp.mean(dn, axis=-1, keepdims=True)
        - normal * jnp.mean(dn * normal, axis=-1, keepdims=True)
    ) * scale
    return grad, jnp.sum(dy * normal, axis=0), jnp.sum(dy, axis=0)


PAIR = 2 * HD
BLOCK = 128
DIMS_NT = (((1,), (1,)), ((), ()))
DIMS_TN = (((0,), (0,)), ((), ()))


def head_of(array, which, scale=None):
    lane = lax.broadcasted_iota(jnp.int32, array.shape, 1)
    mine = (lane < HD) if which == 0 else (lane >= HD)
    out = jnp.where(mine, array.astype(F32), 0.0)
    return (out if scale is None else out * scale).astype(BF)


def probabilities(q, k, bias):
    scores = lax.dot_general(q, k, DIMS_NT, preferred_element_type=F32) + bias
    exponent = jnp.exp(scores - jnp.max(scores, axis=-1, keepdims=True))
    return exponent * (1.0 / jnp.sum(exponent, axis=-1, keepdims=True))


def pair_forward(q, k, v, bias):
    lane = lax.broadcasted_iota(jnp.int32, q.shape, 1)
    outs = []
    for which in range(2):
        probs = probabilities(head_of(q, which, SCORE_SCALE), k, bias)
        outs.append(matmul(probs.astype(BF), v))
    return jnp.where(lane < HD, outs[0], outs[1]).astype(BF)


def pair_backward(q, k, v, grad, bias):
    gq, gk, gv = 0.0, 0.0, 0.0
    for which in range(2):
        q_one = head_of(q, which, SCORE_SCALE)
        g_one = head_of(grad, which)
        probs = probabilities(q_one, k, bias)
        dprob = lax.dot_general(g_one, v, DIMS_NT, preferred_element_type=F32)
        delta = jnp.sum(probs * dprob, axis=-1, keepdims=True)
        dscore = (probs * (dprob - delta)).astype(BF)
        gq = gq + matmul(dscore, head_of(k, which, SCORE_SCALE))
        gk = gk + lax.dot_general(dscore, q_one, DIMS_TN, preferred_element_type=F32)
        gv = gv + lax.dot_general(probs.astype(BF), g_one, DIMS_TN, preferred_element_type=F32)
    return gq, gk, gv


def self_bias(column, row, pad):
    length = column.shape[0]
    at_q = lax.broadcasted_iota(jnp.int32, (length, length), 0)
    at_k = lax.broadcasted_iota(jnp.int32, (length, length), 1)
    live = (column == row) & (at_q >= at_k) & ((at_k < length - pad) | (at_q == at_k))
    return jnp.where(live, 0.0, MASKED)


def pair_spec(array):
    return pl.BlockSpec((array.shape[0], PAIR), lambda n: (0, n))


def whole_spec(array):
    return pl.BlockSpec(array.shape, lambda n: (0,) * array.ndim)


def self_forward(pad, column, row, q, k, v):
    length, width = q.shape

    def kernel(pad_ref, column_ref, row_ref, q_ref, k_ref, v_ref, out_ref, bias_ref):
        @pl.when(pl.program_id(0) == 0)
        def _():
            bias_ref[...] = self_bias(column_ref[...], row_ref[...], pad_ref[0])

        for start in range(0, length, BLOCK):
            mine, seen = pl.ds(start, BLOCK), pl.ds(0, start + BLOCK)
            out_ref[mine, :] = pair_forward(
                q_ref[mine, :], k_ref[seen, :], v_ref[seen, :], bias_ref[mine, seen]
            )

    return call(
        kernel,
        grid=(width // PAIR,),
        out_shape=jax.ShapeDtypeStruct(q.shape, BF),
        in_specs=[pl.BlockSpec(memory_space=pltpu.SMEM), whole_spec(column), whole_spec(row)]
        + [pair_spec(q)] * 3,
        out_specs=pair_spec(q),
        scratch_shapes=[pltpu.VMEM((length, length), F32)],
        compiler_params=pltpu.CompilerParams(vmem_limit_bytes=40 * 2**20),
    )(pad, column, row, q, k, v)


def self_backward(pad, column, row, q, k, v, grad):
    length, width = q.shape

    def kernel(pad_ref, column_ref, row_ref, q_ref, k_ref, v_ref, g_ref, gq_ref, gk_ref, gv_ref, bias_ref, k_sum, v_sum):
        @pl.when(pl.program_id(0) == 0)
        def _():
            bias_ref[...] = self_bias(column_ref[...], row_ref[...], pad_ref[0])

        for start in reversed(range(0, length, BLOCK)):
            mine, seen = pl.ds(start, BLOCK), pl.ds(0, start + BLOCK)
            gq, gk, gv = pair_backward(
                q_ref[mine, :], k_ref[seen, :], v_ref[seen, :], g_ref[mine, :], bias_ref[mine, seen]
            )
            gq_ref[mine, :] = gq.astype(BF)
            if start + BLOCK == length:
                k_sum[...] = gk
                v_sum[...] = gv
            else:
                k_sum[seen, :] += gk
                v_sum[seen, :] += gv
        gk_ref[...] = k_sum[...].astype(BF)
        gv_ref[...] = v_sum[...].astype(BF)

    return call(
        kernel,
        grid=(width // PAIR,),
        out_shape=[jax.ShapeDtypeStruct(q.shape, BF)] * 3,
        in_specs=[pl.BlockSpec(memory_space=pltpu.SMEM), whole_spec(column), whole_spec(row)]
        + [pair_spec(q)] * 4,
        out_specs=[pair_spec(q)] * 3,
        scratch_shapes=[pltpu.VMEM((length, length), F32)] + [pltpu.VMEM((length, PAIR), F32)] * 2,
        compiler_params=pltpu.CompilerParams(vmem_limit_bytes=40 * 2**20),
    )(pad, column, row, q, k, v, grad)


def windows(total):
    return sorted({min(512, total), min(640, total), total})


def choose_window(segment, ids):
    total = ids.shape[0]
    at = jnp.arange(total, dtype=jnp.int32)
    live = (ids >= segment[0]) & (ids <= segment[-1])
    low = jnp.min(jnp.where(live, at, total))
    high = jnp.max(jnp.where(live, at + 1, 0))
    choice, starts, rows = jnp.int32(0), [], []
    for size in windows(total):
        start = jnp.clip(low // 16 * 16, 0, total - size)
        starts.append(start)
        rows.append(lax.dynamic_slice(ids, (start,), (size,)).reshape(1, size))
        choice = choice + (high - start > size).astype(jnp.int32)
    return jnp.stack([choice] + starts), rows


def on_window(window_ref, total, run):
    for n, size in enumerate(windows(total)):
        @pl.when(window_ref[0] == n)
        def _():
            run(n, size, pl.ds(pl.multiple_of(window_ref[1 + n], 16), size))


def cross_forward(window, column, rows, q, k, v):
    length, width = q.shape
    total = k.shape[0]

    def kernel(window_ref, column_ref, *refs):
        row_refs = refs[: len(rows)]
        q_ref, k_ref, v_ref, out_ref, bias_ref = refs[len(rows) :]

        def run(n, size, seen):
            @pl.when(pl.program_id(0) == 0)
            def _():
                bias_ref[:, :size] = jnp.where(column_ref[...] == row_refs[n][...], 0.0, MASKED)

            for start in range(0, length, BLOCK):
                mine = pl.ds(start, BLOCK)
                out_ref[mine, :] = pair_forward(
                    q_ref[mine, :], k_ref[seen, :], v_ref[seen, :], bias_ref[mine, :size]
                )

        on_window(window_ref, total, run)

    return call(
        kernel,
        grid=(width // PAIR,),
        out_shape=jax.ShapeDtypeStruct(q.shape, BF),
        in_specs=[pl.BlockSpec(memory_space=pltpu.SMEM), whole_spec(column)]
        + [whole_spec(row) for row in rows]
        + [pair_spec(q), pair_spec(k), pair_spec(v)],
        out_specs=pair_spec(q),
        scratch_shapes=[pltpu.VMEM((length, total), F32)],
        compiler_params=pltpu.CompilerParams(vmem_limit_bytes=40 * 2**20),
    )(window, column, *rows, q, k, v)


def cross_backward(window, column, rows, q, k, v, grad):
    length, width = q.shape
    total = k.shape[0]

    def kernel(window_ref, column_ref, *refs):
        row_refs = refs[: len(rows)]
        q_ref, k_ref, v_ref, g_ref, gq_ref, gk_ref, gv_ref, bias_ref, k_sum, v_sum = refs[len(rows) :]

        def run(n, size, seen):
            @pl.when(pl.program_id(0) == 0)
            def _():
                bias_ref[:, :size] = jnp.where(column_ref[...] == row_refs[n][...], 0.0, MASKED)

            if size < total:
                gk_ref[...] = jnp.zeros_like(gk_ref)
                gv_ref[...] = jnp.zeros_like(gv_ref)
            for start in range(0, length, BLOCK):
                mine = pl.ds(start, BLOCK)
                gq, gk, gv = pair_backward(
                    q_ref[mine, :], k_ref[seen, :], v_ref[seen, :], g_ref[mine, :], bias_ref[mine, :size]
                )
                gq_ref[mine, :] = gq.astype(BF)
                if start == 0:
                    k_sum[:size, :] = gk
                    v_sum[:size, :] = gv
                else:
                    k_sum[:size, :] += gk
                    v_sum[:size, :] += gv
            gk_ref[seen, :] = k_sum[:size, :].astype(BF)
            gv_ref[seen, :] = v_sum[:size, :].astype(BF)

        on_window(window_ref, total, run)

    return call(
        kernel,
        grid=(width // PAIR,),
        out_shape=[jax.ShapeDtypeStruct(a.shape, BF) for a in (q, k, v)],
        in_specs=[pl.BlockSpec(memory_space=pltpu.SMEM), whole_spec(column)]
        + [whole_spec(row) for row in rows]
        + [pair_spec(q), pair_spec(k), pair_spec(v), pair_spec(q)],
        out_specs=[pair_spec(q), pair_spec(k), pair_spec(v)],
        scratch_shapes=[pltpu.VMEM((length, total), F32)] + [pltpu.VMEM((total, PAIR), F32)] * 2,
        compiler_params=pltpu.CompilerParams(vmem_limit_bytes=40 * 2**20),
    )(window, column, *rows, q, k, v, grad)


def body(
    grid,
    hidden,
    memory,
    cotangent,
    dec_segment,
    pad_length,
    mem_segment,
    self_query,
    self_key,
    self_value,
    self_output,
    norm1_gain,
    norm1_bias,
    cross_query,
    cross_key,
    cross_value,
    cross_output,
    norm2_gain,
    norm2_bias,
    ffn_up,
    ffn_down,
    norm3_gain,
    norm3_bias,
):
    width = hidden.shape[1]
    ffn = ffn_up.shape[1]
    mem_rows = memory.shape[0]
    own_rows = self_query.shape[0]
    nx, ny, nz = grid.size["x"], grid.size["y"], grid.size["z"]
    here = grid.here()
    positions = grid.positions()

    def gather_z(piece):
        return [piece] + grid.others(piece, "z")

    def stacked(line, *before):
        line = [after(a, *before) for a in line] if before else line
        return stack([line[: nz // 2], line[nz // 2 :]])

    def hold(pair, *before):
        return after(pair[0], *before), after(pair[1], *before)

    class Gather:
        def first(self, pair):
            self.pair = pair
            self.got = grid.others(pair[0], "x"), grid.others(pair[1], "y")
            return self.got[0] + self.got[1]

        def second(self, *before):
            got = [[after(a, *before) for a in part] if before else part for part in self.got]
            self.pair = stack([[a] + part for a, part in zip(self.pair, got)])
            self.got = grid.others(self.pair[0], "y"), grid.others(self.pair[1], "x")
            self.core = [[grid.exchange(a, "c", 1)] for a in self.pair]
            return self.pair

        def cores(self, *before):
            got = [[after(a, *before) for a in part] if before else part for part in self.got]
            out = []
            for a, part, core in zip(self.pair, got, self.core):
                out.append([[a] + part, core + [grid.exchange(b, "c", 1) for b in part]])
            return out

    vectors = [norm1_gain, norm1_bias, norm2_gain, norm2_bias, norm3_gain, norm3_bias]
    vectors = jnp.pad(jnp.stack(vectors, axis=1).astype(BF), ((0, 0), (0, 122)))
    self_piece = side_by_side([self_query, self_key, self_value, self_output, vectors])
    self_z = gather_z(self_piece)
    cross_piece = side_by_side([cross_query, cross_key, cross_value, cross_output])
    many = ffn_down.shape[0] // own_rows
    ffn_piece = side_by_side(
        [ffn_up] + [ffn_down[n * own_rows : (n + 1) * own_rows] for n in range(many)]
    )

    self_z = self_z[:1] + [after(a, cross_piece, ffn_piece) for a in self_z[1:]]

    self_ag, cross_ag, ffn_ag = Gather(), Gather(), Gather()
    mem_y = [memory] + grid.others(memory, "y")
    ids_y = [mem_segment] + grid.others(mem_segment, "y")
    self_pair = stacked(self_z, cross_piece, ffn_piece, *mem_y[1:], *ids_y[1:])
    self_ag.first(self_pair)
    cross_z = gather_z(after(cross_piece, *self_pair))
    mem_c = stack([[after(a, *self_z) for a in mem_y]])
    mem_c += grid.others(mem_c[0], "c")
    ids_c = [jnp.stack(ids_y)]
    ids_c += grid.others(ids_c[0], "c")
    self_pair = self_ag.second(*mem_c[1:], *ids_c[1:])
    cross_pair = stacked(cross_z, *self_pair)
    ffn_z = gather_z(after(ffn_piece, *cross_pair))
    self_a, self_b = self_ag.cores(*cross_pair)
    cross_ag.first(hold(cross_pair, *self_ag.got[0], *self_ag.got[1]))

    mem_blocks = jnp.stack(
        [(y ^ here["y"]) * 2 + (c ^ here["c"]) for c in range(2) for y in range(ny)]
    ).astype(jnp.int32)

    def place_kernel(where, *refs):
        target, sems = refs[2], refs[3]
        started = []
        for c in range(2):
            for y in range(ny):
                n = c * ny + y
                started.append(
                    pltpu.make_async_copy(refs[c].at[y], target.at[where[n]], sems.at[n])
                )
        for copy in started:
            copy.start()
        for copy in started:
            copy.wait()

    mem_all = call(
        place_kernel,
        out_shape=jax.ShapeDtypeStruct((2 * ny, mem_rows, width), BF),
        in_specs=[SCALARS, ANYWHERE, ANYWHERE],
        out_specs=pl.BlockSpec(memory_space=pltpu.VMEM),
        scratch_shapes=[pltpu.SemaphoreType.DMA((2 * ny,))],
        compiler_params=params(),
    )(mem_blocks, *mem_c).reshape(-1, width)
    ids_all = jnp.zeros((2 * ny, mem_rows), jnp.int32)
    for c in range(2):
        for y in range(ny):
            ids_all = lax.dynamic_update_slice(
                ids_all, ids_c[c][y][None], (mem_blocks[c * ny + y], 0)
            )
    ids_all = ids_all.reshape(-1)

    w_sq, w_sk, w_sv, w_so, vectors = assemble(
        grid,
        positions,
        self_a,
        self_b,
        [(n * width, width, n, 0) for n in range(4)] + [(4 * width, 128, 4, 0)],
        [(own_rows, width)] * 4 + [(own_rows, 128)],
    )
    vectors = vectors[:, :6].T.astype(F32)
    gain1, bias1, gain2, bias2, gain3, bias3 = [vectors[n] for n in range(6)]

    segment = dec_segment.reshape(-1)
    column, row = segment.reshape(-1, 1), segment.reshape(1, -1)
    window, rows = choose_window(segment, ids_all)
    hidden_t = turn(grid, positions, hidden)
    mem_t = turn(grid, positions, mem_all)
    q = matmul(hidden, w_sq).astype(BF)
    k = matmul(hidden, w_sk).astype(BF)
    v = matmul(hidden, w_sv).astype(BF)
    cross_pair = cross_ag.second(q, k, v)
    self_att = self_forward(pad_length, column, row, after(q, *cross_pair), k, v)
    ffn_pair = stacked(ffn_z, self_att)
    cross_a, cross_b = cross_ag.cores(self_att)
    cross_got = cross_a[0][1:] + cross_b[0][1:]
    ffn_ag.first(hold(ffn_pair, *cross_got))
    first, normal1, scale1 = norm_forward(
        ALPHA_RES * hidden.astype(F32) + matmul(after(self_att, *cross_got), w_so), gain1, bias1
    )
    first_low = first.astype(BF)
    w_cq, w_ck, w_cv, w_co = assemble(
        grid,
        positions,
        cross_a,
        cross_b,
        [(n * width, width, n, 0) for n in range(4)],
        [(own_rows, width)] * 4,
    )
    cq = matmul(first_low, w_cq).astype(BF)
    mk = matmul(mem_all, w_ck).astype(BF)
    mv = matmul(mem_all, w_cv).astype(BF)
    ffn_pair = ffn_ag.second(cq, mk, mv)
    cross_att = cross_forward(window, column, rows, after(cq, *ffn_pair), mk, mv)
    second, normal2, scale2 = norm_forward(
        ALPHA_RES * first + matmul(cross_att, w_co), gain2, bias2
    )
    second_low = second.astype(BF)
    second_t = turn(grid, positions, second_low)
    self_att_t = turn(grid, positions, self_att)
    first_t = turn(grid, positions, first_low)
    cross_att_t = turn(grid, positions, cross_att)
    turned = (hidden_t, mem_t, second_t, self_att_t, first_t, cross_att_t)
    ffn_a, ffn_b = ffn_ag.cores(*turned)
    w_up, w_down = assemble(
        grid,
        positions,
        ffn_a,
        ffn_b,
        [(0, ffn, 0, 0)] + [(ffn + n * width, width, 1, n * own_rows) for n in range(many)],
        [(own_rows, ffn), (own_rows * many, width)],
    )
    pre = matmul(second_low, w_up)
    erf = 1.0 + lax.erf(pre * (0.5**0.5))
    act = (0.5 * pre * erf).astype(BF)
    slope = 0.5 * erf + pre * jnp.exp(-0.5 * pre * pre) * 0.3989422804014327
    third, normal3, scale3 = norm_forward(ALPHA_RES * second + matmul(act, w_down), gain3, bias3)

    grad_third, g_gain3, g_bias3 = norm_backward(cotangent.astype(F32), normal3, scale3, gain3)
    third_low = grad_third.astype(BF)
    down = Reduction(grid, [(turn(grid, positions, act), third_low)])
    down.start()
    down.cores()
    grad_pre = (slope * outer_right(after(third_low, down.away), w_down)).astype(BF)
    down.wait(grad_pre)
    down_kept = down.keep()
    down.first()
    up = Reduction(grid, [(second_t, after(grad_pre, *down_kept))])
    up.start()
    up.cores()
    grad_second = ALPHA_RES * grad_third + outer_right(after(grad_pre, up.away), w_up)
    up.wait(grad_second)
    up_kept = up.keep()
    grad_mid, g_gain2, g_bias2 = norm_backward(
        after(grad_second, *up_kept), normal2, scale2, gain2
    )
    mid_low = grad_mid.astype(BF)
    grad_catt = outer_right(mid_low, w_co).astype(BF)
    down.wait(grad_catt)
    down_kept = down.add_first()
    down.second()
    up.hold(*down_kept)
    up.first()
    unit = jnp.eye(128, dtype=BF)

    def spread(vectors):
        vectors = jnp.pad(jnp.stack(vectors).astype(BF), ((0, 128 - len(vectors)), (0, 0)))
        return turn(grid, positions, vectors), unit

    cross_norms = spread([g_gain2, g_bias2, g_gain3, g_bias3])
    grad_cq, grad_mk, grad_mv = cross_backward(
        window, column, rows, cq, mk, mv, after(grad_catt, *down_kept, cross_norms[0])
    )
    cross = Reduction(
        grid,
        [(cross_att_t, mid_low), (first_t, grad_cq), (mem_t, grad_mk), (mem_t, grad_mv), cross_norms],
    )
    cross.start()
    cross.cores(*down.got_a, *down.got_b, *up.got_a, *up.got_b)
    down.wait(cross.away)
    down_kept = down.add_second()
    down.last()
    up.wait(*down_kept)
    up_kept = up.add_first()
    up.second()
    grad_first = ALPHA_RES * grad_mid + outer_right(after(grad_cq, cross.away, *up_kept), w_cq)
    grad_res, g_gain1, g_bias1 = norm_backward(grad_first, normal1, scale1, gain1)
    res_low = grad_res.astype(BF)
    grad_satt = outer_right(res_low, w_so).astype(BF)
    own_norms = spread([g_gain1, g_bias1])
    cross.wait(grad_satt, own_norms[0])
    cross_kept = cross.keep()
    up.wait(*cross_kept)
    up_kept = up.add_second()
    cross.hold(*up_kept)
    cross.first()
    up.a = [after(a, *down.got_a) for a in up.a]
    up.last()
    grad_q, grad_k, grad_v = self_backward(
        pad_length, column, row, q, k, v, after(grad_satt, *cross_kept, *up_kept, *down.got_a)
    )
    own = Reduction(
        grid,
        [(self_att_t, res_low), (hidden_t, grad_q), (hidden_t, grad_k), (hidden_t, grad_v), own_norms],
    )
    own.start()
    own.cores(*cross.got_a, *cross.got_b, *up.got_a)
    cross.wait(own.away)
    cross_kept = cross.add_first()
    cross.second()
    grad_in = (
        ALPHA_RES * grad_res
        + outer_right(after(grad_q, own.away, *cross_kept), w_sq)
        + outer_right(grad_k, w_sk)
        + outer_right(grad_v, w_sv)
    )
    own.wait(grad_in)
    own_kept = own.keep()
    own.hold(*cross.got_a, *cross.got_b)
    own.first()
    cross.wait(*own_kept)
    cross_kept = cross.add_second()
    cross.last()
    grad_mem = outer_right(after(grad_mk, *cross_kept), w_ck) + outer_right(grad_mv, w_cv)
    grad_mem = grad_mem.reshape(ny, 2, mem_rows, width)
    mem_own = [lax.dynamic_index_in_dim(grad_mem, n ^ here["c"], 1, keepdims=False) for n in range(2)]
    mem_own = mem_own[0] + grid.exchange(mem_own[1].astype(BF), "c", 1).astype(F32)
    mem_own = [lax.dynamic_index_in_dim(mem_own, n ^ here["y"], 0, keepdims=False) for n in range(ny)]
    (out_down,) = down.finish([width])
    (out_up,) = up.finish([ffn])
    own.wait(out_down, out_up, *mem_own)
    own_kept = own.add_first()
    own.second()
    out_mem = mem_own[0]
    mem_own = [after(a, *own.got_a, *own.got_b) for a in mem_own]
    for n in range(1, ny):
        out_mem = out_mem + grid.exchange(mem_own[n].astype(BF), "y", n).astype(F32)
    own.wait(*cross.got_a)
    out_co, out_cq, out_ck, out_cv, late = cross.finish([width] * 4 + [128])
    own.wait(out_co)
    own.add_second()
    own.last()
    out_so, out_sq, out_sk, out_sv, last = own.finish([width] * 4 + [128])
    norms = [last[:, 0], last[:, 1]] + [late[:, n] for n in range(4)]
    return (
        third.astype(BF),
        grad_in,
        out_mem,
        out_sq,
        out_sk,
        out_sv,
        out_so,
        norms[0],
        norms[1],
        out_cq,
        out_ck,
        out_cv,
        out_co,
        norms[2],
        norms[3],
        out_up,
        out_down,
        norms[4],
        norms[5],
    )


def solution(mesh):
    grid = Grid(mesh.shape["dp"], mesh.shape["ctx"])
    row, flat = P(BOTH, None), P(BOTH)
    block = (row,) * 4 + (flat,) * 2
    return jax.shard_map(
        functools.partial(body, grid),
        mesh=mesh,
        in_specs=(row, row, row, row, flat, flat) + block + block + (row, row, flat, flat),
        out_specs=(row, row, row) + block + block + (row, row, flat, flat),
        check_vma=False,
    )
```

```python
import functools

import jax
import jax.numpy as jnp
from jax import lax
from jax.experimental import pallas as pl
from jax.experimental.pallas import tpu as pltpu
from jax.sharding import PartitionSpec as P

HD = 64
ALPHA_RES = 4.16
EPSILON = 1e-05
MASKED = -1e30
SCORE_SCALE = 0.125
BF = jnp.bfloat16
F32 = jnp.float32
BOTH = ("dp", "ctx")


class Grid:
    def __init__(self, dp, ctx):
        y = ctx // 2
        x = y
        self.size = {"z": dp // x, "x": x, "y": y, "c": 2}
        self.total = dp * ctx

    def index(self, coords):
        value = 0
        for name in "zxyc":
            value = value * self.size[name] + coords[name]
        return value

    def coords(self, index):
        out = {}
        for name in "cyxz":
            out[name] = index % self.size[name]
            index = index // self.size[name]
        return out

    def here(self):
        dp, ctx = lax.axis_index("dp"), lax.axis_index("ctx")
        nx = self.size["x"]
        return {"z": dp // nx, "x": dp % nx, "y": ctx // 2, "c": ctx % 2}

    def exchange(self, array, name, bit):
        pairs = []
        for source in range(self.total):
            coords = self.coords(source)
            coords[name] ^= bit
            pairs.append((source, self.index(coords)))
        return lax.ppermute(array, BOTH, pairs)

    def others(self, array, name):
        return [self.exchange(array, name, k) for k in range(1, self.size[name])]

    def blocks(self):
        nz, nx, ny = self.size["z"], self.size["x"], self.size["y"]
        out = []
        for c in range(2):
            out += [(z, x, y, c) for x in range(nx) for y in range(ny) for z in range(nz // 2)]
            out += [(z, x, y, c) for y in range(ny) for x in range(nx) for z in range(nz // 2, nz)]
        return out

    def positions(self):
        here = self.here()
        return jnp.stack(
            [
                self.index({name: k ^ here[name] for name, k in zip("zxyc", block)})
                for block in self.blocks()
            ]
        ).astype(jnp.int32)


def after(value, *before):
    return lax.optimization_barrier((value,) + before)[0]


SHORT = pl.CostEstimate(flops=1, bytes_accessed=1, transcendentals=0)
call = functools.partial(pl.pallas_call, cost_estimate=SHORT)


def params(mib=48):
    return pltpu.CompilerParams(vmem_limit_bytes=mib * 2**20)


def full(shape):
    return pl.BlockSpec(shape, lambda *_: (0,) * len(shape))


SCALARS = pl.BlockSpec(memory_space=pltpu.SMEM)
ANYWHERE = pl.BlockSpec(memory_space=pl.ANY)


def side_by_side(arrays):
    widths = [a.shape[1] for a in arrays]

    def kernel(*refs):
        at = 0
        for ref, width in zip(refs, widths):
            refs[-1][:, at : at + width] = ref[...]
            at += width

    return call(
        kernel, out_shape=jax.ShapeDtypeStruct((arrays[0].shape[0], sum(widths)), BF)
    )(*arrays)


def stack(groups):
    flat = [a for group in groups for a in group]

    def kernel(*refs):
        outs, sems = refs[len(flat) : -1], refs[-1]
        started = []
        for group, out in zip(groups, outs):
            for n in range(len(group)):
                at = len(started)
                started.append(pltpu.make_async_copy(refs[at], out.at[n], sems.at[at]))
        for copy in started:
            copy.start()
        for copy in started:
            copy.wait()

    return list(call(
        kernel,
        out_shape=[
            jax.ShapeDtypeStruct((len(group),) + group[0].shape, group[0].dtype) for group in groups
        ],
        in_specs=[ANYWHERE] * len(flat),
        out_specs=[pl.BlockSpec(memory_space=pltpu.VMEM)] * len(groups),
        scratch_shapes=[pltpu.SemaphoreType.DMA((len(flat),))],
        compiler_params=params(),
    )(*flat))


def assemble(grid, positions, part_a, part_b, parts, shapes):
    blocks = grid.blocks()
    nx, ny, nz = (grid.size[name] for name in "xyz")
    rows = part_a[0][0].shape[2]
    arrays = [a for part in part_a + part_b for a in part]

    def kernel(where, *refs):
        sources = refs[: len(arrays)]
        targets = refs[len(arrays) : -1]
        sems = refs[-1]
        started = []
        for column, width, result, at in parts:
            for n, (z, x, y, c) in enumerate(blocks):
                if z < nz // 2:
                    source = sources[c * ny + y].at[x, z]
                else:
                    source = sources[2 * ny + c * nx + x].at[y, z - nz // 2]
                started.append(
                    pltpu.make_async_copy(
                        source.at[:, pl.ds(column, width)],
                        targets[result].at[where[n], pl.ds(at, rows), :],
                        sems.at[len(started)],
                    )
                )
        for copy in started:
            copy.start()
        for copy in started:
            copy.wait()

    out = call(
        kernel,
        out_shape=[jax.ShapeDtypeStruct((len(blocks),) + shape, BF) for shape in shapes],
        in_specs=[SCALARS] + [ANYWHERE] * len(arrays),
        out_specs=[pl.BlockSpec(memory_space=pltpu.VMEM)] * len(shapes),
        scratch_shapes=[pltpu.SemaphoreType.DMA((len(parts) * len(blocks),))],
        compiler_params=params(),
    )(positions, *arrays)
    return [a.reshape(-1, a.shape[2]) for a in out]


def turn(grid, positions, left):
    tokens, width = left.shape
    rows = width // grid.total

    def kernel(where, left_ref, out_ref, turned):
        turned[...] = left_ref[...].T
        for n in range(grid.total):
            at = pl.multiple_of(where[n] * rows, rows)
            out_ref[n * rows : (n + 1) * rows, :] = turned[pl.ds(at, rows), :]

    return call(
        kernel,
        out_shape=jax.ShapeDtypeStruct((width, tokens), BF),
        in_specs=[SCALARS, pl.BlockSpec(memory_space=pltpu.VMEM)],
        out_specs=pl.BlockSpec(memory_space=pltpu.VMEM),
        scratch_shapes=[pltpu.VMEM((width, tokens), BF)],
        compiler_params=params(),
    )(positions, left)


def products(pairs, core, groups, got=None):
    rows = pairs[0][0].shape[0] // 2
    if len(pairs) == 1:
        width = pairs[0][1].shape[1]
        block = min(width, 1024)
        if width == block:
            block = width // 2
        steps = width // block
    else:
        block = pairs[0][1].shape[1]
        steps = len(pairs)
        width = sum(b.shape[1] for _, b in pairs)
    starts = [sum(groups[:n]) for n in range(len(groups))]

    def kernel(*refs):
        lefts, rights = refs[: len(pairs)], refs[len(pairs) : 2 * len(pairs)]
        rest = refs[2 * len(pairs) :]
        got_ref, outs = (None, rest) if got is None else (rest[0], rest[1:])

        def run(left, right):
            for start, size, out in zip(starts, groups, outs):
                value = matmul(left[start : start + size, :], right[...])
                cols = slice(0, right.shape[1])
                if got_ref is not None:
                    value = value + got_ref[start : start + size, cols].astype(F32)
                out[:, cols] = value.astype(BF)

        if len(pairs) == 1:
            run(lefts[0], rights[0])
        else:
            for n in range(len(pairs)):
                @pl.when(pl.program_id(0) == n)
                def _():
                    run(lefts[n], rights[n])

    left_specs = [pl.BlockSpec((rows, a.shape[1]), lambda n: (core, 0)) for a, _ in pairs]
    if len(pairs) == 1:
        right_specs = [pl.BlockSpec((pairs[0][1].shape[0], block), lambda n: (0, n))]
    else:
        right_specs = [full(b.shape) for _, b in pairs]
    operands = [a for a, _ in pairs] + [b for _, b in pairs]
    got_specs = []
    if got is not None:
        operands.append(got)
        got_specs = [pl.BlockSpec((rows, block), lambda n: (0, n))]
    return call(
        kernel,
        grid=(steps,),
        out_shape=[jax.ShapeDtypeStruct((size, width), BF) for size in groups],
        in_specs=left_specs + right_specs + got_specs,
        out_specs=[pl.BlockSpec((size, block), lambda n: (0, n)) for size in groups],
        compiler_params=params(),
    )(*operands)


def add_split(sums, counts):
    rows = [arrays[0].shape[0] for arrays in sums]
    width = sums[0][0].shape[1]
    steps = next(n for n in (2, 3, 1) if width % (n * 128) == 0)

    def kernel(*refs):
        at = 0
        out = sum(len(arrays) for arrays in sums)
        for arrays, count, total in zip(sums, counts, rows):
            each = total // count
            for n in range(count):
                value = refs[at][n * each : (n + 1) * each, :].astype(F32)
                for m in range(1, len(arrays)):
                    value = value + refs[at + m][n * each : (n + 1) * each, :].astype(F32)
                refs[out + n][...] = value.astype(BF)
            at += len(arrays)
            out += count

    block = width // steps
    out = call(
        kernel,
        grid=(steps,),
        out_shape=[
            jax.ShapeDtypeStruct((total // count, width), BF)
            for count, total in zip(counts, rows)
            for _ in range(count)
        ],
        in_specs=[
            pl.BlockSpec((total, block), lambda n: (0, n))
            for arrays, total in zip(sums, rows)
            for _ in arrays
        ],
        out_specs=[
            pl.BlockSpec((total // count, block), lambda n: (0, n))
            for count, total in zip(counts, rows)
            for _ in range(count)
        ],
        compiler_params=params(),
    )(*[a for arrays in sums for a in arrays])
    split, at = [], 0
    for count in counts:
        split.append(list(out[at : at + count]))
        at += count
    return split


class Reduction:
    def __init__(self, grid, pairs):
        self.grid = grid
        self.pairs = pairs
        self.rows = pairs[0][0].shape[0]
        self.got, self.got_a, self.got_b = None, [], []

    def start(self):
        (self.away,) = products(self.pairs, 1, [self.rows // 2])
        return self.away

    def wait(self, *before):
        if self.got is not None:
            self.got = after(self.got, *before)
        self.got_a = [after(a, *before) for a in self.got_a]
        self.got_b = [after(b, *before) for b in self.got_b]

    def cores(self, *before):
        away = after(self.away, *before) if before else self.away
        self.got = self.grid.exchange(away, "c", 1)

    def keep(self):
        nx, ny = self.grid.size["x"], self.grid.size["y"]
        quarter = self.rows // 4
        outs = products(
            self.pairs, 0, [quarter // nx] * nx + [quarter // ny] * ny, self.got
        )
        self.got = None
        self.a, self.b = list(outs[:nx]), list(outs[nx:])
        return self.a + self.b

    def hold(self, *before):
        self.a = list(lax.optimization_barrier(tuple(self.a) + before)[: len(self.a)])
        self.b = list(lax.optimization_barrier(tuple(self.b) + before)[: len(self.b)])

    def send(self, name_a, name_b):
        self.got_a = [self.grid.exchange(a, name_a, k + 1) for k, a in enumerate(self.a[1:])]
        self.got_b = [self.grid.exchange(b, name_b, k + 1) for k, b in enumerate(self.b[1:])]
        return self.got_a + self.got_b

    def first(self):
        return self.send("x", "y")

    def add_first(self):
        counts = [self.grid.size["y"], self.grid.size["x"]]
        self.a, self.b = add_split([[self.a[0]] + self.got_a, [self.b[0]] + self.got_b], counts)
        return self.a + self.b

    def second(self):
        return self.send("y", "x")

    def add_second(self):
        half = self.grid.size["z"] // 2
        low, high = add_split([[self.a[0]] + self.got_a, [self.b[0]] + self.got_b], [half, half])
        self.a = low + high
        return self.a

    def last(self):
        self.got_a = [self.grid.exchange(a, "z", k + 1) for k, a in enumerate(self.a[1:])]
        self.got_b = []
        return self.got_a

    def finish(self, widths):
        arrays = [self.a[0]] + self.got_a

        def kernel(*refs):
            at = 0
            for width, out in zip(widths, refs[len(arrays) :]):
                value = refs[0][:, at : at + width].astype(F32)
                for ref in refs[1 : len(arrays)]:
                    value = value + ref[:, at : at + width].astype(F32)
                out[...] = value
                at += width

        return call(
            kernel,
            out_shape=[jax.ShapeDtypeStruct((self.a[0].shape[0], width), F32) for width in widths],
            compiler_params=params(),
        )(*arrays)


def matmul(left, right):
    return jnp.dot(left, right, preferred_element_type=F32)


def outer_right(left, right):
    return lax.dot_general(left, right, (((1,), (1,)), ((), ())), preferred_element_type=F32)


def norm_forward(resid, gain, bias):
    center = resid - jnp.mean(resid, axis=-1, keepdims=True)
    scale = lax.rsqrt(jnp.mean(center * center, axis=-1, keepdims=True) + EPSILON)
    normal = center * scale
    return normal * gain + bias, normal, scale


def norm_backward(dy, normal, scale, gain):
    dn = dy * gain
    grad = (
        dn
        - jnp.mean(dn, axis=-1, keepdims=True)
        - normal * jnp.mean(dn * normal, axis=-1, keepdims=True)
    ) * scale
    return grad, jnp.sum(dy * normal, axis=0), jnp.sum(dy, axis=0)


PAIR = 2 * HD
BLOCK = 256
DIMS_NT = (((1,), (1,)), ((), ()))


def head_of(array, which, scale=None):
    lane = lax.broadcasted_iota(jnp.int32, array.shape, 1)
    mine = (lane < HD) if which == 0 else (lane >= HD)
    out = jnp.where(mine, array.astype(F32), 0.0)
    return (out if scale is None else out * scale).astype(BF)


def across(left, right):
    return lax.dot_general(left, right, DIMS_NT, preferred_element_type=F32)


def pair_forward(q, k, v_t, bias):
    probs, sums = [], []
    for n in range(2):
        scores = across(k, head_of(q, n, SCORE_SCALE)) + bias
        peak = jnp.max(scores, axis=0, keepdims=True)
        exponent = jnp.exp(scores - peak)
        total = jnp.sum(exponent, axis=0, keepdims=True)
        probs.append((exponent * (1.0 / total)).astype(BF))
        sums.append(peak + jnp.log(total))
    outs = [matmul(v_t[n * HD : (n + 1) * HD, :], probs[n]) for n in range(2)]
    return jnp.concatenate(outs, axis=0).T.astype(BF), sums


TILE = 128


def pair_backward(tiles, keys, bias_ref, sums_ref, q, k, v, out, grad, probs_ref, dscores_ref):
    length = q.shape[0]
    q_one = [head_of(q, n, SCORE_SCALE) for n in range(2)]
    g_one = [head_of(grad, n) for n in range(2)]
    both = (grad.astype(F32) * out.astype(F32)).T
    delta = [jnp.sum(both[n * HD : (n + 1) * HD, :], axis=0, keepdims=True) for n in range(2)]
    for key, query in tiles:
        down, over = slice(key, key + TILE), slice(query, query + BLOCK)
        for n in range(2):
            scores = across(k[down, :], q_one[n][over, :]) + bias_ref[down, over]
            probs = jnp.exp(scores - sums_ref[0, n : n + 1, over])
            dprob = across(v[down, :], g_one[n][over, :])
            at = slice(n * length + query, n * length + query + BLOCK)
            probs_ref[down, at] = probs.astype(BF)
            dscores_ref[down, at] = (probs * (dprob - delta[n][:, over])).astype(BF)
    k_t = k.T
    gq = [
        matmul(k_t[n * HD : (n + 1) * HD, :], dscores_ref[:keys, n * length : (n + 1) * length])
        for n in range(2)
    ]
    gq = jnp.concatenate(gq, axis=0).T * SCORE_SCALE
    gk = matmul(dscores_ref[:keys, :], jnp.concatenate(q_one, axis=0))
    gv = matmul(probs_ref[:keys, :], jnp.concatenate(g_one, axis=0))
    return gq.astype(BF), gk.astype(BF), gv.astype(BF)


def self_bias(column, row, pad):
    length = column.shape[0]
    at_k = lax.broadcasted_iota(jnp.int32, (length, length), 0)
    at_q = lax.broadcasted_iota(jnp.int32, (length, length), 1)
    live = (column == row) & (at_q >= at_k) & ((at_k < length - pad) | (at_q == at_k))
    return jnp.where(live, 0.0, MASKED)


def pair_spec(array):
    return pl.BlockSpec((array.shape[0], PAIR), lambda n: (0, n))


def sums_spec(length):
    return pl.BlockSpec((1, 8, length), lambda n: (n, 0, 0))


def whole_spec(array):
    return pl.BlockSpec(array.shape, lambda n: (0,) * array.ndim)


def self_forward(pad, column, row, q, k, v):
    length, width = q.shape

    def kernel(pad_ref, column_ref, row_ref, q_ref, k_ref, v_ref, out_ref, sums_ref, bias_ref):
        @pl.when(pl.program_id(0) == 0)
        def _():
            bias_ref[...] = self_bias(column_ref[...], row_ref[...], pad_ref[0])

        v_t = v_ref[...].T
        for start in range(0, length, BLOCK):
            mine, seen = slice(start, start + BLOCK), slice(0, start + BLOCK)
            out_ref[mine, :], sums = pair_forward(
                q_ref[mine, :], k_ref[seen, :], v_t[:, seen], bias_ref[seen, mine]
            )
            for n in range(2):
                sums_ref[0, n : n + 1, mine] = sums[n]

    return call(
        kernel,
        grid=(width // PAIR,),
        out_shape=[
            jax.ShapeDtypeStruct(q.shape, BF),
            jax.ShapeDtypeStruct((width // PAIR, 8, length), F32),
        ],
        in_specs=[pl.BlockSpec(memory_space=pltpu.SMEM), whole_spec(column), whole_spec(row)]
        + [pair_spec(q)] * 3,
        out_specs=[pair_spec(q), sums_spec(length)],
        scratch_shapes=[pltpu.VMEM((length, length), F32)],
        compiler_params=pltpu.CompilerParams(vmem_limit_bytes=40 * 2**20),
    )(pad, column, row, q, k, v)


def self_backward(pad, column, row, sums, q, k, v, out, grad):
    length, width = q.shape
    tiles = [
        (key, query)
        for query in range(0, length, BLOCK)
        for key in range(0, query + BLOCK, TILE)
    ]

    def kernel(pad_ref, column_ref, row_ref, sums_ref, *refs):
        q_ref, k_ref, v_ref, o_ref, g_ref, gq_ref, gk_ref, gv_ref, bias_ref, probs_ref, ds_ref = refs

        @pl.when(pl.program_id(0) == 0)
        def _():
            bias_ref[...] = self_bias(column_ref[...], row_ref[...], pad_ref[0])
            probs_ref[...] = jnp.zeros_like(probs_ref)
            ds_ref[...] = jnp.zeros_like(ds_ref)

        gq_ref[...], gk_ref[...], gv_ref[...] = pair_backward(
            tiles,
            length,
            bias_ref,
            sums_ref,
            q_ref[...],
            k_ref[...],
            v_ref[...],
            o_ref[...],
            g_ref[...],
            probs_ref,
            ds_ref,
        )

    return call(
        kernel,
        grid=(width // PAIR,),
        out_shape=[jax.ShapeDtypeStruct(q.shape, BF)] * 3,
        in_specs=[SCALARS, whole_spec(column), whole_spec(row), sums_spec(length)]
        + [pair_spec(q)] * 5,
        out_specs=[pair_spec(q)] * 3,
        scratch_shapes=[pltpu.VMEM((length, length), F32)]
        + [pltpu.VMEM((length, 2 * length), BF)] * 2,
        compiler_params=params(),
    )(pad, column, row, sums, q, k, v, out, grad)


def windows(total):
    return sorted({min(512, total), min(640, total), total})


def choose_window(segment, ids):
    total = ids.shape[0]
    at = jnp.arange(total, dtype=jnp.int32)
    live = (ids >= segment[0]) & (ids <= segment[-1])
    low = jnp.min(jnp.where(live, at, total))
    high = jnp.max(jnp.where(live, at + 1, 0))
    choice, starts, rows = jnp.int32(0), [], []
    for size in windows(total):
        start = jnp.clip(low // 16 * 16, 0, total - size)
        starts.append(start)
        rows.append(lax.dynamic_slice(ids, (start,), (size,)).reshape(size, 1))
        choice = choice + (high - start > size).astype(jnp.int32)
    return jnp.stack([choice] + starts), rows


def on_window(window_ref, total, run):
    for n, size in enumerate(windows(total)):
        @pl.when(window_ref[0] == n)
        def _():
            run(n, size, pl.ds(pl.multiple_of(window_ref[1 + n], 16), size))


def cross_forward(window, column, rows, q, k, v):
    length, width = q.shape
    total = k.shape[0]

    def kernel(window_ref, column_ref, *refs):
        row_refs = refs[: len(rows)]
        q_ref, k_ref, v_ref, out_ref, sums_ref, bias_ref = refs[len(rows) :]

        def run(n, size, seen):
            @pl.when(pl.program_id(0) == 0)
            def _():
                bias_ref[:size, :] = jnp.where(row_refs[n][...] == column_ref[...], 0.0, MASKED)

            v_t = v_ref[seen, :].T
            for start in range(0, length, BLOCK):
                mine = slice(start, start + BLOCK)
                out_ref[mine, :], sums = pair_forward(
                    q_ref[mine, :], k_ref[seen, :], v_t, bias_ref[:size, mine]
                )
                for m in range(2):
                    sums_ref[0, m : m + 1, mine] = sums[m]

        on_window(window_ref, total, run)

    return call(
        kernel,
        grid=(width // PAIR,),
        out_shape=[
            jax.ShapeDtypeStruct(q.shape, BF),
            jax.ShapeDtypeStruct((width // PAIR, 8, length), F32),
        ],
        in_specs=[pl.BlockSpec(memory_space=pltpu.SMEM), whole_spec(column)]
        + [whole_spec(row) for row in rows]
        + [pair_spec(q), pair_spec(k), pair_spec(v)],
        out_specs=[pair_spec(q), sums_spec(length)],
        scratch_shapes=[pltpu.VMEM((total, length), F32)],
        compiler_params=pltpu.CompilerParams(vmem_limit_bytes=40 * 2**20),
    )(window, column, *rows, q, k, v)


def cross_backward(window, row, ids, sums, q, k, v, out, grad):
    length, width = q.shape
    total = k.shape[0]

    def kernel(window_ref, row_ref, sums_ref, *refs):
        id_refs = refs[: len(ids)]
        q_ref, k_ref, v_ref, o_ref, g_ref, gq_ref, gk_ref, gv_ref, bias_ref, probs_ref, ds_ref = refs[
            len(ids) :
        ]

        def run(n, size, seen):
            @pl.when(pl.program_id(0) == 0)
            def _():
                bias_ref[:size, :] = jnp.where(id_refs[n][...] == row_ref[...], 0.0, MASKED)

            if size < total:
                gk_ref[...] = jnp.zeros_like(gk_ref)
                gv_ref[...] = jnp.zeros_like(gv_ref)
            tiles = [
                (key, query)
                for query in range(0, length, BLOCK)
                for key in range(0, size, TILE)
            ]
            gq_ref[...], gk_ref[seen, :], gv_ref[seen, :] = pair_backward(
                tiles,
                size,
                bias_ref,
                sums_ref,
                q_ref[...],
                k_ref[seen, :],
                v_ref[seen, :],
                o_ref[...],
                g_ref[...],
                probs_ref,
                ds_ref,
            )

        on_window(window_ref, total, run)

    return call(
        kernel,
        grid=(width // PAIR,),
        out_shape=[jax.ShapeDtypeStruct(a.shape, BF) for a in (q, k, v)],
        in_specs=[SCALARS, whole_spec(row), sums_spec(length)]
        + [whole_spec(a) for a in ids]
        + [pair_spec(q), pair_spec(k), pair_spec(v), pair_spec(q), pair_spec(q)],
        out_specs=[pair_spec(q), pair_spec(k), pair_spec(v)],
        scratch_shapes=[pltpu.VMEM((total, length), F32)]
        + [pltpu.VMEM((total, 2 * length), BF)] * 2,
        compiler_params=params(),
    )(window, row, sums, *ids, q, k, v, out, grad)


def body(
    grid,
    hidden,
    memory,
    cotangent,
    dec_segment,
    pad_length,
    mem_segment,
    self_query,
    self_key,
    self_value,
    self_output,
    norm1_gain,
    norm1_bias,
    cross_query,
    cross_key,
    cross_value,
    cross_output,
    norm2_gain,
    norm2_bias,
    ffn_up,
    ffn_down,
    norm3_gain,
    norm3_bias,
):
    width = hidden.shape[1]
    ffn = ffn_up.shape[1]
    mem_rows = memory.shape[0]
    own_rows = self_query.shape[0]
    nx, ny, nz = grid.size["x"], grid.size["y"], grid.size["z"]
    here = grid.here()
    positions = grid.positions()

    def gather_z(piece):
        return [piece] + grid.others(piece, "z")

    def stacked(line, *before):
        line = [after(a, *before) for a in line] if before else line
        return stack([line[: nz // 2], line[nz // 2 :]])

    def hold(pair, *before):
        return after(pair[0], *before), after(pair[1], *before)

    class Gather:
        def first(self, pair):
            self.pair = pair
            self.got = grid.others(pair[0], "x"), grid.others(pair[1], "y")
            return self.got[0] + self.got[1]

        def second(self, *before):
            got = [[after(a, *before) for a in part] if before else part for part in self.got]
            self.pair = stack([[a] + part for a, part in zip(self.pair, got)])
            self.got = grid.others(self.pair[0], "y"), grid.others(self.pair[1], "x")
            self.core = [[grid.exchange(a, "c", 1)] for a in self.pair]
            return self.pair

        def cores(self, *before):
            got = [[after(a, *before) for a in part] if before else part for part in self.got]
            out = []
            for a, part, core in zip(self.pair, got, self.core):
                out.append([[a] + part, core + [grid.exchange(b, "c", 1) for b in part]])
            return out

    vectors = [norm1_gain, norm1_bias, norm2_gain, norm2_bias, norm3_gain, norm3_bias]
    vectors = jnp.pad(jnp.stack(vectors, axis=1).astype(BF), ((0, 0), (0, 122)))
    self_piece = side_by_side([self_query, self_key, self_value, self_output])
    self_z = gather_z(self_piece)
    cross_piece = side_by_side([cross_query, cross_key, cross_value, cross_output, vectors])
    many = ffn_down.shape[0] // own_rows
    ffn_piece = side_by_side(
        [ffn_up] + [ffn_down[n * own_rows : (n + 1) * own_rows] for n in range(many)]
    )

    self_z = self_z[:1] + [after(a, cross_piece, ffn_piece) for a in self_z[1:]]

    self_ag, cross_ag, ffn_ag = Gather(), Gather(), Gather()
    mem_y = [memory] + grid.others(memory, "y")
    ids_y = [mem_segment] + grid.others(mem_segment, "y")
    self_pair = stacked(self_z, cross_piece, ffn_piece, *mem_y[1:], *ids_y[1:])
    self_ag.first(self_pair)
    cross_z = gather_z(after(cross_piece, *self_pair))
    mem_c = stack([[after(a, *self_z) for a in mem_y]])
    mem_c += grid.others(mem_c[0], "c")
    ids_c = [jnp.stack(ids_y)]
    ids_c += grid.others(ids_c[0], "c")
    self_pair = self_ag.second(*mem_c[1:], *ids_c[1:])
    cross_pair = stacked(cross_z, *self_pair)
    ffn_z = gather_z(after(ffn_piece, *cross_pair))
    self_a, self_b = self_ag.cores(*cross_pair)
    cross_ag.first(hold(cross_pair, *self_ag.got[0], *self_ag.got[1]))

    mem_blocks = jnp.stack(
        [(y ^ here["y"]) * 2 + (c ^ here["c"]) for c in range(2) for y in range(ny)]
    ).astype(jnp.int32)

    def place_kernel(where, *refs):
        target, sems = refs[2], refs[3]
        started = []
        for c in range(2):
            for y in range(ny):
                n = c * ny + y
                started.append(
                    pltpu.make_async_copy(refs[c].at[y], target.at[where[n]], sems.at[n])
                )
        for copy in started:
            copy.start()
        for copy in started:
            copy.wait()

    mem_all = call(
        place_kernel,
        out_shape=jax.ShapeDtypeStruct((2 * ny, mem_rows, width), BF),
        in_specs=[SCALARS, ANYWHERE, ANYWHERE],
        out_specs=pl.BlockSpec(memory_space=pltpu.VMEM),
        scratch_shapes=[pltpu.SemaphoreType.DMA((2 * ny,))],
        compiler_params=params(),
    )(mem_blocks, *mem_c).reshape(-1, width)
    ids_all = jnp.zeros((2 * ny, mem_rows), jnp.int32)
    for c in range(2):
        for y in range(ny):
            ids_all = lax.dynamic_update_slice(
                ids_all, ids_c[c][y][None], (mem_blocks[c * ny + y], 0)
            )
    ids_all = ids_all.reshape(-1)

    w_sq, w_sk, w_sv, w_so = assemble(
        grid,
        positions,
        self_a,
        self_b,
        [(n * width, width, n, 0) for n in range(4)],
        [(own_rows, width)] * 4,
    )

    segment = dec_segment.reshape(-1)
    column, row = segment.reshape(-1, 1), segment.reshape(1, -1)
    window, rows = choose_window(segment, ids_all)
    hidden_t = turn(grid, positions, hidden)
    mem_t = turn(grid, positions, mem_all)
    q = matmul(hidden, w_sq).astype(BF)
    k = matmul(hidden, w_sk).astype(BF)
    v = matmul(hidden, w_sv).astype(BF)
    cross_pair = cross_ag.second(w_sq)
    self_att, self_sums = self_forward(pad_length, column, row, after(q, *cross_pair, *rows), k, v)
    ffn_pair = stacked(ffn_z, self_att)
    cross_a, cross_b = cross_ag.cores(self_att)
    cross_got = cross_a[0][1:] + cross_b[0][1:]
    ffn_ag.first(hold(ffn_pair, *cross_got))
    w_cq, w_ck, w_cv, w_co, vectors = assemble(
        grid,
        positions,
        cross_a,
        cross_b,
        [(n * width, width, n, 0) for n in range(4)] + [(4 * width, 128, 4, 0)],
        [(own_rows, width)] * 4 + [(own_rows, 128)],
    )
    vectors = vectors[:, :6].T.astype(F32)
    gain1, bias1, gain2, bias2, gain3, bias3 = [vectors[n] for n in range(6)]
    first, normal1, scale1 = norm_forward(
        ALPHA_RES * hidden.astype(F32) + matmul(after(self_att, *cross_got), w_so), gain1, bias1
    )
    first_low = first.astype(BF)
    cq = matmul(first_low, w_cq).astype(BF)
    mk = matmul(mem_all, w_ck).astype(BF)
    mv = matmul(mem_all, w_cv).astype(BF)
    ffn_pair = ffn_ag.second(cq, mk, mv)
    cross_att, cross_sums = cross_forward(window, row, rows, after(cq, *ffn_pair), mk, mv)
    second, normal2, scale2 = norm_forward(
        ALPHA_RES * first + matmul(cross_att, w_co), gain2, bias2
    )
    second_low = second.astype(BF)
    second_t = turn(grid, positions, second_low)
    self_att_t = turn(grid, positions, self_att)
    first_t = turn(grid, positions, first_low)
    cross_att_t = turn(grid, positions, cross_att)
    turned = (hidden_t, mem_t, second_t, self_att_t, first_t, cross_att_t)
    ffn_a, ffn_b = ffn_ag.cores(*turned)
    w_up, w_down = assemble(
        grid,
        positions,
        ffn_a,
        ffn_b,
        [(0, ffn, 0, 0)] + [(ffn + n * width, width, 1, n * own_rows) for n in range(many)],
        [(own_rows, ffn), (own_rows * many, width)],
    )
    pre = matmul(second_low, w_up)
    erf = 1.0 + lax.erf(pre * (0.5**0.5))
    act = (0.5 * pre * erf).astype(BF)
    slope = 0.5 * erf + pre * jnp.exp(-0.5 * pre * pre) * 0.3989422804014327
    third, normal3, scale3 = norm_forward(ALPHA_RES * second + matmul(act, w_down), gain3, bias3)

    grad_third, g_gain3, g_bias3 = norm_backward(cotangent.astype(F32), normal3, scale3, gain3)
    third_low = grad_third.astype(BF)
    down = Reduction(grid, [(turn(grid, positions, act), third_low)])
    down.start()
    down.cores()
    grad_pre = (slope * outer_right(after(third_low, down.away), w_down)).astype(BF)
    down.wait(grad_pre)
    down_kept = down.keep()
    down.first()
    up = Reduction(grid, [(second_t, after(grad_pre, *down_kept))])
    up.start()
    up.cores()
    grad_second = ALPHA_RES * grad_third + outer_right(after(grad_pre, up.away), w_up)
    up.wait(grad_second)
    up_kept = up.keep()
    grad_mid, g_gain2, g_bias2 = norm_backward(
        after(grad_second, *up_kept), normal2, scale2, gain2
    )
    mid_low = grad_mid.astype(BF)
    grad_catt = outer_right(mid_low, w_co).astype(BF)
    down.wait(grad_catt)
    down_kept = down.add_first()
    down.second()
    up.hold(*down_kept)
    up.first()
    unit = jnp.eye(128, dtype=BF)

    def spread(vectors):
        vectors = jnp.pad(jnp.stack(vectors).astype(BF), ((0, 128 - len(vectors)), (0, 0)))
        return turn(grid, positions, vectors), unit

    cross_norms = spread([g_gain2, g_bias2, g_gain3, g_bias3])
    grad_cq, grad_mk, grad_mv = cross_backward(
        window,
        row,
        rows,
        cross_sums,
        cq,
        mk,
        mv,
        cross_att,
        after(grad_catt, *down_kept, cross_norms[0]),
    )
    cross = Reduction(
        grid,
        [(cross_att_t, mid_low), (first_t, grad_cq), (mem_t, grad_mk), (mem_t, grad_mv), cross_norms],
    )
    cross.start()
    cross.cores(*down.got_a, *down.got_b, *up.got_a, *up.got_b)
    down.wait(cross.away)
    down_kept = down.add_second()
    down.last()
    up.wait(*down_kept)
    up_kept = up.add_first()
    up.second()
    grad_first = ALPHA_RES * grad_mid + outer_right(after(grad_cq, cross.away, *up_kept), w_cq)
    grad_res, g_gain1, g_bias1 = norm_backward(grad_first, normal1, scale1, gain1)
    res_low = grad_res.astype(BF)
    grad_satt = outer_right(res_low, w_so).astype(BF)
    own_norms = spread([g_gain1, g_bias1])
    cross.wait(grad_satt, own_norms[0])
    cross_kept = cross.keep()
    up.wait(*cross_kept)
    up_kept = up.add_second()
    cross.hold(*up_kept, *down.got_a)
    cross.first()
    up.a = [after(a, *down.got_a) for a in up.a]
    up.last()
    grad_q, grad_k, grad_v = self_backward(
        pad_length,
        column,
        row,
        self_sums,
        q,
        k,
        v,
        self_att,
        after(grad_satt, *cross_kept, *up_kept, *down.got_a),
    )
    own = Reduction(
        grid,
        [(self_att_t, res_low), (hidden_t, grad_q), (hidden_t, grad_k), (hidden_t, grad_v), own_norms],
    )
    own.start()
    own.cores(*cross.got_a, *cross.got_b, *up.got_a)
    cross.wait(own.away)
    cross_kept = cross.add_first()
    cross.second()
    grad_in = ALPHA_RES * grad_res + outer_right(after(grad_q, own.away, *cross_kept), w_sq)
    own.wait(grad_in)
    own_kept = own.keep()
    own.hold(*cross.got_a, *cross.got_b)
    own.first()
    cross.wait(*own_kept)
    cross_kept = cross.add_second()
    cross.last()
    grad_in = grad_in + outer_right(after(grad_k, *own_kept), w_sk) + outer_right(grad_v, w_sv)
    grad_mem = outer_right(after(grad_mk, *own_kept), w_ck) + outer_right(grad_mv, w_cv)
    grad_mem = grad_mem.reshape(ny, 2, mem_rows, width)
    mem_own = [lax.dynamic_index_in_dim(grad_mem, n ^ here["c"], 1, keepdims=False) for n in range(2)]
    mem_away = mem_own[1].astype(BF)
    (out_down,) = down.finish([width])
    (out_up,) = up.finish([ffn])
    own.wait(out_down, out_up, mem_away, mem_own[0], grad_in, *cross.got_a)
    own_got = own.got_a + own.got_b
    own_kept = own.add_first()
    own.second()
    mem_own = mem_own[0] + grid.exchange(after(mem_away, *own_got), "c", 1).astype(F32)
    mem_own = [lax.dynamic_index_in_dim(mem_own, n ^ here["y"], 0, keepdims=False) for n in range(ny)]
    mem_away = [a.astype(BF) for a in mem_own[1:]]
    out_mem = mem_own[0]
    for n in range(1, ny):
        got = grid.exchange(after(mem_away[n - 1], *own.got_a, *own.got_b), "y", n)
        out_mem = out_mem + got.astype(F32)
    out_co, out_cq, out_ck, out_cv, late = cross.finish([width] * 4 + [128])
    own.wait(out_co)
    own.add_second()
    own.last()
    out_so, out_sq, out_sk, out_sv, last = own.finish([width] * 4 + [128])
    norms = [last[:, 0], last[:, 1]] + [late[:, n] for n in range(4)]
    return (
        third.astype(BF),
        grad_in,
        out_mem,
        out_sq,
        out_sk,
        out_sv,
        out_so,
        norms[0],
        norms[1],
        out_cq,
        out_ck,
        out_cv,
        out_co,
        norms[2],
        norms[3],
        out_up,
        out_down,
        norms[4],
        norms[5],
    )


def solution(mesh):
    grid = Grid(mesh.shape["dp"], mesh.shape["ctx"])
    row, flat = P(BOTH, None), P(BOTH)
    block = (row,) * 4 + (flat,) * 2
    return jax.shard_map(
        functools.partial(body, grid),
        mesh=mesh,
        in_specs=(row, row, row, row, flat, flat) + block + block + (row, row, flat, flat),
        out_specs=(row, row, row) + block + block + (row, row, flat, flat),
        check_vma=False,
    )
```

```python
import functools

import jax
import jax.numpy as jnp
from jax import lax
from jax.experimental import pallas as pl
from jax.experimental.pallas import tpu as pltpu
from jax.sharding import PartitionSpec as P

HD = 64
ALPHA_RES = 4.16
EPSILON = 1e-05
MASKED = -1e30
SCORE_SCALE = 0.125
BF = jnp.bfloat16
F32 = jnp.float32
BOTH = ("dp", "ctx")


class Grid:
    def __init__(self, dp, ctx):
        y = ctx // 2
        x = y
        self.size = {"z": dp // x, "x": x, "y": y, "c": 2}
        self.total = dp * ctx

    def index(self, coords):
        value = 0
        for name in "zxyc":
            value = value * self.size[name] + coords[name]
        return value

    def coords(self, index):
        out = {}
        for name in "cyxz":
            out[name] = index % self.size[name]
            index = index // self.size[name]
        return out

    def here(self):
        dp, ctx = lax.axis_index("dp"), lax.axis_index("ctx")
        nx = self.size["x"]
        return {"z": dp // nx, "x": dp % nx, "y": ctx // 2, "c": ctx % 2}

    def exchange(self, array, name, bit):
        pairs = []
        for source in range(self.total):
            coords = self.coords(source)
            coords[name] ^= bit
            pairs.append((source, self.index(coords)))
        return lax.ppermute(array, BOTH, pairs)

    def others(self, array, name):
        return [self.exchange(array, name, k) for k in range(1, self.size[name])]

    def blocks(self):
        nz, nx, ny = self.size["z"], self.size["x"], self.size["y"]
        out = []
        for c in range(2):
            out += [(z, x, y, c) for x in range(nx) for y in range(ny) for z in range(nz // 2)]
            out += [(z, x, y, c) for y in range(ny) for x in range(nx) for z in range(nz // 2, nz)]
        return out

    def positions(self):
        here = self.here()
        return jnp.stack(
            [
                self.index({name: k ^ here[name] for name, k in zip("zxyc", block)})
                for block in self.blocks()
            ]
        ).astype(jnp.int32)


def after(value, *before):
    return lax.optimization_barrier((value,) + before)[0]


SHORT = pl.CostEstimate(flops=1, bytes_accessed=1, transcendentals=0)
call = functools.partial(pl.pallas_call, cost_estimate=SHORT)


def params(mib=16):
    return pltpu.CompilerParams(vmem_limit_bytes=mib * 2**20)


def full(shape):
    return pl.BlockSpec(shape, lambda *_: (0,) * len(shape))


SCALARS = pl.BlockSpec(memory_space=pltpu.SMEM)
ANYWHERE = pl.BlockSpec(memory_space=pl.ANY)


def side_by_side(arrays):
    widths = [a.shape[1] for a in arrays]

    def kernel(*refs):
        at = 0
        for ref, width in zip(refs, widths):
            refs[-1][:, at : at + width] = ref[...]
            at += width

    return call(
        kernel, out_shape=jax.ShapeDtypeStruct((arrays[0].shape[0], sum(widths)), BF)
    )(*arrays)


def stack(groups):
    flat = [a for group in groups for a in group]

    def kernel(*refs):
        outs, sems = refs[len(flat) : -1], refs[-1]
        started = []
        for group, out in zip(groups, outs):
            for n in range(len(group)):
                at = len(started)
                started.append(pltpu.make_async_copy(refs[at], out.at[n], sems.at[at]))
        for copy in started:
            copy.start()
        for copy in started:
            copy.wait()

    return list(call(
        kernel,
        out_shape=[
            jax.ShapeDtypeStruct((len(group),) + group[0].shape, group[0].dtype) for group in groups
        ],
        in_specs=[ANYWHERE] * len(flat),
        out_specs=[pl.BlockSpec(memory_space=pltpu.VMEM)] * len(groups),
        scratch_shapes=[pltpu.SemaphoreType.DMA((len(flat),))],
        compiler_params=params(),
    )(*flat))


def assemble(grid, positions, part_a, part_b, parts, shapes):
    blocks = grid.blocks()
    nx, ny, nz = (grid.size[name] for name in "xyz")
    rows = part_a[0][0].shape[2]
    arrays = [a for part in part_a + part_b for a in part]

    def kernel(where, *refs):
        sources = refs[: len(arrays)]
        targets = refs[len(arrays) : -1]
        sems = refs[-1]
        started = []
        for column, width, result, at in parts:
            for n, (z, x, y, c) in enumerate(blocks):
                if z < nz // 2:
                    source = sources[c * ny + y].at[x, z]
                else:
                    source = sources[2 * ny + c * nx + x].at[y, z - nz // 2]
                started.append(
                    pltpu.make_async_copy(
                        source.at[:, pl.ds(column, width)],
                        targets[result].at[where[n], pl.ds(at, rows), :],
                        sems.at[len(started)],
                    )
                )
        for copy in started:
            copy.start()
        for copy in started:
            copy.wait()

    out = call(
        kernel,
        out_shape=[jax.ShapeDtypeStruct((len(blocks),) + shape, BF) for shape in shapes],
        in_specs=[SCALARS] + [ANYWHERE] * len(arrays),
        out_specs=[pl.BlockSpec(memory_space=pltpu.VMEM)] * len(shapes),
        scratch_shapes=[pltpu.SemaphoreType.DMA((len(parts) * len(blocks),))],
        compiler_params=params(4 + len(blocks) * sum(m * n for m, n in shapes) // 2**19),
    )(positions, *arrays)
    return [a.reshape(-1, a.shape[2]) for a in out]


def turn(grid, positions, left):
    tokens, width = left.shape
    rows = width // grid.total

    def kernel(where, left_ref, out_ref, turned):
        turned[...] = left_ref[...].T
        for n in range(grid.total):
            at = pl.multiple_of(where[n] * rows, rows)
            out_ref[n * rows : (n + 1) * rows, :] = turned[pl.ds(at, rows), :]

    return call(
        kernel,
        out_shape=jax.ShapeDtypeStruct((width, tokens), BF),
        in_specs=[SCALARS, pl.BlockSpec(memory_space=pltpu.VMEM)],
        out_specs=pl.BlockSpec(memory_space=pltpu.VMEM),
        scratch_shapes=[pltpu.VMEM((width, tokens), BF)],
        compiler_params=params(),
    )(positions, left)


def products(pairs, core, groups, got=None):
    rows = pairs[0][0].shape[0] // 2
    if len(pairs) == 1:
        width = pairs[0][1].shape[1]
        block = min(width, 1024)
        if width == block:
            block = width // 2
        steps = width // block
    else:
        block = pairs[0][1].shape[1]
        steps = len(pairs)
        width = sum(b.shape[1] for _, b in pairs)
    starts = [sum(groups[:n]) for n in range(len(groups))]

    def kernel(*refs):
        lefts, rights = refs[: len(pairs)], refs[len(pairs) : 2 * len(pairs)]
        rest = refs[2 * len(pairs) :]
        got_ref, outs = (None, rest) if got is None else (rest[0], rest[1:])

        def run(left, right):
            for start, size, out in zip(starts, groups, outs):
                value = matmul(left[start : start + size, :], right[...])
                cols = slice(0, right.shape[1])
                if got_ref is not None:
                    value = value + got_ref[start : start + size, cols].astype(F32)
                out[:, cols] = value.astype(BF)

        if len(pairs) == 1:
            run(lefts[0], rights[0])
        else:
            for n in range(len(pairs)):
                @pl.when(pl.program_id(0) == n)
                def _():
                    run(lefts[n], rights[n])

    left_specs = [pl.BlockSpec((rows, a.shape[1]), lambda n: (core, 0)) for a, _ in pairs]
    if len(pairs) == 1:
        right_specs = [pl.BlockSpec((pairs[0][1].shape[0], block), lambda n: (0, n))]
    else:
        right_specs = [full(b.shape) for _, b in pairs]
    operands = [a for a, _ in pairs] + [b for _, b in pairs]
    got_specs = []
    if got is not None:
        operands.append(got)
        got_specs = [pl.BlockSpec((rows, block), lambda n: (0, n))]
    return call(
        kernel,
        grid=(steps,),
        out_shape=[jax.ShapeDtypeStruct((size, width), BF) for size in groups],
        in_specs=left_specs + right_specs + got_specs,
        out_specs=[pl.BlockSpec((size, block), lambda n: (0, n)) for size in groups],
        compiler_params=params(),
    )(*operands)


def add_split(sums, counts):
    rows = [arrays[0].shape[0] for arrays in sums]
    width = sums[0][0].shape[1]
    steps = next(n for n in (2, 3, 1) if width % (n * 128) == 0)

    def kernel(*refs):
        at = 0
        out = sum(len(arrays) for arrays in sums)
        for arrays, count, total in zip(sums, counts, rows):
            each = total // count
            for n in range(count):
                value = refs[at][n * each : (n + 1) * each, :].astype(F32)
                for m in range(1, len(arrays)):
                    value = value + refs[at + m][n * each : (n + 1) * each, :].astype(F32)
                refs[out + n][...] = value.astype(BF)
            at += len(arrays)
            out += count

    block = width // steps
    out = call(
        kernel,
        grid=(steps,),
        out_shape=[
            jax.ShapeDtypeStruct((total // count, width), BF)
            for count, total in zip(counts, rows)
            for _ in range(count)
        ],
        in_specs=[
            pl.BlockSpec((total, block), lambda n: (0, n))
            for arrays, total in zip(sums, rows)
            for _ in arrays
        ],
        out_specs=[
            pl.BlockSpec((total // count, block), lambda n: (0, n))
            for count, total in zip(counts, rows)
            for _ in range(count)
        ],
        compiler_params=params(),
    )(*[a for arrays in sums for a in arrays])
    split, at = [], 0
    for count in counts:
        split.append(list(out[at : at + count]))
        at += count
    return split


def ffn_fits(grid, ffn):
    return ffn // grid.total % 128 == 0


def ffn_layer(grid, positions, part_a, part_b, second, cotangent, gain, bias):
    tokens, width = second.shape
    blocks = grid.blocks()
    count = len(blocks)
    nx, ny, nz = (grid.size[name] for name in "xyz")
    arrays = [a for part in part_a + part_b for a in part]
    rows = arrays[0].shape[2]
    ffn = arrays[0].shape[3] // 2
    each = ffn // count
    many = each // rows
    group = max(1, 512 // each)
    chunk = group * each
    piece = 64

    def kernel(where, second_ref, cot_ref, gain_ref, bias_ref, *refs):
        sources = refs[: len(arrays)]
        out_ref, low_ref, second_grad, act_t, pre_grad, g_gain, g_bias = refs[len(arrays) : len(arrays) + 7]
        up, down, slope, total, pre, act, low, sems = refs[len(arrays) + 7 :]

        def source(n):
            z, x, y, c = blocks[n]
            if z < nz // 2:
                return sources[c * ny + y].at[x, z]
            return sources[2 * ny + c * nx + x].at[y, z - nz // 2]

        up_copies, down_copies = [], []
        for n in range(count):
            at = pl.multiple_of(where[n] * rows, rows)
            up_copies.append(
                pltpu.make_async_copy(
                    source(n).at[:, pl.ds(0, ffn)], up.at[pl.ds(at, rows), :], sems.at[n]
                )
            )
        for n in range(count):
            for m in range(many):
                down_copies.append(
                    pltpu.make_async_copy(
                        source(n).at[:, pl.ds(ffn + m * width, width)],
                        down.at[pl.ds(n * each + m * rows, rows), :],
                        sems.at[count + n * many + m],
                    )
                )
        for copy in up_copies + down_copies:
            copy.start()
        low[...] = second_ref[...].astype(BF)
        for copy in up_copies:
            copy.wait()

        def units(n):
            return pl.ds(pl.multiple_of(where[n] * each, each), each)

        for g in range(count // group):
            mine = slice(g * chunk, (g + 1) * chunk)
            slot = g % 2
            here = [up[:, units(g * group + n)] for n in range(group)]
            pre[slot] = matmul(low[...], jnp.concatenate(here, axis=1))
            for start in range(0, tokens, piece):
                some = slice(start, start + piece)
                x = pre[slot, some, :]
                erf = 1.0 + lax.erf(x * (0.5**0.5))
                act[slot, some, :] = (0.5 * x * erf).astype(BF)
                slope[some, mine] = (
                    0.5 * erf + x * jnp.exp(-0.5 * x * x) * 0.3989422804014327
                ).astype(BF)
            act_t[mine, :] = act[slot].T
            for copy in down_copies[g * group * many : (g + 1) * group * many]:
                copy.wait()
            value = matmul(act[slot], down[mine, :])
            if g == 0:
                total[...] = value
            else:
                total[...] += value

        gains, biases = 0.0, 0.0
        for start in range(0, tokens, piece):
            some = slice(start, start + piece)
            value, normal, scale = norm_forward(
                ALPHA_RES * second_ref[some, :] + total[some, :], gain_ref[...], bias_ref[...]
            )
            out_ref[some, :] = value.astype(BF)
            grad, one, two = norm_backward(cot_ref[some, :].astype(F32), normal, scale, gain_ref[...])
            gains, biases = gains + one.reshape(1, -1), biases + two.reshape(1, -1)
            total[some, :] = grad
            low_ref[some, :] = grad.astype(BF)
        g_gain[...] = gains
        g_bias[...] = biases

        for g in range(count // group):
            mine = slice(g * chunk, (g + 1) * chunk)
            value = (across(low_ref[...], down[mine, :]) * slope[:, mine].astype(F32)).astype(BF)
            for n in range(group):
                pre_grad[:, units(g * group + n)] = value[:, n * each : (n + 1) * each]
        for start in range(0, width, 256):
            some = slice(start, start + 256)
            second_grad[:, some] = ALPHA_RES * total[:, some] + across(pre_grad[...], up[some, :])

    vmem = pl.BlockSpec(memory_space=pltpu.VMEM)
    shapes = [
        ((tokens, width), BF),
        ((tokens, width), BF),
        ((tokens, width), F32),
        ((ffn, tokens), BF),
        ((tokens, ffn), BF),
        ((1, width), F32),
        ((1, width), F32),
    ]
    return call(
        kernel,
        out_shape=[jax.ShapeDtypeStruct(shape, dtype) for shape, dtype in shapes],
        in_specs=[SCALARS] + [vmem] * 4 + [ANYWHERE] * len(arrays),
        out_specs=[vmem] * len(shapes),
        scratch_shapes=[
            pltpu.VMEM((width, ffn), BF),
            pltpu.VMEM((ffn, width), BF),
            pltpu.VMEM((tokens, ffn), BF),
            pltpu.VMEM((tokens, width), F32),
            pltpu.VMEM((2, tokens, chunk), F32),
            pltpu.VMEM((2, tokens, chunk), BF),
            pltpu.VMEM((tokens, width), BF),
            pltpu.SemaphoreType.DMA((count * (1 + many),)),
        ],
        compiler_params=params(60),
    )(positions, second, cotangent, gain.reshape(1, -1), bias.reshape(1, -1), *arrays)


class Reduction:
    def __init__(self, grid, pairs):
        self.grid = grid
        self.pairs = pairs
        self.rows = pairs[0][0].shape[0]
        self.got, self.got_a, self.got_b = None, [], []

    def start(self):
        (self.away,) = products(self.pairs, 1, [self.rows // 2])
        return self.away

    def wait(self, *before):
        if self.got is not None:
            self.got = after(self.got, *before)
        self.got_a = [after(a, *before) for a in self.got_a]
        self.got_b = [after(b, *before) for b in self.got_b]

    def cores(self, *before):
        away = after(self.away, *before) if before else self.away
        self.got = self.grid.exchange(away, "c", 1)

    def keep(self):
        nx, ny = self.grid.size["x"], self.grid.size["y"]
        quarter = self.rows // 4
        outs = products(
            self.pairs, 0, [quarter // nx] * nx + [quarter // ny] * ny, self.got
        )
        self.got = None
        self.a, self.b = list(outs[:nx]), list(outs[nx:])
        return self.a + self.b

    def hold(self, *before):
        self.a = list(lax.optimization_barrier(tuple(self.a) + before)[: len(self.a)])
        self.b = list(lax.optimization_barrier(tuple(self.b) + before)[: len(self.b)])

    def send(self, name_a, name_b):
        self.got_a = [self.grid.exchange(a, name_a, k + 1) for k, a in enumerate(self.a[1:])]
        self.got_b = [self.grid.exchange(b, name_b, k + 1) for k, b in enumerate(self.b[1:])]
        return self.got_a + self.got_b

    def first(self):
        return self.send("x", "y")

    def add_first(self):
        counts = [self.grid.size["y"], self.grid.size["x"]]
        self.a, self.b = add_split([[self.a[0]] + self.got_a, [self.b[0]] + self.got_b], counts)
        return self.a + self.b

    def second(self):
        return self.send("y", "x")

    def add_second(self):
        half = self.grid.size["z"] // 2
        low, high = add_split([[self.a[0]] + self.got_a, [self.b[0]] + self.got_b], [half, half])
        self.a = low + high
        return self.a

    def last(self):
        self.got_a = [self.grid.exchange(a, "z", k + 1) for k, a in enumerate(self.a[1:])]
        self.got_b = []
        return self.got_a

    def finish(self, widths):
        arrays = [self.a[0]] + self.got_a

        def kernel(*refs):
            at = 0
            for width, out in zip(widths, refs[len(arrays) :]):
                value = refs[0][:, at : at + width].astype(F32)
                for ref in refs[1 : len(arrays)]:
                    value = value + ref[:, at : at + width].astype(F32)
                out[...] = value
                at += width

        return call(
            kernel,
            out_shape=[jax.ShapeDtypeStruct((self.a[0].shape[0], width), F32) for width in widths],
            compiler_params=params(),
        )(*arrays)


def matmul(left, right):
    return jnp.dot(left, right, preferred_element_type=F32)


def outer_right(left, right):
    return lax.dot_general(left, right, (((1,), (1,)), ((), ())), preferred_element_type=F32)


def norm_forward(resid, gain, bias):
    center = resid - jnp.mean(resid, axis=-1, keepdims=True)
    scale = lax.rsqrt(jnp.mean(center * center, axis=-1, keepdims=True) + EPSILON)
    normal = center * scale
    return normal * gain + bias, normal, scale


def norm_backward(dy, normal, scale, gain):
    dn = dy * gain
    grad = (
        dn
        - jnp.mean(dn, axis=-1, keepdims=True)
        - normal * jnp.mean(dn * normal, axis=-1, keepdims=True)
    ) * scale
    return grad, jnp.sum(dy * normal, axis=0), jnp.sum(dy, axis=0)


PAIR = 2 * HD
BLOCK = 256
DIMS_NT = (((1,), (1,)), ((), ()))


def head_of(array, which, scale=None):
    lane = lax.broadcasted_iota(jnp.int32, array.shape, 1)
    mine = (lane < HD) if which == 0 else (lane >= HD)
    out = jnp.where(mine, array.astype(F32), 0.0)
    return (out if scale is None else out * scale).astype(BF)


def across(left, right):
    return lax.dot_general(left, right, DIMS_NT, preferred_element_type=F32)


def pair_forward(q, k, v_t, bias):
    probs, sums = [], []
    for n in range(2):
        scores = across(k, head_of(q, n, SCORE_SCALE)) + bias
        peak = jnp.max(scores, axis=0, keepdims=True)
        exponent = jnp.exp(scores - peak)
        total = jnp.sum(exponent, axis=0, keepdims=True)
        probs.append((exponent * (1.0 / total)).astype(BF))
        sums.append(peak + jnp.log(total))
    outs = [matmul(v_t[n * HD : (n + 1) * HD, :], probs[n]) for n in range(2)]
    return jnp.concatenate(outs, axis=0).T.astype(BF), sums


TILE = 128
FORWARD = 40
BACKWARD = 40


def pair_backward(tiles, keys, bias_ref, sums_ref, q, k, v, out, grad, probs_ref, dscores_ref):
    length = q.shape[0]
    q_one = [head_of(q, n, SCORE_SCALE) for n in range(2)]
    g_one = [head_of(grad, n) for n in range(2)]
    both = (grad.astype(F32) * out.astype(F32)).T
    delta = [jnp.sum(both[n * HD : (n + 1) * HD, :], axis=0, keepdims=True) for n in range(2)]
    for key, query in tiles:
        down, over = slice(key, key + TILE), slice(query, query + BLOCK)
        for n in range(2):
            scores = across(k[down, :], q_one[n][over, :]) + bias_ref[down, over]
            probs = jnp.exp(scores - sums_ref[0, n : n + 1, over])
            dprob = across(v[down, :], g_one[n][over, :])
            at = slice(n * length + query, n * length + query + BLOCK)
            probs_ref[down, at] = probs.astype(BF)
            dscores_ref[down, at] = (probs * (dprob - delta[n][:, over])).astype(BF)
    k_t = k.T
    gq = [
        matmul(k_t[n * HD : (n + 1) * HD, :], dscores_ref[:keys, n * length : (n + 1) * length])
        for n in range(2)
    ]
    gq = jnp.concatenate(gq, axis=0).T * SCORE_SCALE
    gk = matmul(dscores_ref[:keys, :], jnp.concatenate(q_one, axis=0))
    gv = matmul(probs_ref[:keys, :], jnp.concatenate(g_one, axis=0))
    return gq.astype(BF), gk.astype(BF), gv.astype(BF)


def self_bias(column, row, pad):
    length = column.shape[0]
    at_k = lax.broadcasted_iota(jnp.int32, (length, length), 0)
    at_q = lax.broadcasted_iota(jnp.int32, (length, length), 1)
    live = (column == row) & (at_q >= at_k) & ((at_k < length - pad) | (at_q == at_k))
    return jnp.where(live, 0.0, MASKED)


def pair_spec(array):
    return pl.BlockSpec((array.shape[0], PAIR), lambda n: (0, n))


def sums_spec(length):
    return pl.BlockSpec((1, 8, length), lambda n: (n, 0, 0))


def whole_spec(array):
    return pl.BlockSpec(array.shape, lambda n: (0,) * array.ndim)


def self_forward(pad, column, row, q, k, v):
    length, width = q.shape

    def kernel(pad_ref, column_ref, row_ref, q_ref, k_ref, v_ref, out_ref, sums_ref, bias_ref):
        @pl.when(pl.program_id(0) == 0)
        def _():
            bias_ref[...] = self_bias(column_ref[...], row_ref[...], pad_ref[0])

        v_t = v_ref[...].T
        for start in range(0, length, BLOCK):
            mine, seen = slice(start, start + BLOCK), slice(0, start + BLOCK)
            out_ref[mine, :], sums = pair_forward(
                q_ref[mine, :], k_ref[seen, :], v_t[:, seen], bias_ref[seen, mine]
            )
            for n in range(2):
                sums_ref[0, n : n + 1, mine] = sums[n]

    return call(
        kernel,
        grid=(width // PAIR,),
        out_shape=[
            jax.ShapeDtypeStruct(q.shape, BF),
            jax.ShapeDtypeStruct((width // PAIR, 8, length), F32),
        ],
        in_specs=[pl.BlockSpec(memory_space=pltpu.SMEM), whole_spec(column), whole_spec(row)]
        + [pair_spec(q)] * 3,
        out_specs=[pair_spec(q), sums_spec(length)],
        scratch_shapes=[pltpu.VMEM((length, length), F32)],
        compiler_params=params(FORWARD),
    )(pad, column, row, q, k, v)


def self_backward(pad, column, row, sums, q, k, v, out, grad):
    length, width = q.shape
    tiles = [
        (key, query)
        for query in range(0, length, BLOCK)
        for key in range(0, query + BLOCK, TILE)
    ]

    def kernel(pad_ref, column_ref, row_ref, sums_ref, *refs):
        q_ref, k_ref, v_ref, o_ref, g_ref, gq_ref, gk_ref, gv_ref, bias_ref, probs_ref, ds_ref = refs

        @pl.when(pl.program_id(0) == 0)
        def _():
            bias_ref[...] = self_bias(column_ref[...], row_ref[...], pad_ref[0])
            probs_ref[...] = jnp.zeros_like(probs_ref)
            ds_ref[...] = jnp.zeros_like(ds_ref)

        gq_ref[...], gk_ref[...], gv_ref[...] = pair_backward(
            tiles,
            length,
            bias_ref,
            sums_ref,
            q_ref[...],
            k_ref[...],
            v_ref[...],
            o_ref[...],
            g_ref[...],
            probs_ref,
            ds_ref,
        )

    return call(
        kernel,
        grid=(width // PAIR,),
        out_shape=[jax.ShapeDtypeStruct(q.shape, BF)] * 3,
        in_specs=[SCALARS, whole_spec(column), whole_spec(row), sums_spec(length)]
        + [pair_spec(q)] * 5,
        out_specs=[pair_spec(q)] * 3,
        scratch_shapes=[pltpu.VMEM((length, length), F32)]
        + [pltpu.VMEM((length, 2 * length), BF)] * 2,
        compiler_params=params(BACKWARD),
    )(pad, column, row, sums, q, k, v, out, grad)


def windows(total):
    return sorted({min(512, total), min(640, total), total})


def choose_window(segment, ids):
    total = ids.shape[0]
    at = jnp.arange(total, dtype=jnp.int32)
    live = (ids >= segment[0]) & (ids <= segment[-1])
    low = jnp.min(jnp.where(live, at, total))
    high = jnp.max(jnp.where(live, at + 1, 0))
    choice, starts, rows = jnp.int32(0), [], []
    for size in windows(total):
        start = jnp.clip(low // 16 * 16, 0, total - size)
        starts.append(start)
        rows.append(lax.dynamic_slice(ids, (start,), (size,)).reshape(size, 1))
        choice = choice + (high - start > size).astype(jnp.int32)
    return jnp.stack([choice] + starts), rows


def on_window(window_ref, total, run):
    for n, size in enumerate(windows(total)):
        @pl.when(window_ref[0] == n)
        def _():
            run(n, size, pl.ds(pl.multiple_of(window_ref[1 + n], 16), size))


def cross_forward(window, column, rows, q, k, v):
    length, width = q.shape
    total = k.shape[0]

    def kernel(window_ref, column_ref, *refs):
        row_refs = refs[: len(rows)]
        q_ref, k_ref, v_ref, out_ref, sums_ref, bias_ref = refs[len(rows) :]

        def run(n, size, seen):
            @pl.when(pl.program_id(0) == 0)
            def _():
                bias_ref[:size, :] = jnp.where(row_refs[n][...] == column_ref[...], 0.0, MASKED)

            v_t = v_ref[seen, :].T
            for start in range(0, length, BLOCK):
                mine = slice(start, start + BLOCK)
                out_ref[mine, :], sums = pair_forward(
                    q_ref[mine, :], k_ref[seen, :], v_t, bias_ref[:size, mine]
                )
                for m in range(2):
                    sums_ref[0, m : m + 1, mine] = sums[m]

        on_window(window_ref, total, run)

    return call(
        kernel,
        grid=(width // PAIR,),
        out_shape=[
            jax.ShapeDtypeStruct(q.shape, BF),
            jax.ShapeDtypeStruct((width // PAIR, 8, length), F32),
        ],
        in_specs=[pl.BlockSpec(memory_space=pltpu.SMEM), whole_spec(column)]
        + [whole_spec(row) for row in rows]
        + [pair_spec(q), pair_spec(k), pair_spec(v)],
        out_specs=[pair_spec(q), sums_spec(length)],
        scratch_shapes=[pltpu.VMEM((total, length), F32)],
        compiler_params=params(FORWARD),
    )(window, column, *rows, q, k, v)


def cross_backward(window, row, ids, sums, q, k, v, out, grad):
    length, width = q.shape
    total = k.shape[0]

    def kernel(window_ref, row_ref, sums_ref, *refs):
        id_refs = refs[: len(ids)]
        q_ref, k_ref, v_ref, o_ref, g_ref, gq_ref, gk_ref, gv_ref, bias_ref, probs_ref, ds_ref = refs[
            len(ids) :
        ]

        def run(n, size, seen):
            @pl.when(pl.program_id(0) == 0)
            def _():
                bias_ref[:size, :] = jnp.where(id_refs[n][...] == row_ref[...], 0.0, MASKED)

            if size < total:
                gk_ref[...] = jnp.zeros_like(gk_ref)
                gv_ref[...] = jnp.zeros_like(gv_ref)
            tiles = [
                (key, query)
                for query in range(0, length, BLOCK)
                for key in range(0, size, TILE)
            ]
            gq_ref[...], gk_ref[seen, :], gv_ref[seen, :] = pair_backward(
                tiles,
                size,
                bias_ref,
                sums_ref,
                q_ref[...],
                k_ref[seen, :],
                v_ref[seen, :],
                o_ref[...],
                g_ref[...],
                probs_ref,
                ds_ref,
            )

        on_window(window_ref, total, run)

    return call(
        kernel,
        grid=(width // PAIR,),
        out_shape=[jax.ShapeDtypeStruct(a.shape, BF) for a in (q, k, v)],
        in_specs=[SCALARS, whole_spec(row), sums_spec(length)]
        + [whole_spec(a) for a in ids]
        + [pair_spec(q), pair_spec(k), pair_spec(v), pair_spec(q), pair_spec(q)],
        out_specs=[pair_spec(q), pair_spec(k), pair_spec(v)],
        scratch_shapes=[pltpu.VMEM((total, length), F32)]
        + [pltpu.VMEM((total, 2 * length), BF)] * 2,
        compiler_params=params(BACKWARD),
    )(window, row, sums, *ids, q, k, v, out, grad)


def body(
    grid,
    hidden,
    memory,
    cotangent,
    dec_segment,
    pad_length,
    mem_segment,
    self_query,
    self_key,
    self_value,
    self_output,
    norm1_gain,
    norm1_bias,
    cross_query,
    cross_key,
    cross_value,
    cross_output,
    norm2_gain,
    norm2_bias,
    ffn_up,
    ffn_down,
    norm3_gain,
    norm3_bias,
):
    width = hidden.shape[1]
    ffn = ffn_up.shape[1]
    mem_rows = memory.shape[0]
    own_rows = self_query.shape[0]
    nx, ny, nz = grid.size["x"], grid.size["y"], grid.size["z"]
    here = grid.here()
    positions = grid.positions()

    def gather_z(piece):
        return [piece] + grid.others(piece, "z")

    def stacked(line, *before):
        line = [after(a, *before) for a in line] if before else line
        return stack([line[: nz // 2], line[nz // 2 :]])

    def hold(pair, *before):
        return after(pair[0], *before), after(pair[1], *before)

    class Gather:
        def first(self, pair):
            self.pair = pair
            self.got = grid.others(pair[0], "x"), grid.others(pair[1], "y")
            return self.got[0] + self.got[1]

        def second(self, *before):
            got = [[after(a, *before) for a in part] if before else part for part in self.got]
            self.pair = stack([[a] + part for a, part in zip(self.pair, got)])
            self.got = grid.others(self.pair[0], "y"), grid.others(self.pair[1], "x")
            self.core = [[grid.exchange(a, "c", 1)] for a in self.pair]
            return self.pair

        def cores(self, *before):
            got = [[after(a, *before) for a in part] if before else part for part in self.got]
            out = []
            for a, part, core in zip(self.pair, got, self.core):
                out.append([[a] + part, core + [grid.exchange(b, "c", 1) for b in part]])
            return out

    vectors = [norm1_gain, norm1_bias, norm2_gain, norm2_bias, norm3_gain, norm3_bias]
    vectors = jnp.pad(jnp.stack(vectors, axis=1).astype(BF), ((0, 0), (0, 122)))
    self_piece = side_by_side([self_query, self_key, self_value, self_output])
    self_z = gather_z(self_piece)
    cross_piece = side_by_side([cross_query, cross_key, cross_value, cross_output, vectors])
    many = ffn_down.shape[0] // own_rows
    ffn_piece = side_by_side(
        [ffn_up] + [ffn_down[n * own_rows : (n + 1) * own_rows] for n in range(many)]
    )

    self_z = self_z[:1] + [after(a, cross_piece, ffn_piece) for a in self_z[1:]]

    self_ag, cross_ag, ffn_ag = Gather(), Gather(), Gather()
    mem_y = [memory] + grid.others(memory, "y")
    ids_y = [mem_segment] + grid.others(mem_segment, "y")
    self_pair = stacked(self_z, cross_piece, ffn_piece, *mem_y[1:], *ids_y[1:])
    self_ag.first(self_pair)
    cross_z = gather_z(after(cross_piece, *self_pair))
    mem_c = stack([[after(a, *self_z) for a in mem_y]])
    mem_c += grid.others(mem_c[0], "c")
    ids_c = [jnp.stack(ids_y)]
    ids_c += grid.others(ids_c[0], "c")
    self_pair = self_ag.second(*mem_c[1:], *ids_c[1:])
    cross_pair = stacked(cross_z, *self_pair)
    ffn_z = gather_z(after(ffn_piece, *cross_pair))
    self_a, self_b = self_ag.cores(*cross_pair)
    cross_ag.first(hold(cross_pair, *self_ag.got[0], *self_ag.got[1]))

    mem_blocks = jnp.stack(
        [(y ^ here["y"]) * 2 + (c ^ here["c"]) for c in range(2) for y in range(ny)]
    ).astype(jnp.int32)

    def place_kernel(where, *refs):
        target, sems = refs[2], refs[3]
        started = []
        for c in range(2):
            for y in range(ny):
                n = c * ny + y
                started.append(
                    pltpu.make_async_copy(refs[c].at[y], target.at[where[n]], sems.at[n])
                )
        for copy in started:
            copy.start()
        for copy in started:
            copy.wait()

    mem_all = call(
        place_kernel,
        out_shape=jax.ShapeDtypeStruct((2 * ny, mem_rows, width), BF),
        in_specs=[SCALARS, ANYWHERE, ANYWHERE],
        out_specs=pl.BlockSpec(memory_space=pltpu.VMEM),
        scratch_shapes=[pltpu.SemaphoreType.DMA((2 * ny,))],
        compiler_params=params(),
    )(mem_blocks, *mem_c).reshape(-1, width)
    ids_all = jnp.zeros((2 * ny, mem_rows), jnp.int32)
    for c in range(2):
        for y in range(ny):
            ids_all = lax.dynamic_update_slice(
                ids_all, ids_c[c][y][None], (mem_blocks[c * ny + y], 0)
            )
    ids_all = ids_all.reshape(-1)

    w_sq, w_sk, w_sv, w_so = assemble(
        grid,
        positions,
        self_a,
        self_b,
        [(n * width, width, n, 0) for n in range(4)],
        [(own_rows, width)] * 4,
    )

    segment = dec_segment.reshape(-1)
    column, row = segment.reshape(-1, 1), segment.reshape(1, -1)
    hidden_t = turn(grid, positions, hidden)
    mem_t = turn(grid, positions, mem_all)
    q = matmul(hidden, w_sq).astype(BF)
    k = matmul(hidden, w_sk).astype(BF)
    v = matmul(hidden, w_sv).astype(BF)
    cross_pair = cross_ag.second(w_sq)
    self_att, self_sums = self_forward(pad_length, column, row, after(q, *cross_pair), k, v)
    ffn_pair = stacked(ffn_z, self_att)
    window, rows = choose_window(segment, after(ids_all, *ffn_pair))
    cross_a, cross_b = cross_ag.cores(self_att)
    cross_got = cross_a[0][1:] + cross_b[0][1:]
    ffn_ag.first(hold(ffn_pair, *cross_got))
    w_cq, w_ck, w_cv, w_co, vectors = assemble(
        grid,
        positions,
        cross_a,
        cross_b,
        [(n * width, width, n, 0) for n in range(4)] + [(4 * width, 128, 4, 0)],
        [(own_rows, width)] * 4 + [(own_rows, 128)],
    )
    vectors = vectors[:, :6].T.astype(F32)
    gain1, bias1, gain2, bias2, gain3, bias3 = [vectors[n] for n in range(6)]
    first, normal1, scale1 = norm_forward(
        ALPHA_RES * hidden.astype(F32) + matmul(after(self_att, *cross_got), w_so), gain1, bias1
    )
    first_low = first.astype(BF)
    cq = matmul(first_low, w_cq).astype(BF)
    mk = matmul(mem_all, w_ck).astype(BF)
    mv = matmul(mem_all, w_cv).astype(BF)
    ffn_pair = ffn_ag.second(cq, mk, mv)
    cross_att, cross_sums = cross_forward(window, row, rows, after(cq, *ffn_pair), mk, mv)
    second, normal2, scale2 = norm_forward(
        ALPHA_RES * first + matmul(cross_att, w_co), gain2, bias2
    )
    second_low = second.astype(BF)
    second_t = turn(grid, positions, second_low)
    self_att_t = turn(grid, positions, self_att)
    first_t = turn(grid, positions, first_low)
    cross_att_t = turn(grid, positions, cross_att)
    turned = (hidden_t, mem_t, second_t, self_att_t, first_t, cross_att_t)
    ffn_a, ffn_b = ffn_ag.cores(*turned)
    if ffn_fits(grid, ffn):
        out, third_low, grad_second, act_t, grad_pre, g_gain3, g_bias3 = ffn_layer(
            grid, positions, ffn_a, ffn_b, second, cotangent, gain3, bias3
        )
        g_gain3, g_bias3 = g_gain3.reshape(-1), g_bias3.reshape(-1)
    else:
        w_up, w_down = assemble(
            grid,
            positions,
            ffn_a,
            ffn_b,
            [(0, ffn, 0, 0)] + [(ffn + n * width, width, 1, n * own_rows) for n in range(many)],
            [(own_rows, ffn), (own_rows * many, width)],
        )
        pre = matmul(second_low, w_up)
        erf = 1.0 + lax.erf(pre * (0.5**0.5))
        act = (0.5 * pre * erf).astype(BF)
        slope = 0.5 * erf + pre * jnp.exp(-0.5 * pre * pre) * 0.3989422804014327
        third, normal3, scale3 = norm_forward(
            ALPHA_RES * second + matmul(act, w_down), gain3, bias3
        )
        out = third.astype(BF)
        grad_third, g_gain3, g_bias3 = norm_backward(
            cotangent.astype(F32), normal3, scale3, gain3
        )
        third_low = grad_third.astype(BF)
        act_t = turn(grid, positions, act)
        grad_pre = (slope * outer_right(third_low, w_down)).astype(BF)
        grad_second = ALPHA_RES * grad_third + outer_right(grad_pre, w_up)

    down = Reduction(grid, [(act_t, third_low)])
    down.start()
    down.cores()
    up = Reduction(grid, [(second_t, after(grad_pre, down.away))])
    up.start()
    up.cores()
    grad_mid, g_gain2, g_bias2 = norm_backward(
        after(grad_second, up.away), normal2, scale2, gain2
    )
    mid_low = grad_mid.astype(BF)
    grad_catt = outer_right(mid_low, w_co).astype(BF)
    down.wait(grad_catt)
    down_kept = down.keep()
    down.first()
    up.wait(*down_kept)
    up_kept = up.keep()
    unit = jnp.eye(128, dtype=BF)

    def spread(vectors):
        vectors = jnp.pad(jnp.stack(vectors).astype(BF), ((0, 128 - len(vectors)), (0, 0)))
        return turn(grid, positions, vectors), unit

    cross_norms = spread([g_gain2, g_bias2, g_gain3, g_bias3])
    grad_cq, grad_mk, grad_mv = cross_backward(
        window,
        row,
        rows,
        cross_sums,
        cq,
        mk,
        mv,
        cross_att,
        after(grad_catt, *up_kept, cross_norms[0]),
    )
    down.wait(grad_cq)
    down_kept = down.add_first()
    down.second()
    up.hold(*down_kept)
    up.first()
    cross = Reduction(
        grid,
        [
            (cross_att_t, mid_low),
            (first_t, after(grad_cq, *down_kept)),
            (mem_t, grad_mk),
            (mem_t, grad_mv),
            cross_norms,
        ],
    )
    cross.start()
    cross.cores(*down.got_a, *down.got_b)
    grad_first = ALPHA_RES * grad_mid + outer_right(after(grad_cq, cross.away), w_cq)
    grad_res, g_gain1, g_bias1 = norm_backward(grad_first, normal1, scale1, gain1)
    res_low = grad_res.astype(BF)
    grad_satt = outer_right(res_low, w_so).astype(BF)
    own_norms = spread([g_gain1, g_bias1])
    grad_q, grad_k, grad_v = self_backward(
        pad_length,
        column,
        row,
        self_sums,
        q,
        k,
        v,
        self_att,
        after(grad_satt, own_norms[0]),
    )
    down.wait(grad_q)
    down_kept = down.add_second()
    down.last()
    up.wait(*down_kept)
    up_kept = up.add_first()
    up.second()
    cross.wait(*up_kept)
    cross_kept = cross.keep()
    cross.hold(*up.got_a, *up.got_b)
    cross.first()
    own = Reduction(
        grid,
        [
            (self_att_t, res_low),
            (hidden_t, after(grad_q, *cross_kept)),
            (hidden_t, grad_k),
            (hidden_t, grad_v),
            own_norms,
        ],
    )
    own.start()
    own.cores(*up.got_a, *up.got_b, *down.got_a)
    grad_in = ALPHA_RES * grad_res + outer_right(after(grad_q, own.away), w_sq)
    up.wait(grad_in)
    up_kept = up.add_second()
    up.a = [after(a, *down.got_a) for a in up.a]
    up.last()
    own.wait(grad_in, *up_kept)
    own_kept = own.keep()
    cross.wait(*up_kept, *own_kept)
    cross_kept = cross.add_first()
    cross.second()
    own.hold(*cross.got_a, *cross.got_b)
    own.first()
    cross.wait(*own_kept)
    cross_kept = cross.add_second()
    cross.a = [after(a, *up.got_a) for a in cross.a]
    cross.last()
    grad_in = grad_in + outer_right(after(grad_k, *own_kept), w_sk) + outer_right(grad_v, w_sv)
    grad_mem = outer_right(after(grad_mk, *own_kept), w_ck) + outer_right(grad_mv, w_cv)
    grad_mem = grad_mem.reshape(ny, 2, mem_rows, width)
    mem_own = [lax.dynamic_index_in_dim(grad_mem, n ^ here["c"], 1, keepdims=False) for n in range(2)]
    mem_away = mem_own[1].astype(BF)
    (out_down,) = down.finish([width])
    (out_up,) = up.finish([ffn])
    own.wait(out_down, out_up, mem_away, mem_own[0], grad_in, *cross.got_a)
    own_got = own.got_a + own.got_b
    own_kept = own.add_first()
    own.second()
    mem_own = mem_own[0] + grid.exchange(after(mem_away, *own_got), "c", 1).astype(F32)
    mem_own = [lax.dynamic_index_in_dim(mem_own, n ^ here["y"], 0, keepdims=False) for n in range(ny)]
    mem_away = [a.astype(BF) for a in mem_own[1:]]
    out_mem = mem_own[0]
    for n in range(1, ny):
        got = grid.exchange(after(mem_away[n - 1], *own.got_a, *own.got_b), "y", n)
        out_mem = out_mem + got.astype(F32)
    out_co, out_cq, out_ck, out_cv, late = cross.finish([width] * 4 + [128])
    own.wait(out_co)
    own.add_second()
    own.last()
    out_so, out_sq, out_sk, out_sv, last = own.finish([width] * 4 + [128])
    norms = [last[:, 0], last[:, 1]] + [late[:, n] for n in range(4)]
    return (
        out,
        grad_in,
        out_mem,
        out_sq,
        out_sk,
        out_sv,
        out_so,
        norms[0],
        norms[1],
        out_cq,
        out_ck,
        out_cv,
        out_co,
        norms[2],
        norms[3],
        out_up,
        out_down,
        norms[4],
        norms[5],
    )


def solution(mesh):
    grid = Grid(mesh.shape["dp"], mesh.shape["ctx"])
    row, flat = P(BOTH, None), P(BOTH)
    block = (row,) * 4 + (flat,) * 2
    return jax.shard_map(
        functools.partial(body, grid),
        mesh=mesh,
        in_specs=(row, row, row, row, flat, flat) + block + block + (row, row, flat, flat),
        out_specs=(row, row, row) + block + block + (row, row, flat, flat),
        check_vma=False,
    )
```

```python
import functools

import jax
import jax.numpy as jnp
from jax import lax
from jax.experimental import pallas as pl
from jax.experimental.pallas import tpu as pltpu
from jax.sharding import PartitionSpec as P

HD = 64
ALPHA_RES = 4.16
EPSILON = 1e-05
MASKED = -1e30
SCORE_SCALE = 0.125
BF = jnp.bfloat16
F32 = jnp.float32
BOTH = ("dp", "ctx")


class Grid:
    def __init__(self, dp, ctx):
        y = ctx // 2
        x = y
        self.size = {"z": dp // x, "x": x, "y": y, "c": 2}
        self.total = dp * ctx

    def index(self, coords):
        value = 0
        for name in "zxyc":
            value = value * self.size[name] + coords[name]
        return value

    def coords(self, index):
        out = {}
        for name in "cyxz":
            out[name] = index % self.size[name]
            index = index // self.size[name]
        return out

    def here(self):
        dp, ctx = lax.axis_index("dp"), lax.axis_index("ctx")
        nx = self.size["x"]
        return {"z": dp // nx, "x": dp % nx, "y": ctx // 2, "c": ctx % 2}

    def exchange(self, array, name, bit):
        pairs = []
        for source in range(self.total):
            coords = self.coords(source)
            coords[name] ^= bit
            pairs.append((source, self.index(coords)))
        return lax.ppermute(array, BOTH, pairs)

    def others(self, array, name):
        return [self.exchange(array, name, k) for k in range(1, self.size[name])]

    def blocks(self):
        nz, nx, ny = self.size["z"], self.size["x"], self.size["y"]
        out = []
        for c in range(2):
            out += [(z, x, y, c) for x in range(nx) for y in range(ny) for z in range(nz // 2)]
            out += [(z, x, y, c) for y in range(ny) for x in range(nx) for z in range(nz // 2, nz)]
        return out

    def positions(self):
        here = self.here()
        return jnp.stack(
            [
                self.index({name: k ^ here[name] for name, k in zip("zxyc", block)})
                for block in self.blocks()
            ]
        ).astype(jnp.int32)


def after(value, *before):
    return lax.optimization_barrier((value,) + before)[0]


SHORT = pl.CostEstimate(flops=1, bytes_accessed=1, transcendentals=0)
call = functools.partial(pl.pallas_call, cost_estimate=SHORT)


def params(mib=16):
    return pltpu.CompilerParams(vmem_limit_bytes=mib * 2**20)


def full(shape):
    return pl.BlockSpec(shape, lambda *_: (0,) * len(shape))


SCALARS = pl.BlockSpec(memory_space=pltpu.SMEM)
ANYWHERE = pl.BlockSpec(memory_space=pl.ANY)


def side_by_side(arrays):
    widths = [a.shape[1] for a in arrays]

    def kernel(*refs):
        at = 0
        for ref, width in zip(refs, widths):
            refs[-1][:, at : at + width] = ref[...]
            at += width

    return call(
        kernel, out_shape=jax.ShapeDtypeStruct((arrays[0].shape[0], sum(widths)), BF)
    )(*arrays)


def stack(groups):
    flat = [a for group in groups for a in group]

    def kernel(*refs):
        outs, sems = refs[len(flat) : -1], refs[-1]
        started = []
        for group, out in zip(groups, outs):
            for n in range(len(group)):
                at = len(started)
                started.append(pltpu.make_async_copy(refs[at], out.at[n], sems.at[at]))
        for copy in started:
            copy.start()
        for copy in started:
            copy.wait()

    return list(call(
        kernel,
        out_shape=[
            jax.ShapeDtypeStruct((len(group),) + group[0].shape, group[0].dtype) for group in groups
        ],
        in_specs=[ANYWHERE] * len(flat),
        out_specs=[pl.BlockSpec(memory_space=pltpu.VMEM)] * len(groups),
        scratch_shapes=[pltpu.SemaphoreType.DMA((len(flat),))],
        compiler_params=params(),
    )(*flat))


def assemble(grid, positions, part_a, part_b, parts, shapes):
    blocks = grid.blocks()
    nx, ny, nz = (grid.size[name] for name in "xyz")
    rows = part_a[0][0].shape[2]
    arrays = [a for part in part_a + part_b for a in part]

    def kernel(where, *refs):
        sources = refs[: len(arrays)]
        targets = refs[len(arrays) : -1]
        sems = refs[-1]
        started = []
        for column, width, result, at in parts:
            for n, (z, x, y, c) in enumerate(blocks):
                if z < nz // 2:
                    source = sources[c * ny + y].at[x, z]
                else:
                    source = sources[2 * ny + c * nx + x].at[y, z - nz // 2]
                started.append(
                    pltpu.make_async_copy(
                        source.at[:, pl.ds(column, width)],
                        targets[result].at[where[n], pl.ds(at, rows), :],
                        sems.at[len(started)],
                    )
                )
        for copy in started:
            copy.start()
        for copy in started:
            copy.wait()

    out = call(
        kernel,
        out_shape=[jax.ShapeDtypeStruct((len(blocks),) + shape, BF) for shape in shapes],
        in_specs=[SCALARS] + [ANYWHERE] * len(arrays),
        out_specs=[pl.BlockSpec(memory_space=pltpu.VMEM)] * len(shapes),
        scratch_shapes=[pltpu.SemaphoreType.DMA((len(parts) * len(blocks),))],
        compiler_params=params(4 + len(blocks) * sum(m * n for m, n in shapes) // 2**19),
    )(positions, *arrays)
    return [a.reshape(-1, a.shape[2]) for a in out]


def turn(grid, positions, left):
    tokens, width = left.shape
    rows = width // grid.total

    def kernel(where, left_ref, out_ref, turned):
        turned[...] = left_ref[...].T
        for n in range(grid.total):
            at = pl.multiple_of(where[n] * rows, rows)
            out_ref[n * rows : (n + 1) * rows, :] = turned[pl.ds(at, rows), :]

    return call(
        kernel,
        out_shape=jax.ShapeDtypeStruct((width, tokens), BF),
        in_specs=[SCALARS, pl.BlockSpec(memory_space=pltpu.VMEM)],
        out_specs=pl.BlockSpec(memory_space=pltpu.VMEM),
        scratch_shapes=[pltpu.VMEM((width, tokens), BF)],
        compiler_params=params(),
    )(positions, left)


def products(pairs, core, groups, got=None):
    rows = pairs[0][0].shape[0] // 2
    if len(pairs) == 1:
        width = pairs[0][1].shape[1]
        block = min(width, 1024)
        if width == block:
            block = width // 2
        steps = width // block
    else:
        block = pairs[0][1].shape[1]
        steps = len(pairs)
        width = sum(b.shape[1] for _, b in pairs)
    starts = [sum(groups[:n]) for n in range(len(groups))]

    def kernel(*refs):
        lefts, rights = refs[: len(pairs)], refs[len(pairs) : 2 * len(pairs)]
        rest = refs[2 * len(pairs) :]
        got_ref, outs = (None, rest) if got is None else (rest[0], rest[1:])

        def run(left, right):
            for start, size, out in zip(starts, groups, outs):
                value = matmul(left[start : start + size, :], right[...])
                cols = slice(0, right.shape[1])
                if got_ref is not None:
                    value = value + got_ref[start : start + size, cols].astype(F32)
                out[:, cols] = value.astype(BF)

        if len(pairs) == 1:
            run(lefts[0], rights[0])
        else:
            for n in range(len(pairs)):
                @pl.when(pl.program_id(0) == n)
                def _():
                    run(lefts[n], rights[n])

    left_specs = [pl.BlockSpec((rows, a.shape[1]), lambda n: (core, 0)) for a, _ in pairs]
    if len(pairs) == 1:
        right_specs = [pl.BlockSpec((pairs[0][1].shape[0], block), lambda n: (0, n))]
    else:
        right_specs = [full(b.shape) for _, b in pairs]
    operands = [a for a, _ in pairs] + [b for _, b in pairs]
    got_specs = []
    if got is not None:
        operands.append(got)
        got_specs = [pl.BlockSpec((rows, block), lambda n: (0, n))]
    return call(
        kernel,
        grid=(steps,),
        out_shape=[jax.ShapeDtypeStruct((size, width), BF) for size in groups],
        in_specs=left_specs + right_specs + got_specs,
        out_specs=[pl.BlockSpec((size, block), lambda n: (0, n)) for size in groups],
        compiler_params=params(),
    )(*operands)


def add_split(sums, counts):
    rows = [arrays[0].shape[0] for arrays in sums]
    width = sums[0][0].shape[1]
    steps = next(n for n in (2, 3, 1) if width % (n * 128) == 0)

    def kernel(*refs):
        at = 0
        out = sum(len(arrays) for arrays in sums)
        for arrays, count, total in zip(sums, counts, rows):
            each = total // count
            for n in range(count):
                value = refs[at][n * each : (n + 1) * each, :].astype(F32)
                for m in range(1, len(arrays)):
                    value = value + refs[at + m][n * each : (n + 1) * each, :].astype(F32)
                refs[out + n][...] = value.astype(BF)
            at += len(arrays)
            out += count

    block = width // steps
    out = call(
        kernel,
        grid=(steps,),
        out_shape=[
            jax.ShapeDtypeStruct((total // count, width), BF)
            for count, total in zip(counts, rows)
            for _ in range(count)
        ],
        in_specs=[
            pl.BlockSpec((total, block), lambda n: (0, n))
            for arrays, total in zip(sums, rows)
            for _ in arrays
        ],
        out_specs=[
            pl.BlockSpec((total // count, block), lambda n: (0, n))
            for count, total in zip(counts, rows)
            for _ in range(count)
        ],
        compiler_params=params(),
    )(*[a for arrays in sums for a in arrays])
    split, at = [], 0
    for count in counts:
        split.append(list(out[at : at + count]))
        at += count
    return split


def ffn_fits(grid, ffn):
    return ffn // grid.total % 128 == 0


def ffn_layer(grid, positions, part_a, part_b, second, cotangent, gain, bias):
    tokens, width = second.shape
    blocks = grid.blocks()
    count = len(blocks)
    nx, ny, nz = (grid.size[name] for name in "xyz")
    arrays = [a for part in part_a + part_b for a in part]
    rows = arrays[0].shape[2]
    ffn = arrays[0].shape[3] // 2
    each = ffn // count
    many = each // rows
    group = max(1, 512 // each)
    chunk = group * each
    piece = 256

    def kernel(where, second_ref, cot_ref, gain_ref, bias_ref, *refs):
        sources = refs[: len(arrays)]
        out_ref, low_ref, second_grad, act_t, pre_grad, g_gain, g_bias = refs[len(arrays) : len(arrays) + 7]
        up, down, slope, total, pre, act, low, sems = refs[len(arrays) + 7 :]

        def source(n):
            z, x, y, c = blocks[n]
            if z < nz // 2:
                return sources[c * ny + y].at[x, z]
            return sources[2 * ny + c * nx + x].at[y, z - nz // 2]

        up_copies, down_copies = [], []
        for n in range(count):
            at = pl.multiple_of(where[n] * rows, rows)
            up_copies.append(
                pltpu.make_async_copy(
                    source(n).at[:, pl.ds(0, ffn)], up.at[pl.ds(at, rows), :], sems.at[n]
                )
            )
        for n in range(count):
            for m in range(many):
                down_copies.append(
                    pltpu.make_async_copy(
                        source(n).at[:, pl.ds(ffn + m * width, width)],
                        down.at[pl.ds(n * each + m * rows, rows), :],
                        sems.at[count + n * many + m],
                    )
                )
        for copy in up_copies:
            copy.start()
        low[...] = second_ref[...].astype(BF)
        for copy in up_copies:
            copy.wait()
        for copy in down_copies:
            copy.start()

        def units(n):
            return pl.ds(pl.multiple_of(where[n] * each, each), each)

        for g in range(count // group):
            mine = slice(g * chunk, (g + 1) * chunk)
            slot = g % 2
            here = [up[:, units(g * group + n)] for n in range(group)]
            pre[slot] = matmul(low[...], jnp.concatenate(here, axis=1))
            for start in range(0, tokens, piece):
                some = slice(start, start + piece)
                x = pre[slot, some, :]
                erf = 1.0 + lax.erf(x * (0.5**0.5))
                act[slot, some, :] = (0.5 * x * erf).astype(BF)
                slope[some, mine] = (
                    0.5 * erf + x * jnp.exp(-0.5 * x * x) * 0.3989422804014327
                ).astype(BF)
            act_t[mine, :] = act[slot].T
            for copy in down_copies[g * group * many : (g + 1) * group * many]:
                copy.wait()
            value = matmul(act[slot], down[mine, :])
            if g == 0:
                total[...] = value
            else:
                total[...] += value

        gains, biases = 0.0, 0.0
        for start in range(0, tokens, piece):
            some = slice(start, start + piece)
            value, normal, scale = norm_forward(
                ALPHA_RES * second_ref[some, :] + total[some, :], gain_ref[...], bias_ref[...]
            )
            out_ref[some, :] = value.astype(BF)
            grad, one, two = norm_backward(cot_ref[some, :].astype(F32), normal, scale, gain_ref[...])
            gains, biases = gains + one.reshape(1, -1), biases + two.reshape(1, -1)
            total[some, :] = grad
            low_ref[some, :] = grad.astype(BF)
        g_gain[...] = gains
        g_bias[...] = biases

        for g in range(count // group):
            mine = slice(g * chunk, (g + 1) * chunk)
            value = (across(low_ref[...], down[mine, :]) * slope[:, mine].astype(F32)).astype(BF)
            for n in range(group):
                pre_grad[:, units(g * group + n)] = value[:, n * each : (n + 1) * each]
        for start in range(0, width, 256):
            some = slice(start, start + 256)
            second_grad[:, some] = ALPHA_RES * total[:, some] + across(pre_grad[...], up[some, :])

    vmem = pl.BlockSpec(memory_space=pltpu.VMEM)
    shapes = [
        ((tokens, width), BF),
        ((tokens, width), BF),
        ((tokens, width), F32),
        ((ffn, tokens), BF),
        ((tokens, ffn), BF),
        ((1, width), F32),
        ((1, width), F32),
    ]
    return call(
        kernel,
        out_shape=[jax.ShapeDtypeStruct(shape, dtype) for shape, dtype in shapes],
        in_specs=[SCALARS] + [vmem] * 4 + [ANYWHERE] * len(arrays),
        out_specs=[vmem] * len(shapes),
        scratch_shapes=[
            pltpu.VMEM((width, ffn), BF),
            pltpu.VMEM((ffn, width), BF),
            pltpu.VMEM((tokens, ffn), BF),
            pltpu.VMEM((tokens, width), F32),
            pltpu.VMEM((2, tokens, chunk), F32),
            pltpu.VMEM((2, tokens, chunk), BF),
            pltpu.VMEM((tokens, width), BF),
            pltpu.SemaphoreType.DMA((count * (1 + many),)),
        ],
        compiler_params=params(60),
    )(positions, second, cotangent, gain.reshape(1, -1), bias.reshape(1, -1), *arrays)


class Reduction:
    def __init__(self, grid, pairs):
        self.grid = grid
        self.pairs = pairs
        self.rows = pairs[0][0].shape[0]
        self.got, self.got_a, self.got_b = None, [], []

    def start(self):
        (self.away,) = products(self.pairs, 1, [self.rows // 2])
        return self.away

    def wait(self, *before):
        if self.got is not None:
            self.got = after(self.got, *before)
        self.got_a = [after(a, *before) for a in self.got_a]
        self.got_b = [after(b, *before) for b in self.got_b]

    def cores(self, *before):
        away = after(self.away, *before) if before else self.away
        self.got = self.grid.exchange(away, "c", 1)

    def keep(self):
        nx, ny = self.grid.size["x"], self.grid.size["y"]
        quarter = self.rows // 4
        outs = products(
            self.pairs, 0, [quarter // nx] * nx + [quarter // ny] * ny, self.got
        )
        self.got = None
        self.a, self.b = list(outs[:nx]), list(outs[nx:])
        return self.a + self.b

    def hold(self, *before):
        self.a = list(lax.optimization_barrier(tuple(self.a) + before)[: len(self.a)])
        self.b = list(lax.optimization_barrier(tuple(self.b) + before)[: len(self.b)])

    def send(self, name_a, name_b):
        self.got_a = [self.grid.exchange(a, name_a, k + 1) for k, a in enumerate(self.a[1:])]
        self.got_b = [self.grid.exchange(b, name_b, k + 1) for k, b in enumerate(self.b[1:])]
        return self.got_a + self.got_b

    def first(self):
        return self.send("x", "y")

    def add_first(self):
        counts = [self.grid.size["y"], self.grid.size["x"]]
        self.a, self.b = add_split([[self.a[0]] + self.got_a, [self.b[0]] + self.got_b], counts)
        return self.a + self.b

    def second(self):
        return self.send("y", "x")

    def add_second(self):
        half = self.grid.size["z"] // 2
        low, high = add_split([[self.a[0]] + self.got_a, [self.b[0]] + self.got_b], [half, half])
        self.a = low + high
        return self.a

    def last(self):
        self.got_a = [self.grid.exchange(a, "z", k + 1) for k, a in enumerate(self.a[1:])]
        self.got_b = []
        return self.got_a

    def finish(self, widths):
        arrays = [self.a[0]] + self.got_a

        def kernel(*refs):
            at = 0
            for width, out in zip(widths, refs[len(arrays) :]):
                value = refs[0][:, at : at + width].astype(F32)
                for ref in refs[1 : len(arrays)]:
                    value = value + ref[:, at : at + width].astype(F32)
                out[...] = value
                at += width

        return call(
            kernel,
            out_shape=[jax.ShapeDtypeStruct((self.a[0].shape[0], width), F32) for width in widths],
            compiler_params=params(),
        )(*arrays)


def matmul(left, right):
    return jnp.dot(left, right, preferred_element_type=F32)


def outer_right(left, right):
    return lax.dot_general(left, right, (((1,), (1,)), ((), ())), preferred_element_type=F32)


def norm_forward(resid, gain, bias):
    center = resid - jnp.mean(resid, axis=-1, keepdims=True)
    scale = lax.rsqrt(jnp.mean(center * center, axis=-1, keepdims=True) + EPSILON)
    normal = center * scale
    return normal * gain + bias, normal, scale


def norm_backward(dy, normal, scale, gain):
    dn = dy * gain
    grad = (
        dn
        - jnp.mean(dn, axis=-1, keepdims=True)
        - normal * jnp.mean(dn * normal, axis=-1, keepdims=True)
    ) * scale
    return grad, jnp.sum(dy * normal, axis=0), jnp.sum(dy, axis=0)


PAIR = 2 * HD
BLOCK = 256
DIMS_NT = (((1,), (1,)), ((), ()))


def head_of(array, which, scale=None):
    lane = lax.broadcasted_iota(jnp.int32, array.shape, 1)
    mine = (lane < HD) if which == 0 else (lane >= HD)
    out = jnp.where(mine, array.astype(F32), 0.0)
    return (out if scale is None else out * scale).astype(BF)


def across(left, right):
    return lax.dot_general(left, right, DIMS_NT, preferred_element_type=F32)


def pair_forward(q, k, v_t, bias):
    probs, sums = [], []
    for n in range(2):
        scores = across(k, head_of(q, n, SCORE_SCALE)) + bias
        peak = jnp.max(scores, axis=0, keepdims=True)
        exponent = jnp.exp(scores - peak)
        total = jnp.sum(exponent, axis=0, keepdims=True)
        probs.append((exponent * (1.0 / total)).astype(BF))
        sums.append(peak + jnp.log(total))
    outs = [matmul(v_t[n * HD : (n + 1) * HD, :], probs[n]) for n in range(2)]
    return jnp.concatenate(outs, axis=0).T.astype(BF), sums


TILE = 128
FORWARD = 40
BACKWARD = 40


def pair_backward(tiles, keys, bias_ref, sums_ref, q, k, v, out, grad, probs_ref, dscores_ref):
    length = q.shape[0]
    q_one = [head_of(q, n, SCORE_SCALE) for n in range(2)]
    g_one = [head_of(grad, n) for n in range(2)]
    both = (grad.astype(F32) * out.astype(F32)).T
    delta = [jnp.sum(both[n * HD : (n + 1) * HD, :], axis=0, keepdims=True) for n in range(2)]
    for key, query in tiles:
        down, over = slice(key, key + TILE), slice(query, query + BLOCK)
        for n in range(2):
            scores = across(k[down, :], q_one[n][over, :]) + bias_ref[down, over]
            probs = jnp.exp(scores - sums_ref[0, n : n + 1, over])
            dprob = across(v[down, :], g_one[n][over, :])
            at = slice(n * length + query, n * length + query + BLOCK)
            probs_ref[down, at] = probs.astype(BF)
            dscores_ref[down, at] = (probs * (dprob - delta[n][:, over])).astype(BF)
    k_t = k.T
    gq = [
        matmul(k_t[n * HD : (n + 1) * HD, :], dscores_ref[:keys, n * length : (n + 1) * length])
        for n in range(2)
    ]
    gq = jnp.concatenate(gq, axis=0).T * SCORE_SCALE
    gk = matmul(dscores_ref[:keys, :], jnp.concatenate(q_one, axis=0))
    gv = matmul(probs_ref[:keys, :], jnp.concatenate(g_one, axis=0))
    return gq.astype(BF), gk.astype(BF), gv.astype(BF)


def self_bias(column, row, pad):
    length = column.shape[0]
    at_k = lax.broadcasted_iota(jnp.int32, (length, length), 0)
    at_q = lax.broadcasted_iota(jnp.int32, (length, length), 1)
    live = (column == row) & (at_q >= at_k) & ((at_k < length - pad) | (at_q == at_k))
    return jnp.where(live, 0.0, MASKED)


def pair_spec(array):
    return pl.BlockSpec((array.shape[0], PAIR), lambda n: (0, n))


def sums_spec(length):
    return pl.BlockSpec((1, 8, length), lambda n: (n, 0, 0))


def whole_spec(array):
    return pl.BlockSpec(array.shape, lambda n: (0,) * array.ndim)


def self_forward(pad, column, row, q, k, v):
    length, width = q.shape

    def kernel(pad_ref, column_ref, row_ref, q_ref, k_ref, v_ref, out_ref, sums_ref, bias_ref):
        @pl.when(pl.program_id(0) == 0)
        def _():
            bias_ref[...] = self_bias(column_ref[...], row_ref[...], pad_ref[0])

        v_t = v_ref[...].T
        for start in range(0, length, BLOCK):
            mine, seen = slice(start, start + BLOCK), slice(0, start + BLOCK)
            out_ref[mine, :], sums = pair_forward(
                q_ref[mine, :], k_ref[seen, :], v_t[:, seen], bias_ref[seen, mine]
            )
            for n in range(2):
                sums_ref[0, n : n + 1, mine] = sums[n]

    return call(
        kernel,
        grid=(width // PAIR,),
        out_shape=[
            jax.ShapeDtypeStruct(q.shape, BF),
            jax.ShapeDtypeStruct((width // PAIR, 8, length), F32),
        ],
        in_specs=[pl.BlockSpec(memory_space=pltpu.SMEM), whole_spec(column), whole_spec(row)]
        + [pair_spec(q)] * 3,
        out_specs=[pair_spec(q), sums_spec(length)],
        scratch_shapes=[pltpu.VMEM((length, length), F32)],
        compiler_params=params(FORWARD),
    )(pad, column, row, q, k, v)


def self_backward(pad, column, row, sums, q, k, v, out, grad):
    length, width = q.shape
    tiles = [
        (key, query)
        for query in range(0, length, BLOCK)
        for key in range(0, query + BLOCK, TILE)
    ]

    def kernel(pad_ref, column_ref, row_ref, sums_ref, *refs):
        q_ref, k_ref, v_ref, o_ref, g_ref, gq_ref, gk_ref, gv_ref, bias_ref, probs_ref, ds_ref = refs

        @pl.when(pl.program_id(0) == 0)
        def _():
            bias_ref[...] = self_bias(column_ref[...], row_ref[...], pad_ref[0])
            probs_ref[...] = jnp.zeros_like(probs_ref)
            ds_ref[...] = jnp.zeros_like(ds_ref)

        gq_ref[...], gk_ref[...], gv_ref[...] = pair_backward(
            tiles,
            length,
            bias_ref,
            sums_ref,
            q_ref[...],
            k_ref[...],
            v_ref[...],
            o_ref[...],
            g_ref[...],
            probs_ref,
            ds_ref,
        )

    return call(
        kernel,
        grid=(width // PAIR,),
        out_shape=[jax.ShapeDtypeStruct(q.shape, BF)] * 3,
        in_specs=[SCALARS, whole_spec(column), whole_spec(row), sums_spec(length)]
        + [pair_spec(q)] * 5,
        out_specs=[pair_spec(q)] * 3,
        scratch_shapes=[pltpu.VMEM((length, length), F32)]
        + [pltpu.VMEM((length, 2 * length), BF)] * 2,
        compiler_params=params(BACKWARD),
    )(pad, column, row, sums, q, k, v, out, grad)


def windows(total):
    return sorted({min(512, total), min(640, total), total})


def choose_window(segment, ids):
    total = ids.shape[0]
    at = jnp.arange(total, dtype=jnp.int32)
    live = (ids >= segment[0]) & (ids <= segment[-1])
    low = jnp.min(jnp.where(live, at, total))
    high = jnp.max(jnp.where(live, at + 1, 0))
    choice, starts, rows = jnp.int32(0), [], []
    for size in windows(total):
        start = jnp.clip(low // 16 * 16, 0, total - size)
        starts.append(start)
        rows.append(lax.dynamic_slice(ids, (start,), (size,)).reshape(size, 1))
        choice = choice + (high - start > size).astype(jnp.int32)
    return jnp.stack([choice] + starts), rows


def on_window(window_ref, total, run):
    for n, size in enumerate(windows(total)):
        @pl.when(window_ref[0] == n)
        def _():
            run(n, size, pl.ds(pl.multiple_of(window_ref[1 + n], 16), size))


def cross_forward(window, column, rows, q, k, v):
    length, width = q.shape
    total = k.shape[0]

    def kernel(window_ref, column_ref, *refs):
        row_refs = refs[: len(rows)]
        q_ref, k_ref, v_ref, out_ref, sums_ref, bias_ref = refs[len(rows) :]

        def run(n, size, seen):
            @pl.when(pl.program_id(0) == 0)
            def _():
                bias_ref[:size, :] = jnp.where(row_refs[n][...] == column_ref[...], 0.0, MASKED)

            v_t = v_ref[seen, :].T
            for start in range(0, length, BLOCK):
                mine = slice(start, start + BLOCK)
                out_ref[mine, :], sums = pair_forward(
                    q_ref[mine, :], k_ref[seen, :], v_t, bias_ref[:size, mine]
                )
                for m in range(2):
                    sums_ref[0, m : m + 1, mine] = sums[m]

        on_window(window_ref, total, run)

    return call(
        kernel,
        grid=(width // PAIR,),
        out_shape=[
            jax.ShapeDtypeStruct(q.shape, BF),
            jax.ShapeDtypeStruct((width // PAIR, 8, length), F32),
        ],
        in_specs=[pl.BlockSpec(memory_space=pltpu.SMEM), whole_spec(column)]
        + [whole_spec(row) for row in rows]
        + [pair_spec(q), pair_spec(k), pair_spec(v)],
        out_specs=[pair_spec(q), sums_spec(length)],
        scratch_shapes=[pltpu.VMEM((total, length), F32)],
        compiler_params=params(FORWARD),
    )(window, column, *rows, q, k, v)


def cross_backward(window, row, ids, sums, q, k, v, out, grad):
    length, width = q.shape
    total = k.shape[0]

    def kernel(window_ref, row_ref, sums_ref, *refs):
        id_refs = refs[: len(ids)]
        q_ref, k_ref, v_ref, o_ref, g_ref, gq_ref, gk_ref, gv_ref, bias_ref, probs_ref, ds_ref = refs[
            len(ids) :
        ]

        def run(n, size, seen):
            @pl.when(pl.program_id(0) == 0)
            def _():
                bias_ref[:size, :] = jnp.where(id_refs[n][...] == row_ref[...], 0.0, MASKED)

            if size < total:
                gk_ref[...] = jnp.zeros_like(gk_ref)
                gv_ref[...] = jnp.zeros_like(gv_ref)
            tiles = [
                (key, query)
                for query in range(0, length, BLOCK)
                for key in range(0, size, TILE)
            ]
            gq_ref[...], gk_ref[seen, :], gv_ref[seen, :] = pair_backward(
                tiles,
                size,
                bias_ref,
                sums_ref,
                q_ref[...],
                k_ref[seen, :],
                v_ref[seen, :],
                o_ref[...],
                g_ref[...],
                probs_ref,
                ds_ref,
            )

        on_window(window_ref, total, run)

    return call(
        kernel,
        grid=(width // PAIR,),
        out_shape=[jax.ShapeDtypeStruct(a.shape, BF) for a in (q, k, v)],
        in_specs=[SCALARS, whole_spec(row), sums_spec(length)]
        + [whole_spec(a) for a in ids]
        + [pair_spec(q), pair_spec(k), pair_spec(v), pair_spec(q), pair_spec(q)],
        out_specs=[pair_spec(q), pair_spec(k), pair_spec(v)],
        scratch_shapes=[pltpu.VMEM((total, length), F32)]
        + [pltpu.VMEM((total, 2 * length), BF)] * 2,
        compiler_params=params(BACKWARD),
    )(window, row, sums, *ids, q, k, v, out, grad)


def body(
    grid,
    hidden,
    memory,
    cotangent,
    dec_segment,
    pad_length,
    mem_segment,
    self_query,
    self_key,
    self_value,
    self_output,
    norm1_gain,
    norm1_bias,
    cross_query,
    cross_key,
    cross_value,
    cross_output,
    norm2_gain,
    norm2_bias,
    ffn_up,
    ffn_down,
    norm3_gain,
    norm3_bias,
):
    width = hidden.shape[1]
    ffn = ffn_up.shape[1]
    mem_rows = memory.shape[0]
    own_rows = self_query.shape[0]
    nx, ny, nz = grid.size["x"], grid.size["y"], grid.size["z"]
    here = grid.here()
    positions = grid.positions()

    def gather_z(piece):
        return [piece] + grid.others(piece, "z")

    def stacked(line, *before):
        line = [after(a, *before) for a in line] if before else line
        return stack([line[: nz // 2], line[nz // 2 :]])

    def hold(pair, *before):
        return after(pair[0], *before), after(pair[1], *before)

    class Gather:
        def first(self, pair):
            self.pair = pair
            self.got = grid.others(pair[0], "x"), grid.others(pair[1], "y")
            return self.got[0] + self.got[1]

        def second(self, *before):
            got = [[after(a, *before) for a in part] if before else part for part in self.got]
            self.pair = stack([[a] + part for a, part in zip(self.pair, got)])
            self.got = grid.others(self.pair[0], "y"), grid.others(self.pair[1], "x")
            self.core = [[grid.exchange(a, "c", 1)] for a in self.pair]
            return self.pair

        def cores(self, *before):
            got = [[after(a, *before) for a in part] if before else part for part in self.got]
            out = []
            for a, part, core in zip(self.pair, got, self.core):
                out.append([[a] + part, core + [grid.exchange(b, "c", 1) for b in part]])
            return out

    vectors = [norm1_gain, norm1_bias, norm2_gain, norm2_bias, norm3_gain, norm3_bias]
    vectors = jnp.pad(jnp.stack(vectors, axis=1).astype(BF), ((0, 0), (0, 122)))
    self_piece = side_by_side([self_query, self_key, self_value, self_output])
    self_z = gather_z(self_piece)
    cross_piece = side_by_side([cross_query, cross_key, cross_value, cross_output, vectors])
    many = ffn_down.shape[0] // own_rows
    ffn_piece = side_by_side(
        [ffn_up] + [ffn_down[n * own_rows : (n + 1) * own_rows] for n in range(many)]
    )

    self_z = self_z[:1] + [after(a, cross_piece, ffn_piece) for a in self_z[1:]]

    self_ag, cross_ag, ffn_ag = Gather(), Gather(), Gather()
    mem_y = [memory] + grid.others(memory, "y")
    ids_y = [mem_segment] + grid.others(mem_segment, "y")
    self_pair = stacked(self_z, cross_piece, ffn_piece, *mem_y[1:], *ids_y[1:])
    self_ag.first(self_pair)
    cross_z = gather_z(after(cross_piece, *self_pair))
    mem_c = stack([[after(a, *self_z) for a in mem_y]])
    mem_c += grid.others(mem_c[0], "c")
    ids_c = [jnp.stack(ids_y)]
    ids_c += grid.others(ids_c[0], "c")
    self_pair = self_ag.second(*mem_c[1:], *ids_c[1:])
    cross_pair = stacked(cross_z, *self_pair)
    ffn_z = gather_z(after(ffn_piece, *cross_pair))
    self_a, self_b = self_ag.cores(*cross_pair)
    cross_ag.first(hold(cross_pair, *self_ag.got[0], *self_ag.got[1]))

    mem_blocks = jnp.stack(
        [(y ^ here["y"]) * 2 + (c ^ here["c"]) for c in range(2) for y in range(ny)]
    ).astype(jnp.int32)

    def place_kernel(where, *refs):
        target, sems = refs[2], refs[3]
        started = []
        for c in range(2):
            for y in range(ny):
                n = c * ny + y
                started.append(
                    pltpu.make_async_copy(refs[c].at[y], target.at[where[n]], sems.at[n])
                )
        for copy in started:
            copy.start()
        for copy in started:
            copy.wait()

    mem_all = call(
        place_kernel,
        out_shape=jax.ShapeDtypeStruct((2 * ny, mem_rows, width), BF),
        in_specs=[SCALARS, ANYWHERE, ANYWHERE],
        out_specs=pl.BlockSpec(memory_space=pltpu.VMEM),
        scratch_shapes=[pltpu.SemaphoreType.DMA((2 * ny,))],
        compiler_params=params(),
    )(mem_blocks, *mem_c).reshape(-1, width)
    ids_all = jnp.zeros((2 * ny, mem_rows), jnp.int32)
    for c in range(2):
        for y in range(ny):
            ids_all = lax.dynamic_update_slice(
                ids_all, ids_c[c][y][None], (mem_blocks[c * ny + y], 0)
            )
    ids_all = ids_all.reshape(-1)

    w_sq, w_sk, w_sv, w_so = assemble(
        grid,
        positions,
        self_a,
        self_b,
        [(n * width, width, n, 0) for n in range(4)],
        [(own_rows, width)] * 4,
    )

    segment = dec_segment.reshape(-1)
    column, row = segment.reshape(-1, 1), segment.reshape(1, -1)
    hidden_t = turn(grid, positions, hidden)
    mem_t = turn(grid, positions, mem_all)
    q = matmul(hidden, w_sq).astype(BF)
    k = matmul(hidden, w_sk).astype(BF)
    v = matmul(hidden, w_sv).astype(BF)
    cross_pair = cross_ag.second(w_sq)
    self_att, self_sums = self_forward(pad_length, column, row, after(q, *cross_pair), k, v)
    ffn_pair = stacked(ffn_z, self_att)
    window, rows = choose_window(segment, after(ids_all, *ffn_pair))
    cross_a, cross_b = cross_ag.cores(self_att)
    cross_got = cross_a[0][1:] + cross_b[0][1:]
    ffn_ag.first(hold(ffn_pair, *cross_got))
    w_cq, w_ck, w_cv, w_co, vectors = assemble(
        grid,
        positions,
        cross_a,
        cross_b,
        [(n * width, width, n, 0) for n in range(4)] + [(4 * width, 128, 4, 0)],
        [(own_rows, width)] * 4 + [(own_rows, 128)],
    )
    vectors = vectors[:, :6].T.astype(F32)
    gain1, bias1, gain2, bias2, gain3, bias3 = [vectors[n] for n in range(6)]
    first, normal1, scale1 = norm_forward(
        ALPHA_RES * hidden.astype(F32) + matmul(after(self_att, *cross_got), w_so), gain1, bias1
    )
    first_low = first.astype(BF)
    cq = matmul(first_low, w_cq).astype(BF)
    mk = matmul(mem_all, w_ck).astype(BF)
    mv = matmul(mem_all, w_cv).astype(BF)
    ffn_pair = ffn_ag.second(cq, mk, mv)
    cross_att, cross_sums = cross_forward(window, row, rows, after(cq, *ffn_pair), mk, mv)
    second, normal2, scale2 = norm_forward(
        ALPHA_RES * first + matmul(cross_att, w_co), gain2, bias2
    )
    second_low = second.astype(BF)
    second_t = turn(grid, positions, second_low)
    self_att_t = turn(grid, positions, self_att)
    first_t = turn(grid, positions, first_low)
    cross_att_t = turn(grid, positions, cross_att)
    turned = (hidden_t, mem_t, second_t, self_att_t, first_t, cross_att_t)
    ffn_a, ffn_b = ffn_ag.cores(*turned)
    if ffn_fits(grid, ffn):
        out, third_low, grad_second, act_t, grad_pre, g_gain3, g_bias3 = ffn_layer(
            grid, positions, ffn_a, ffn_b, second, cotangent, gain3, bias3
        )
        g_gain3, g_bias3 = g_gain3.reshape(-1), g_bias3.reshape(-1)
    else:
        w_up, w_down = assemble(
            grid,
            positions,
            ffn_a,
            ffn_b,
            [(0, ffn, 0, 0)] + [(ffn + n * width, width, 1, n * own_rows) for n in range(many)],
            [(own_rows, ffn), (own_rows * many, width)],
        )
        pre = matmul(second_low, w_up)
        erf = 1.0 + lax.erf(pre * (0.5**0.5))
        act = (0.5 * pre * erf).astype(BF)
        slope = 0.5 * erf + pre * jnp.exp(-0.5 * pre * pre) * 0.3989422804014327
        third, normal3, scale3 = norm_forward(
            ALPHA_RES * second + matmul(act, w_down), gain3, bias3
        )
        out = third.astype(BF)
        grad_third, g_gain3, g_bias3 = norm_backward(
            cotangent.astype(F32), normal3, scale3, gain3
        )
        third_low = grad_third.astype(BF)
        act_t = turn(grid, positions, act)
        grad_pre = (slope * outer_right(third_low, w_down)).astype(BF)
        grad_second = ALPHA_RES * grad_third + outer_right(grad_pre, w_up)

    down = Reduction(grid, [(act_t, third_low)])
    down.start()
    down.cores()
    up = Reduction(grid, [(second_t, after(grad_pre, down.away))])
    up.start()
    up.cores()
    grad_mid, g_gain2, g_bias2 = norm_backward(
        after(grad_second, up.away), normal2, scale2, gain2
    )
    mid_low = grad_mid.astype(BF)
    grad_catt = outer_right(mid_low, w_co).astype(BF)
    down.wait(grad_catt)
    down_kept = down.keep()
    down.first()
    up.wait(*down_kept)
    up_kept = up.keep()
    unit = jnp.eye(128, dtype=BF)

    def spread(vectors):
        vectors = jnp.pad(jnp.stack(vectors).astype(BF), ((0, 128 - len(vectors)), (0, 0)))
        return turn(grid, positions, vectors), unit

    cross_norms = spread([g_gain2, g_bias2, g_gain3, g_bias3])
    grad_cq, grad_mk, grad_mv = cross_backward(
        window,
        row,
        rows,
        cross_sums,
        cq,
        mk,
        mv,
        cross_att,
        after(grad_catt, *up_kept, cross_norms[0]),
    )
    down.wait(grad_cq)
    down_kept = down.add_first()
    down.second()
    up.hold(*down_kept)
    up.first()
    cross = Reduction(
        grid,
        [
            (cross_att_t, mid_low),
            (first_t, after(grad_cq, *down_kept)),
            (mem_t, grad_mk),
            (mem_t, grad_mv),
            cross_norms,
        ],
    )
    cross.start()
    cross.cores(*down.got_a, *down.got_b)
    grad_first = ALPHA_RES * grad_mid + outer_right(after(grad_cq, cross.away), w_cq)
    grad_res, g_gain1, g_bias1 = norm_backward(grad_first, normal1, scale1, gain1)
    res_low = grad_res.astype(BF)
    grad_satt = outer_right(res_low, w_so).astype(BF)
    own_norms = spread([g_gain1, g_bias1])
    grad_q, grad_k, grad_v = self_backward(
        pad_length,
        column,
        row,
        self_sums,
        q,
        k,
        v,
        self_att,
        after(grad_satt, own_norms[0]),
    )
    down.wait(grad_q)
    down_kept = down.add_second()
    down.last()
    up.wait(*down_kept)
    up_kept = up.add_first()
    up.second()
    cross.wait(*up_kept)
    cross_kept = cross.keep()
    cross.hold(*up.got_a, *up.got_b)
    cross.first()
    own = Reduction(
        grid,
        [
            (self_att_t, res_low),
            (hidden_t, after(grad_q, *cross_kept)),
            (hidden_t, grad_k),
            (hidden_t, grad_v),
            own_norms,
        ],
    )
    own.start()
    own.cores(*up.got_a, *up.got_b, *down.got_a)
    grad_in = ALPHA_RES * grad_res + outer_right(after(grad_q, own.away), w_sq)
    up.wait(grad_in)
    up_kept = up.add_second()
    up.a = [after(a, *down.got_a) for a in up.a]
    up.last()
    own.wait(grad_in, *up_kept)
    own_kept = own.keep()
    cross.wait(*up_kept, *own_kept)
    cross_kept = cross.add_first()
    cross.second()
    own.hold(*cross.got_a, *cross.got_b)
    own.first()
    cross.wait(*own_kept)
    cross_kept = cross.add_second()
    cross.a = [after(a, *up.got_a) for a in cross.a]
    cross.last()
    grad_in = grad_in + outer_right(after(grad_k, *own_kept), w_sk) + outer_right(grad_v, w_sv)
    grad_mem = outer_right(after(grad_mk, *own_kept), w_ck) + outer_right(grad_mv, w_cv)
    grad_mem = grad_mem.reshape(ny, 2, mem_rows, width)
    mem_own = [lax.dynamic_index_in_dim(grad_mem, n ^ here["c"], 1, keepdims=False) for n in range(2)]
    mem_away = mem_own[1].astype(BF)
    (out_down,) = down.finish([width])
    (out_up,) = up.finish([ffn])
    own.wait(out_down, out_up, mem_away, mem_own[0], grad_in, *cross.got_a)
    own_got = own.got_a + own.got_b
    own_kept = own.add_first()
    own.second()
    mem_own = mem_own[0] + grid.exchange(after(mem_away, *own_got), "c", 1).astype(F32)
    mem_own = [lax.dynamic_index_in_dim(mem_own, n ^ here["y"], 0, keepdims=False) for n in range(ny)]
    mem_away = [a.astype(BF) for a in mem_own[1:]]
    out_mem = mem_own[0]
    for n in range(1, ny):
        got = grid.exchange(after(mem_away[n - 1], *own.got_a, *own.got_b), "y", n)
        out_mem = out_mem + got.astype(F32)
    out_co, out_cq, out_ck, out_cv, late = cross.finish([width] * 4 + [128])
    own.wait(out_co)
    own.add_second()
    own.last()
    out_so, out_sq, out_sk, out_sv, last = own.finish([width] * 4 + [128])
    norms = [last[:, 0], last[:, 1]] + [late[:, n] for n in range(4)]
    return (
        out,
        grad_in,
        out_mem,
        out_sq,
        out_sk,
        out_sv,
        out_so,
        norms[0],
        norms[1],
        out_cq,
        out_ck,
        out_cv,
        out_co,
        norms[2],
        norms[3],
        out_up,
        out_down,
        norms[4],
        norms[5],
    )


def solution(mesh):
    grid = Grid(mesh.shape["dp"], mesh.shape["ctx"])
    row, flat = P(BOTH, None), P(BOTH)
    block = (row,) * 4 + (flat,) * 2
    return jax.shard_map(
        functools.partial(body, grid),
        mesh=mesh,
        in_specs=(row, row, row, row, flat, flat) + block + block + (row, row, flat, flat),
        out_specs=(row, row, row) + block + block + (row, row, flat, flat),
        check_vma=False,
    )
```
